32 devices in a mesh: batch: 8 (over y, x, core), blk: 4 (over z).
Axes of the slice: x: 2, y: 2, z: 4, core: 2. Of those that a mesh axis runs over, the one named last changes fastest.
Arguments:
- tokens: bfloat16 [32, 640, 768], P('batch', 'blk'), may hold values from -6 to 6
- resolution: int32 [32], P('batch'), may hold values from 0 to 1, as said below
- positions: int32 [32, 640], P('batch'), may hold values from 0 to 575, as said below
- ln1_gain: bfloat16 [768], replicated, may hold values from 0.5 to 1.5
- ln1_bias: bfloat16 [768], replicated, may hold values from -1.75 to 1.75
- w_qkv: bfloat16 [768, 2304], replicated, may hold values from -0.21875 to 0.21875
- q_bias: bfloat16 [768], replicated, may hold values from -3 to 3
- v_bias: bfloat16 [768], replicated, may hold values from -0.625 to 0.625
- w_proj: bfloat16 [768, 768], replicated, may hold values from -1.75 to 1.75
- proj_bias: bfloat16 [768], replicated, may hold values from -1.75 to 1.75
- gamma1: bfloat16 [768], replicated, may hold values from 0.5 to 2
- ln2_gain: bfloat16 [768], replicated, may hold values from 0.5 to 1.5
- ln2_bias: bfloat16 [768], replicated, may hold values from -1.75 to 1.75
- w_fc1: bfloat16 [768, 3072], replicated, may hold values from -0.21875 to 0.21875
- fc1_bias: bfloat16 [3072], replicated, may hold values from -3 to 3
- w_fc2: bfloat16 [3072, 768], replicated, may hold values from -0.109375 to 0.109375
- fc2_bias: bfloat16 [768], replicated, may hold values from -1.75 to 1.75
- gamma2: bfloat16 [768], replicated, may hold values from 0.5 to 2
- rel_low: bfloat16 [732, 12], replicated, may hold values from -4 to 4
- rel_high: bfloat16 [2212, 12], replicated, may hold values from -4 to 4
- grad_out: bfloat16 [32, 640, 768], P('batch', 'blk'), may hold values from -6 to 6
Outputs:
- output: bfloat16 [32, 640, 768], P('batch', 'blk')
- grad_tokens: bfloat16 [32, 640, 768], P('batch', 'blk')
- grad_ln1_gain: float32 [768], replicated
- grad_ln1_bias: float32 [768], replicated
- grad_w_qkv: float32 [768, 2304], P(('batch', 'blk'))
- grad_q_bias: float32 [768], replicated
- grad_v_bias: float32 [768], replicated
- grad_w_proj: float32 [768, 768], P(('batch', 'blk'))
- grad_proj_bias: float32 [768], replicated
- grad_gamma1: float32 [768], replicated
- grad_ln2_gain: float32 [768], replicated
- grad_ln2_bias: float32 [768], replicated
- grad_w_fc1: float32 [768, 3072], P(('batch', 'blk'))
- grad_fc1_bias: float32 [3072], replicated
- grad_w_fc2: float32 [3072, 768], P(('batch', 'blk'))
- grad_fc2_bias: float32 [768], replicated
- grad_gamma2: float32 [768], replicated
- grad_rel_low: float32 [732, 12], replicated
- grad_rel_high: float32 [2212, 12], replicated
The draws below stay inside these ranges and needn't reach their ends.
Inputs may be any that keep to these rules, and one draw needn't show every extreme that they name: Among each 4 consecutive images (those of one index of batch) at least one has resolution 1. `positions`: for an image of grid side G, entries 1 to G * G hold every cell 0 to G * G - 1 once (cell = row * G + column); all other entries are 0.
All inputs are finite; a program needn't handle non-finite values.
Results may differ from the reference program's by a relative error of at most 0.015.
Values may be sent and summed in bfloat16 or wider, within the bound.
A program may use at most 384 MiB of HBM per device.

```python
import math
import jax
import jax.numpy as jnp
from jax import lax

D = 768
H = 12
HD = 64
FF = 3072
SEQ = 640
G_LOW = 14
G_HIGH = 24
IMG_GROUP = 4
IMAGES = 32
R_LOW = 732
R_HIGH = 2212


def resolution_groups(key):
    groups = IMAGES // IMG_GROUP
    bits = jax.random.randint(key, (groups, IMG_GROUP), 0, 2)
    leader = jax.random.randint(jax.random.fold_in(key, 11), (groups, 1), 0, IMG_GROUP)
    chosen = jnp.arange(IMG_GROUP)[None, :] == leader
    return jnp.where(chosen, 1, bits).reshape(IMAGES).astype(jnp.int32)


def draw_resolution(key, part):
    return resolution_groups(key)


def draw_positions(key, part):
    flags = resolution_groups(key)
    key = jax.random.fold_in(key, 5)
    image_keys = jax.random.split(key, IMAGES)

    def single(image_key, flag):
        high = jax.random.permutation(image_key, G_HIGH * G_HIGH).astype(jnp.int32)
        lower = jax.random.permutation(jax.random.fold_in(image_key, 1), G_LOW * G_LOW).astype(jnp.int32)
        padded = jnp.concatenate([lower, jnp.zeros((G_HIGH * G_HIGH - G_LOW * G_LOW,), jnp.int32)])
        cells = jnp.where(flag == 1, high, padded)
        return jnp.concatenate([jnp.zeros((1,), jnp.int32), cells, jnp.zeros((SEQ - 1 - G_HIGH * G_HIGH,), jnp.int32)])
    return jax.vmap(single)(image_keys, flags).astype(jnp.int32)


def block_levels(own_key, shape, cuts, least, high):
    factor_of, own = 1.0, jax.random.fold_in(own_key, 6)
    for axis_at, shards_of in cuts:
        heights = jnp.exp(jax.random.uniform(jax.random.fold_in(own, axis_at), (shards_of,), jnp.float32, least / len(cuts), high / len(cuts)))
        factor_of = factor_of * jnp.repeat(heights, shape[axis_at] // shards_of).reshape([-1 if axis == axis_at else 1 for axis in range(len(shape))])
    return factor_of


def noise(key, extent, deviation, most, shards=(), held_as=jnp.bfloat16):
    loudness = block_levels(key, extent, shards, -0.22, 0.18) if shards else 1.0
    array = jax.random.normal(key, extent, jnp.float32) * deviation * loudness
    return jnp.minimum(jnp.maximum(array, -most), most).astype(held_as)


def setup_inputs(seed: int = 0) -> dict:
    streams_of = jax.random.split(jax.random.key(seed), 22)
    tokens = noise(streams_of[0], (IMAGES, SEQ, D), 1.0, 6.0, ((0, 8), (1, 4)))
    resolution = draw_resolution(jax.random.fold_in(streams_of[21], 71), 0)
    positions = draw_positions(jax.random.fold_in(streams_of[21], 71), 0)
    ln1_gain = jnp.clip(1.0 + 0.1 * jax.random.normal(streams_of[3], (D,), jnp.float32), 0.5, 1.5).astype(jnp.bfloat16)
    ln1_bias = noise(streams_of[4], (D,), 0.3, 1.75)
    w_qkv = noise(streams_of[5], (D, 3 * D), D ** -0.5, 0.21875)
    q_bias = noise(streams_of[6], (D,), 0.5, 3.0)
    v_bias = noise(streams_of[7], (D,), 0.1, 0.625)
    w_proj = noise(streams_of[8], (D, D), (D // 64) ** -0.5, 1.75)
    proj_bias = noise(streams_of[9], (D,), 0.3, 1.75)
    gamma1 = jnp.clip(jnp.exp(jax.random.uniform(streams_of[10], (D,), jnp.float32, math.log(0.5), math.log(2.0))), 0.5, 2.0).astype(jnp.bfloat16)
    ln2_gain = jnp.clip(1.0 + 0.1 * jax.random.normal(streams_of[11], (D,), jnp.float32), 0.5, 1.5).astype(jnp.bfloat16)
    ln2_bias = noise(streams_of[12], (D,), 0.3, 1.75)
    w_fc1 = noise(streams_of[13], (D, FF), D ** -0.5, 0.21875)
    fc1_bias = noise(streams_of[14], (FF,), 0.5, 3.0)
    w_fc2 = noise(streams_of[15], (FF, D), FF ** -0.5, 0.109375)
    fc2_bias = noise(streams_of[16], (D,), 0.3, 1.75)
    gamma2 = jnp.clip(jnp.exp(jax.random.uniform(streams_of[17], (D,), jnp.float32, math.log(0.5), math.log(2.0))), 0.5, 2.0).astype(jnp.bfloat16)
    rel_low = noise(streams_of[18], (R_LOW, H), 1.0, 4.0)
    rel_high = noise(streams_of[19], (R_HIGH, H), 1.0, 4.0)
    grad_out = noise(streams_of[20], (IMAGES, SEQ, D), 1.0, 6.0, ((0, 8), (1, 4)))
    return dict(tokens=tokens, resolution=resolution, positions=positions, ln1_gain=ln1_gain, ln1_bias=ln1_bias, w_qkv=w_qkv, q_bias=q_bias, v_bias=v_bias, w_proj=w_proj, proj_bias=proj_bias, gamma1=gamma1, ln2_gain=ln2_gain, ln2_bias=ln2_bias, w_fc1=w_fc1, fc1_bias=fc1_bias, w_fc2=w_fc2, fc2_bias=fc2_bias, gamma2=gamma2, rel_low=rel_low, rel_high=rel_high, grad_out=grad_out)


@jax.custom_vjp
def low(v):
    return lax.optimization_barrier(v.astype(jnp.bfloat16)).astype(jnp.float32)

@jax.custom_vjp
def low_back(v):
    return v

def low_keep(v):
    return (low(v), None)

def low_pass(kept, grad):
    return (grad,)

def back_keep(v):
    return (v, None)

def back_low(kept, grad):
    return (low(grad),)
low.defvjp(low_keep, low_pass)
low_back.defvjp(back_keep, back_low)

def product(left, right):
    return jnp.dot(left, right, precision=lax.Precision.HIGHEST)

def layer_norm(values, gain, shift):
    center = values - lax.optimization_barrier(jnp.mean(values, axis=-1, keepdims=True))
    spread = lax.optimization_barrier(jnp.mean(center * center, axis=-1, keepdims=True))
    return center * lax.rsqrt(spread + 1e-06) * gain + shift

def token_codes(cells, grid, lengths, rows):
    patch = (rows[None, :] >= 1) & (rows[None, :] < lengths[:, None])
    return (cells // grid[:, None], cells % grid[:, None], patch)

def table_index(query, keyside, grid, base):
    row_q, col_q, patch_q = query
    row_k, col_k, patch_k = keyside
    span = grid[:, None, None]
    side = 2 * span - 1
    inner = (row_q[:, :, None] - row_k[:, None, :] + span - 1) * side + (col_q[:, :, None] - col_k[:, None, :] + span - 1)
    top = side * side
    both = patch_q[:, :, None] & patch_k[:, None, :]
    index = jnp.where(both, inner, jnp.where(patch_k[:, None, :], top, jnp.where(patch_q[:, :, None], top + 1, top + 2)))
    return (index + base[:, None, None]).astype(jnp.int32)

def forward(inputs, cells, grid, lengths, base, params):
    ln1_gain, ln1_bias, w_qkv, q_bias, v_bias, w_proj, proj_bias, gamma1, ln2_gain, ln2_bias, w_fc1, fc1_bias, w_fc2, fc2_bias, gamma2, rel_low, rel_high = params
    count = inputs.shape[0]
    flat = inputs.reshape(count * SEQ, D)
    hidden1 = low(layer_norm(flat, ln1_gain, ln1_bias))
    qkv = product(hidden1, w_qkv) + jnp.concatenate([q_bias, jnp.zeros_like(q_bias), v_bias])
    qkv = low_back(low(qkv)).reshape(count, SEQ, 3, H, HD)
    query, keys, values = (qkv[:, :, 0], qkv[:, :, 1], qkv[:, :, 2])
    rows = jnp.arange(SEQ).astype(jnp.int32)
    codes = token_codes(cells, grid, lengths, rows)
    index = table_index(codes, codes, grid, base)
    table = jnp.concatenate([rel_low, rel_high], axis=0)
    bias = jnp.moveaxis(jnp.take(table, index, axis=0), 3, 1)
    dots = jnp.einsum('bqhd,bkhd->bhqk', query, keys, precision=lax.Precision.HIGHEST) * HD ** (-0.5)
    scores = low_back(dots) + bias
    valid = (rows[None, :] < lengths[:, None])[:, None, None, :]
    scores = jnp.where(valid, scores, -1e+30)
    expo = jnp.exp(scores - lax.optimization_barrier(jnp.max(scores, axis=-1, keepdims=True)))
    probs = expo / lax.optimization_barrier(jnp.sum(expo, axis=-1, keepdims=True))
    mixed = jnp.einsum('bhqk,bkhd->bqhd', low(probs), values, precision=lax.Precision.HIGHEST)
    mixed = low_back(low(mixed)).reshape(count * SEQ, D)
    attn = low_back(product(mixed, w_proj) + proj_bias)
    resid = flat + gamma1 * attn
    hidden2 = low(layer_norm(resid, ln2_gain, ln2_bias))
    pre = low_back(product(hidden2, w_fc1) + fc1_bias)
    act = low(jax.nn.gelu(pre, approximate=False))
    branch = low_back(product(act, w_fc2) + fc2_bias)
    return (resid + gamma2 * branch).reshape(count, SEQ, D)

def reference(tokens, resolution, positions, ln1_gain, ln1_bias, w_qkv, q_bias, v_bias, w_proj, proj_bias, gamma1, ln2_gain, ln2_bias, w_fc1, fc1_bias, w_fc2, fc2_bias, gamma2, rel_low, rel_high, grad_out):
    params = tuple((p.astype(jnp.float32) for p in (ln1_gain, ln1_bias, w_qkv, q_bias, v_bias, w_proj, proj_bias, gamma1, ln2_gain, ln2_bias, w_fc1, fc1_bias, w_fc2, fc2_bias, gamma2, rel_low, rel_high)))
    grid = jnp.where(resolution == 1, G_HIGH, G_LOW).astype(jnp.int32)
    lengths = (1 + grid * grid).astype(jnp.int32)
    base = jnp.where(resolution == 1, R_LOW, 0).astype(jnp.int32)
    blocks = IMAGES // 2

    def step(total, item):
        inputs, cells, grids, lens, bases, upstream = item

        def apply(values, weights):
            return forward(values, cells, grids, lens, bases, weights)
        result, pull = jax.vjp(apply, inputs.astype(jnp.float32), params)
        d_inputs, d_params = pull(upstream.astype(jnp.float32))
        total = jax.tree.map(jnp.add, total, d_params)
        return (total, (result.astype(jnp.bfloat16), d_inputs.astype(jnp.bfloat16)))
    zeros = jax.tree.map(jnp.zeros_like, params)
    stacked = tuple((a.reshape((blocks, 2) + a.shape[1:]) for a in (tokens, positions, grid, lengths, base, grad_out)))
    grads, (output, grad_tokens) = lax.scan(step, zeros, stacked)
    return (output.reshape(IMAGES, SEQ, D), grad_tokens.reshape(IMAGES, SEQ, D), grads[0], grads[1], grads[2], grads[3], grads[4], grads[5], grads[6], grads[7], grads[8], grads[9], grads[10], grads[11], grads[12], grads[13], grads[14], grads[15], grads[16])
```

```python
import functools

import jax
import jax.numpy as jnp
import numpy as np
from jax import lax
from jax.experimental import pallas as pl
from jax.experimental.pallas import tpu as pltpu
from jax.sharding import PartitionSpec as P

G_LOW = 14
G_HIGH = 24
SIDE_LOW = 2 * G_LOW - 1
SIDE = 2 * G_HIGH - 1
CELLS = G_HIGH * G_HIGH
SPAN = 1152
F32 = jnp.float32
BF16 = jnp.bfloat16


def layer_stats(values):
    center = values - jnp.mean(values, axis=-1, keepdims=True)
    factor = lax.rsqrt(jnp.mean(center * center, axis=-1, keepdims=True) + 1e-06)
    return (center * factor, factor)


def norm_back(grad, normed, factor, gain):
    scaled = grad * gain
    return factor * (
        scaled
        - jnp.mean(scaled, axis=-1, keepdims=True)
        - normed * jnp.mean(scaled * normed, axis=-1, keepdims=True)
    )


def gelu_slope(values):
    return (
        0.5 * (1.0 + lax.erf(values * 0.7071067811865476))
        + values * jnp.exp(-0.5 * values * values) * 0.3989422804014327
    )


def matmul(left, right):
    return jnp.dot(left, right, preferred_element_type=F32)


def matmul_t(left, right):
    return lax.dot_general(left, right, (((1,), (1,)), ((), ())), preferred_element_type=F32)


def t_matmul(left, right):
    return lax.dot_general(left, right, (((0,), (0,)), ((), ())), preferred_element_type=F32)


def slot_tables(seq):
    tokens = np.arange(seq)
    tables = []
    for grid in (G_LOW, G_HIGH):
        cells = np.arange(CELLS)
        used = (cells // G_HIGH < grid) & (cells % G_HIGH < grid)
        free = np.concatenate([cells[~used], np.arange(CELLS + 1, seq)])
        slot = np.full(seq, CELLS)
        slot[1 + grid * grid :] = free
        patch = np.concatenate([used, np.zeros(seq - CELLS, bool)])
        key = patch.copy()
        key[CELLS] = True
        tables.append((slot, (tokens >= 1) & (tokens < 1 + grid * grid), patch, key))
    return [np.stack(parts) for parts in zip(*tables)]


def lane_tables():
    lanes = np.arange(SPAN)
    spread = (lanes[None, :] // G_HIGH == np.arange(128)[:, None]) & (np.arange(128)[:, None] < SIDE)
    code = np.arange(48)[:, None] + (lanes % G_HIGH)[None, :]
    return spread, code.astype(np.int32)


def bias_kernel(special, table, spread, code, patch, mask, out, wide, full):
    head = pl.program_id(0)
    flat = matmul(table[0], spread[...])
    codes = code[...]
    for a in range(G_HIGH):
        picked = jnp.where(codes == a + G_HIGH - 1, flat, 0.0)
        wide[a : a + 1, :] = jnp.sum(picked, axis=0, keepdims=True)
    for r in range(G_HIGH):
        at = (G_HIGH - 1 - r) * G_HIGH
        full[r * G_HIGH : (r + 1) * G_HIGH, 0:CELLS] = wide[:, at : at + CELLS]
    seq = full.shape[0]
    column = lax.broadcasted_iota(jnp.int32, (1, seq), 1)
    inner_row = jnp.where(column < CELLS, special[head, 0], special[head, 2])
    values = jnp.where(column < CELLS, full[...], special[head, 1])
    values = jnp.where(patch[...] > 0.0, values, inner_row)
    out[0] = (values + mask[...]).astype(BF16)


def make_bias(table, special, spread, code, patch, mask):
    heads, seq = table.shape[0], patch.shape[0]
    whole = lambda shape: pl.BlockSpec(shape, lambda h: (0,) * len(shape))
    return pl.pallas_call(
        bias_kernel,
        grid=(heads,),
        out_shape=jax.ShapeDtypeStruct((heads, seq, seq), BF16),
        in_specs=[
            pl.BlockSpec(memory_space=pltpu.SMEM),
            pl.BlockSpec((1, 48, 128), lambda h: (h, 0, 0)),
            whole(spread.shape),
            whole(code.shape),
            whole(patch.shape),
            whole(mask.shape),
        ],
        out_specs=pl.BlockSpec((1, seq, seq), lambda h: (h, 0, 0)),
        scratch_shapes=[pltpu.VMEM((G_HIGH, SPAN), F32), pltpu.VMEM((seq, seq), F32)],
        compiler_params=pltpu.CompilerParams(vmem_limit_bytes=48 << 20),
        name="bias",
    )(special, table, spread, code, patch, mask)


FWD_ROWS = 128


def forward_kernel(query, keys, values, bias, probs, mixed):
    seq = query.shape[0]
    for h in range(2):
        at = slice(h * 64, h * 64 + 64)
        k = keys[:, at]
        v = values[:, at]
        for r in range(0, seq, FWD_ROWS):
            rows = slice(r, r + FWD_ROWS)
            scores = matmul_t(query[rows, at] * 0.125, k) + bias[h, rows, :].astype(F32)
            expo = jnp.exp(scores - jnp.max(scores, axis=-1, keepdims=True))
            low = (expo / jnp.sum(expo, axis=-1, keepdims=True)).astype(BF16)
            probs[h, rows, :] = low
            mixed[rows, at] = matmul(low, v).astype(BF16)


def attention(qkv, bias):
    seq = qkv.shape[0]
    width = qkv.shape[1] // 3
    pairs = width // 128
    column = lambda part: pl.BlockSpec((seq, 128), lambda h: (0, part * pairs + h))
    square = pl.BlockSpec((2, seq, seq), lambda h: (h, 0, 0))
    return pl.pallas_call(
        forward_kernel,
        grid=(pairs,),
        out_shape=(
            jax.ShapeDtypeStruct((2 * pairs, seq, seq), BF16),
            jax.ShapeDtypeStruct((seq, width), BF16),
        ),
        in_specs=[column(0), column(1), column(2), square],
        out_specs=(square, column(0)),
        compiler_params=pltpu.CompilerParams(vmem_limit_bytes=48 << 20),
        name="attention",
    )(qkv, qkv, qkv, bias)


def backward_kernel(query, keys, values, probs, upstream, patch, spread, code, d_query, d_key, d_value, d_table, d_edge, score, wide):
    seq = query.shape[0]
    step = 128
    for h in range(2):
        at = slice(h * 64, h * 64 + 64)
        k = keys[:, at]
        v = values[:, at]
        dk = jnp.zeros((seq, 64), F32)
        dv = jnp.zeros((seq, 64), F32)
        for r in range(0, seq, step):
            rows = slice(r, r + step)
            low = probs[h, rows, :]
            up = upstream[rows, at]
            weight = low.astype(F32)
            product = weight * matmul_t(up, v)
            ds = product - weight * jnp.sum(product, axis=-1, keepdims=True)
            score[rows, :] = ds
            ds_low = ds.astype(BF16)
            d_query[rows, at] = (matmul(ds_low, k) * 0.125).astype(BF16)
            dk += t_matmul(ds_low, query[rows, at] * 0.125)
            dv += t_matmul(low, up)
        d_key[:, at] = dk.astype(BF16)
        d_value[:, at] = dv.astype(BF16)
        wide[...] = jnp.zeros_like(wide)
        inside = jnp.zeros((1, seq), F32)
        total = jnp.zeros((1, seq), F32)
        for r in range(0, seq, 128):
            rows = slice(r, r + 128)
            ds = score[rows, :]
            total += jnp.sum(ds, axis=0, keepdims=True)
            ds = ds * patch[rows, :]
            inside += jnp.sum(ds, axis=0, keepdims=True)
        for r in range(G_HIGH):
            rows = slice(r * G_HIGH, (r + 1) * G_HIGH)
            off = (G_HIGH - 1 - r) * G_HIGH
            wide[:, off : off + CELLS] += score[rows, 0:CELLS] * patch[rows, :]
        d_edge[h, 0:1, :] = inside
        d_edge[h, 1:2, :] = total - inside
        codes = code[...]
        flat = jnp.zeros((48, SPAN), F32)
        for a in range(G_HIGH):
            flat += jnp.where(codes == a + G_HIGH - 1, wide[a : a + 1, :], 0.0)
        high = flat.astype(BF16)
        rest = flat - high.astype(F32)
        middle = rest.astype(BF16)
        last = (rest - middle.astype(F32)).astype(BF16)
        d_table[h] = matmul_t(high, spread[...]) + matmul_t(middle, spread[...]) + matmul_t(last, spread[...])


def attention_back(qkv, probs, upstream, patch, spread, code):
    seq = qkv.shape[0]
    width = qkv.shape[1] // 3
    pairs = width // 128
    column = lambda part: pl.BlockSpec((seq, 128), lambda h: (0, part * pairs + h))
    whole = lambda shape: pl.BlockSpec(shape, lambda h: (0,) * len(shape))
    flat = jax.ShapeDtypeStruct((seq, width), BF16)
    return pl.pallas_call(
        backward_kernel,
        grid=(pairs,),
        out_shape=(
            flat,
            flat,
            flat,
            jax.ShapeDtypeStruct((2 * pairs, 48, 128), F32),
            jax.ShapeDtypeStruct((2 * pairs, 8, seq), F32),
        ),
        in_specs=[
            column(0),
            column(1),
            column(2),
            pl.BlockSpec((2, seq, seq), lambda h: (h, 0, 0)),
            column(0),
            whole(patch.shape),
            whole(spread.shape),
            whole(code.shape),
        ],
        out_specs=(
            column(0),
            column(0),
            column(0),
            pl.BlockSpec((2, 48, 128), lambda h: (h, 0, 0)),
            pl.BlockSpec((2, 8, seq), lambda h: (h, 0, 0)),
        ),
        scratch_shapes=[pltpu.VMEM((seq, seq), F32), pltpu.VMEM((G_HIGH, SPAN), F32)],
        compiler_params=pltpu.CompilerParams(vmem_limit_bytes=48 << 20),
        name="attention_back",
    )(qkv, qkv, qkv, probs, upstream, patch, spread, code)


def exchange(blocks, count, me):
    result = jnp.zeros_like(blocks)
    result = lax.dynamic_update_index_in_dim(
        result, lax.dynamic_index_in_dim(blocks, me, 0, keepdims=False), me, 0
    )
    for shift in range(1, count):
        there = lax.rem(me + shift, count)
        back = lax.rem(me + count - shift, count)
        part = lax.ppermute(
            lax.dynamic_index_in_dim(blocks, there, 0, keepdims=False),
            "blk",
            [(i, (i + shift) % count) for i in range(count)],
        )
        result = lax.dynamic_update_index_in_dim(result, part, back, 0)
    return result


def swap(value, axis, bit, count):
    return lax.ppermute(value, axis, [(i, i ^ bit) for i in range(count)])


def bits_of(count):
    return [1 << i for i in range(count.bit_length() - 1)]


def scatter_sum(grad, batch, blk, flip):
    places = [("batch", bit, batch) for bit in bits_of(batch)][::-1]
    places += [("blk", bit, blk) for bit in bits_of(blk)][::-1]
    value = grad.reshape((2,) * len(places) + (grad.shape[0] >> len(places), grad.shape[1]))
    order = [p for p in places if p[0] == "batch"][::-1] + [p for p in places if p[0] == "blk"][::-1]
    if flip:
        order = order[:1] + order[1 : len(bits_of(batch))][::-1] + order[len(bits_of(batch)) :]
    left = list(places)
    for place in order:
        axis, bit, count = place
        at = left.index(place)
        left.remove(place)
        mine = jnp.bitwise_and(lax.axis_index(axis) // bit, 1)
        sent = lax.dynamic_index_in_dim(value, 1 - mine, at, keepdims=False)
        kept = lax.dynamic_index_in_dim(value, mine, at, keepdims=False)
        got = swap(sent, axis, bit, count)
        value = kept.astype(F32) + got.astype(F32)
        if left:
            value = value.astype(BF16)
    return value


def total_sum(value, batch, blk):
    for bit in bits_of(batch):
        value = value + swap(value, "batch", bit, batch)
    for bit in bits_of(blk):
        value = value + swap(value, "blk", bit, blk)
    return value


def packed(parts):
    flat = jnp.concatenate([p.reshape(-1) for p in parts])
    size = flat.shape[0]
    rows = -(-size // 1024) * 8
    return jnp.pad(flat, (0, rows * 128 - size)).reshape(rows, 128)


def unpacked(value, shapes):
    flat = value.reshape(-1)
    result, at = [], 0
    for shape in shapes:
        size = int(np.prod(shape))
        result.append(flat[at : at + size].reshape(shape))
        at += size
    return result


def shards(
    batch,
    blk,
    tokens,
    resolution,
    positions,
    ln1_gain,
    ln1_bias,
    w_qkv,
    q_bias,
    v_bias,
    w_proj,
    proj_bias,
    gamma1,
    ln2_gain,
    ln2_bias,
    w_fc1,
    fc1_bias,
    w_fc2,
    fc2_bias,
    gamma2,
    rel_low,
    rel_high,
    grad_out,
):
    images, rows, width = tokens.shape
    seq = positions.shape[1]
    heads = rel_low.shape[1]
    assert images == blk and rows * blk == seq and width == heads * 64
    me = lax.axis_index("blk")

    slot_np, token_np, patch_np, key_np = slot_tables(seq)
    high = lax.dynamic_index_in_dim(resolution, me, 0, keepdims=False) == 1
    cells = lax.dynamic_index_in_dim(positions, me, 0, keepdims=False)
    grid = jnp.where(high, G_HIGH, G_LOW)
    pick = lambda pair: jnp.where(high, pair[1], pair[0])
    slot = jnp.where(pick(token_np), (cells // grid) * G_HIGH + cells % grid, pick(slot_np))
    patch = pick(patch_np).astype(F32)[:, None]
    mask = jnp.where(pick(key_np), 0.0, -1e30).astype(F32)[None, :]
    slots = jnp.arange(seq, dtype=jnp.int32)
    to_slot = (slots[:, None] == slot[None, :]).astype(BF16)
    to_token = (slots[None, :] == slot[:, None]).astype(BF16)

    pad = G_HIGH - G_LOW
    top_low, top_high = SIDE_LOW * SIDE_LOW, SIDE * SIDE
    inner_low = jnp.pad(
        rel_low[:top_low].T.reshape(heads, SIDE_LOW, SIDE_LOW), ((0, 0), (pad, pad), (pad, pad))
    )
    inner_high = rel_high[:top_high].T.reshape(heads, SIDE, SIDE)
    inner = jnp.where(high, inner_high, inner_low)[:, ::-1, :].transpose(0, 2, 1)
    table = jnp.pad(inner, ((0, 0), (0, 48 - SIDE), (0, 128 - SIDE)))
    special = jnp.where(high, rel_high[top_high:], rel_low[top_low:]).T.astype(F32)
    spread_np, code_np = lane_tables()
    spread = jnp.asarray(spread_np, BF16)
    code = jnp.asarray(code_np)
    bias = make_bias(table, special, spread, code, patch, mask)

    raw = exchange(tokens, blk, me).reshape(seq, width)
    inputs = matmul(to_slot, raw)
    raw_up = exchange(grad_out, blk, me).reshape(seq, width)

    gain1 = ln1_gain.astype(F32)
    gain2 = ln2_gain.astype(F32)
    scale1_layer = gamma1.astype(F32)
    scale2_layer = gamma2.astype(F32)
    normed1, factor1 = layer_stats(inputs)
    hidden1 = (normed1 * gain1 + ln1_bias.astype(F32)).astype(BF16)
    qkv_shift = jnp.concatenate([q_bias, jnp.zeros_like(q_bias), v_bias]).astype(F32)
    qkv = (matmul(hidden1, w_qkv) + qkv_shift).astype(BF16)
    probs, mixed = attention(qkv, bias)
    attn = matmul(mixed, w_proj) + proj_bias.astype(F32)
    resid = inputs + scale1_layer * attn
    normed2, factor2 = layer_stats(resid)
    hidden2 = (normed2 * gain2 + ln2_bias.astype(F32)).astype(BF16)
    pre = matmul(hidden2, w_fc1) + fc1_bias.astype(F32)
    act = jax.nn.gelu(pre, approximate=False).astype(BF16)
    branch = matmul(act, w_fc2) + fc2_bias.astype(F32)
    out_slot = (resid + scale2_layer * branch).astype(BF16)
    output = exchange(matmul(to_token, out_slot).astype(BF16).reshape(blk, rows, width), blk, me)

    upstream = matmul(to_slot, raw_up)
    d_gamma2 = jnp.sum(upstream * branch, axis=0)
    d_branch = (scale2_layer * upstream).astype(BF16)
    g_fc2 = scatter_sum(t_matmul(act, d_branch).astype(BF16), batch, blk, False)
    d_fc2b = jnp.sum(d_branch.astype(F32), axis=0)
    d_pre = (matmul_t(d_branch, w_fc2) * gelu_slope(pre)).astype(BF16)
    g_fc1 = scatter_sum(t_matmul(hidden2, d_pre).astype(BF16), batch, blk, True)
    d_fc1b = jnp.sum(d_pre.astype(F32), axis=0)
    d_hidden2 = matmul_t(d_pre, w_fc1)
    d_ln2g = jnp.sum(d_hidden2 * normed2, axis=0)
    d_ln2b = jnp.sum(d_hidden2, axis=0)
    d_resid = upstream + norm_back(d_hidden2, normed2, factor2, gain2)
    d_gamma1 = jnp.sum(d_resid * attn, axis=0)
    d_attn = (scale1_layer * d_resid).astype(BF16)
    g_proj = scatter_sum(t_matmul(mixed, d_attn).astype(BF16), batch, blk, False)
    d_projb = jnp.sum(d_attn.astype(F32), axis=0)
    d_mixed = matmul_t(d_attn, w_proj).astype(BF16)
    early = [d_gamma2, d_fc2b, d_fc1b, d_ln2g, d_ln2b, d_gamma1, d_projb]
    early_sum = total_sum(packed(early), batch, blk)

    d_query, d_key, d_value, d_table, d_edge = attention_back(qkv, probs, d_mixed, patch, spread, code)
    d_qkv = jnp.concatenate([d_query, d_key, d_value], axis=1)
    g_qkv = scatter_sum(t_matmul(hidden1, d_qkv).astype(BF16), batch, blk, True)
    d_qb = jnp.sum(d_query.astype(F32), axis=0)
    d_vb = jnp.sum(d_value.astype(F32), axis=0)
    d_hidden1 = matmul_t(d_qkv, w_qkv)
    d_ln1g = jnp.sum(d_hidden1 * normed1, axis=0)
    d_ln1b = jnp.sum(d_hidden1, axis=0)
    d_inputs = (d_resid + norm_back(d_hidden1, normed1, factor1, gain1)).astype(BF16)
    grad_tokens = exchange(matmul(to_token, d_inputs).astype(BF16).reshape(blk, rows, width), blk, me)

    offsets = d_table[:, :SIDE, :SIDE].transpose(0, 2, 1)[:, ::-1, :]
    tops = jnp.stack(
        [jnp.sum(d_edge[:, 1, :CELLS], axis=1), d_edge[:, 0, CELLS], d_edge[:, 1, CELLS]], axis=1
    )
    high_grad = jnp.concatenate([offsets.reshape(heads, top_high), tops], axis=1)
    small = offsets[:, pad : pad + SIDE_LOW, pad : pad + SIDE_LOW]
    low_grad = jnp.concatenate([small.reshape(heads, top_low), tops], axis=1)
    high_grad = jnp.where(high, high_grad, 0.0)
    low_grad = jnp.where(high, 0.0, low_grad)
    late = [d_ln1g, d_ln1b, d_qb, d_vb, low_grad, high_grad]
    late_sum = total_sum(packed(late), batch, blk)

    s_gamma2, s_fc2b, s_fc1b, s_ln2g, s_ln2b, s_gamma1, s_projb = unpacked(
        early_sum, [p.shape for p in early]
    )
    s_ln1g, s_ln1b, s_qb, s_vb, s_low, s_high = unpacked(late_sum, [p.shape for p in late])
    return (
        output,
        grad_tokens,
        s_ln1g,
        s_ln1b,
        g_qkv,
        s_qb,
        s_vb,
        g_proj,
        s_projb,
        s_gamma1,
        s_ln2g,
        s_ln2b,
        g_fc1,
        s_fc1b,
        g_fc2,
        s_fc2b,
        s_gamma2,
        s_low.T,
        s_high.T,
    )


def solution(mesh):
    rows = P("batch", "blk", None)
    shared = P(("batch", "blk"), None)
    in_specs = (rows, P("batch"), P("batch", None)) + (P(),) * 17 + (rows,)
    out_specs = (
        (rows, rows, P(), P(), shared, P(), P(), shared)
        + (P(),) * 4
        + (shared, P(), shared)
        + (P(),) * 4
    )
    return jax.shard_map(
        functools.partial(shards, mesh.shape["batch"], mesh.shape["blk"]),
        mesh=mesh,
        in_specs=in_specs,
        out_specs=out_specs,
        check_vma=False,
    )
```

```python
import functools

import jax
import jax.numpy as jnp
import numpy as np
from jax import lax
from jax.experimental import pallas as pl
from jax.experimental.pallas import tpu as pltpu
from jax.sharding import PartitionSpec as P

G_LOW = 14
G_HIGH = 24
SIDE_LOW = 2 * G_LOW - 1
SIDE = 2 * G_HIGH - 1
CELLS = G_HIGH * G_HIGH
SPAN = 1152
F32 = jnp.float32
BF16 = jnp.bfloat16


def layer_stats(values):
    center = values - jnp.mean(values, axis=-1, keepdims=True)
    factor = lax.rsqrt(jnp.mean(center * center, axis=-1, keepdims=True) + 1e-06)
    return (center * factor, factor)


def norm_back(grad, normed, factor, gain):
    scaled = grad * gain
    return factor * (
        scaled
        - jnp.mean(scaled, axis=-1, keepdims=True)
        - normed * jnp.mean(scaled * normed, axis=-1, keepdims=True)
    )


def gelu_slope(values):
    return (
        0.5 * (1.0 + lax.erf(values * 0.7071067811865476))
        + values * jnp.exp(-0.5 * values * values) * 0.3989422804014327
    )


def matmul(left, right):
    return jnp.dot(left, right, preferred_element_type=F32)


def matmul_t(left, right):
    return lax.dot_general(left, right, (((1,), (1,)), ((), ())), preferred_element_type=F32)


def t_matmul(left, right):
    return lax.dot_general(left, right, (((0,), (0,)), ((), ())), preferred_element_type=F32)


def slot_tables(seq):
    tokens = np.arange(seq)
    tables = []
    for grid in (G_LOW, G_HIGH):
        cells = np.arange(CELLS)
        used = (cells // G_HIGH < grid) & (cells % G_HIGH < grid)
        free = np.concatenate([cells[~used], np.arange(CELLS + 1, seq)])
        slot = np.full(seq, CELLS)
        slot[1 + grid * grid :] = free
        patch = np.concatenate([used, np.zeros(seq - CELLS, bool)])
        key = patch.copy()
        key[CELLS] = True
        tables.append((slot, (tokens >= 1) & (tokens < 1 + grid * grid), patch, key))
    return [np.stack(parts) for parts in zip(*tables)]


def lane_tables():
    lanes = np.arange(SPAN)
    spread = (lanes[None, :] // G_HIGH == np.arange(128)[:, None]) & (np.arange(128)[:, None] < SIDE)
    code = np.arange(48)[:, None] + (lanes % G_HIGH)[None, :]
    return np.stack([spread, np.roll(spread, 64, axis=0)]), code.astype(np.int32)


FWD_ROWS = 128


def whole(shape):
    return pl.BlockSpec(shape, lambda h: (0,) * len(shape))


ANY = pl.BlockSpec(memory_space=pl.ANY)
SMEM = pl.BlockSpec(memory_space=pltpu.SMEM)


def prepare_kernel(
    count, resolution, cells, low_t, high_t, spread, code, slot_of, is_patch, patches, masks, tokens,
    bias, to_slot, raw, inner_low, inner_high, wide, full, *refs,
):
    head = pl.program_id(0)
    me = lax.axis_index("blk")
    high = resolution[me] == 1
    seq = full.shape[0]
    heads = low_t.shape[0]
    move = Exchange(count).bind(tokens, raw, refs)

    @pl.when(head == 0)
    def _():
        greet(move.partners())
        move.start()
        here = cells[pl.ds(me, 1), :]
        grid = jnp.where(high, G_HIGH, G_LOW)
        row = jnp.zeros_like(here)
        for k in range(1, G_HIGH):
            row += (here >= k * grid).astype(jnp.int32)
        at = row * G_HIGH + here - row * grid
        patch = jnp.where(high, is_patch[1:2, :], is_patch[0:1, :])
        other = jnp.where(high, slot_of[1:2, :], slot_of[0:1, :])
        slot = jnp.where(patch > 0, at, other)
        spots = lax.broadcasted_iota(jnp.int32, (seq, seq), 0)
        to_slot[...] = jnp.where(spots == slot, 1.0, 0.0).astype(BF16)
        inner_low[...] = jnp.zeros_like(inner_low)
        inner_high[...] = jnp.zeros_like(inner_high)
        pad = G_HIGH - G_LOW
        for j in range(SIDE):
            r = SIDE - 1 - j
            inner_high[j * 16 : j * 16 + heads, 0:SIDE] = high_t[:, r * SIDE : (r + 1) * SIDE]
            r -= pad
            if 0 <= r < SIDE_LOW:
                inner_low[j * 16 : j * 16 + heads, pad : pad + SIDE_LOW] = low_t[
                    :, r * SIDE_LOW : (r + 1) * SIDE_LOW
                ]

    rows = pl.ds(head, 48, stride=16)
    table = jnp.where(high, inner_high[rows, :], inner_low[rows, :]).astype(BF16)
    flat = t_matmul(table, spread[0, 0:48, :])[0:48]
    codes = code[...]
    for a in range(G_HIGH):
        picked = jnp.where(codes == a + G_HIGH - 1, flat, 0.0)
        wide[a : a + 1, :] = jnp.sum(picked, axis=0, keepdims=True)
    for r in range(G_HIGH):
        at = (G_HIGH - 1 - r) * G_HIGH
        full[r * G_HIGH : (r + 1) * G_HIGH, 0:CELLS] = wide[:, at : at + CELLS]
    column = lax.broadcasted_iota(jnp.int32, (1, seq), 1)
    end_low, end_high = low_t.shape[1], high_t.shape[1]
    special = jnp.where(high, high_t[:, end_high - 3 : end_high], low_t[:, end_low - 3 : end_low])
    here = lax.broadcasted_iota(jnp.int32, special.shape, 0) == head
    special = jnp.sum(jnp.where(here, special, 0.0), axis=0, keepdims=True)
    inner_row = jnp.where(column < CELLS, special[:, 0:1], special[:, 2:3])
    values = jnp.where(column < CELLS, full[...], special[:, 1:2])
    patch = jnp.where(high, patches[:, 1:2], patches[:, 0:1])
    mask = jnp.where(high, masks[1:2, :], masks[0:1, :])
    values = jnp.where(patch > 0.0, values, inner_row)
    bias[0] = (values + mask).astype(BF16)

    @pl.when(head == heads - 1)
    def _():
        move.finish()


def prepare(resolution, cells, rel_low, rel_high, spread, code, patches, tokens, count):
    heads = rel_low.shape[1]
    seq = cells.shape[1]
    slot_np, token_np, patch_np, key_np = slot_tables(seq)
    low_t, high_t = rel_low.T.astype(F32), rel_high.T.astype(F32)
    slot_of = jnp.asarray(slot_np, jnp.int32)
    is_patch = jnp.asarray(token_np, jnp.int32)
    masks = jnp.asarray(np.where(key_np, 0.0, -1e30), F32)
    operands = (low_t, high_t, spread, code, slot_of, is_patch, patches, masks)
    return pl.pallas_call(
        functools.partial(prepare_kernel, count),
        grid=(heads,),
        out_shape=(
            jax.ShapeDtypeStruct((heads, seq, seq), BF16),
            jax.ShapeDtypeStruct((seq, seq), BF16),
            jax.ShapeDtypeStruct(tokens.shape, BF16),
        ),
        in_specs=[SMEM, whole(cells.shape)] + [whole(o.shape) for o in operands] + [ANY],
        out_specs=(pl.BlockSpec((1, seq, seq), lambda h: (h, 0, 0)), whole((seq, seq)), ANY),
        scratch_shapes=[
            pltpu.VMEM((48 * 16, 128), F32),
            pltpu.VMEM((48 * 16, 128), F32),
            pltpu.VMEM((G_HIGH, SPAN), F32),
            pltpu.VMEM((seq, seq), F32),
        ]
        + Exchange(count).scratch(),
        compiler_params=pltpu.CompilerParams(
            collective_id=0, has_side_effects=True, vmem_limit_bytes=48 << 20
        ),
        name="prepare",
    )(resolution, cells, *operands, tokens)


def forward_kernel(count, query, keys, values, bias, upstream, probs, mixed, raw, *refs):
    seq = query.shape[0]
    step = pl.program_id(0)
    move = Exchange(count).bind(upstream, raw, refs)

    @pl.when(step == 0)
    def _():
        greet(move.partners())
        move.start()

    for h in range(2):
        at = slice(h * 64, h * 64 + 64)
        k = keys[:, at]
        v = values[:, at]
        for r in range(0, seq, FWD_ROWS):
            rows = slice(r, r + FWD_ROWS)
            scores = matmul_t(query[rows, at] * 0.125, k) + bias[h, rows, :].astype(F32)
            expo = jnp.exp(scores - jnp.max(scores, axis=-1, keepdims=True))
            low = (expo / jnp.sum(expo, axis=-1, keepdims=True)).astype(BF16)
            probs[h, rows, :] = low
            mixed[rows, at] = matmul(low, v).astype(BF16)

    @pl.when(step == pl.num_programs(0) - 1)
    def _():
        move.finish()


def attention(qkv, bias, upstream, count):
    seq = qkv.shape[0]
    width = qkv.shape[1] // 3
    pairs = width // 128
    column = lambda part: pl.BlockSpec((seq, 128), lambda h: (0, part * pairs + h))
    square = pl.BlockSpec((2, seq, seq), lambda h: (h, 0, 0))
    return pl.pallas_call(
        functools.partial(forward_kernel, count),
        grid=(pairs,),
        out_shape=(
            jax.ShapeDtypeStruct((2 * pairs, seq, seq), BF16),
            jax.ShapeDtypeStruct((seq, width), BF16),
            jax.ShapeDtypeStruct(upstream.shape, BF16),
        ),
        in_specs=[column(0), column(1), column(2), square, ANY],
        out_specs=(square, column(0), ANY),
        scratch_shapes=Exchange(count).scratch(),
        compiler_params=pltpu.CompilerParams(
            collective_id=1, has_side_effects=True, vmem_limit_bytes=48 << 20
        ),
        name="attention",
    )(qkv, qkv, qkv, bias, upstream)


def backward_kernel(
    setup, resolution, query, keys, values, probs, upstream, patches, spread, code, output, *refs
):
    count, pairs, grads = setup
    refs = list(refs)
    take = lambda n: [refs.pop(0) for _ in range(n)]
    partials = take(grads)
    vector = take(1) if grads else []
    d_query, d_key, d_value, d_table, moved = take(5)
    sums = take(grads)
    vector_sum = take(1) if grads else []
    score, wide = take(2)
    move = Exchange(count)
    move.bind(output, moved, take(len(move.scratch())))
    step = pl.program_id(0)
    ticks = [[] for _ in range(12)]
    if grads:
        small = VectorSum(vector[0].shape[1])
        small.bind(vector[0], vector_sum[0], take(len(small.scratch())))
        for k in range(6):
            ticks[k].append(functools.partial(small.stage, k))
        for k, tick in enumerate(plan_ticks(pairs, partials, sums, refs)):
            ticks[min(k, 11)].append(tick)
    ticks[0].append(move.start)
    ticks[11].append(move.finish)

    @pl.when(step == 0)
    def _():
        greet(sum_partners() if grads else move.partners())

    seq = query.shape[0]
    patch = jnp.where(resolution[lax.axis_index("blk")] == 1, patches[:, 1:2], patches[:, 0:1])
    rows_at = 128
    table = jnp.zeros((48, 128), F32)
    column = lax.broadcasted_iota(jnp.int32, (1, seq), 1)
    lane = lax.broadcasted_iota(jnp.int32, (1, 128), 1)
    edge = jnp.zeros((1, 128), F32)
    for h in range(2):
        for k in range(6):

            @pl.when(step == k)
            def _(at=2 * k + h):
                for tick in ticks[at]:
                    tick()

        at = slice(h * 64, h * 64 + 64)
        k = keys[:, at]
        v = values[:, at]
        dk = jnp.zeros((seq, 64), F32)
        dv = jnp.zeros((seq, 64), F32)
        inside = jnp.zeros((1, seq), F32)
        total = jnp.zeros((1, seq), F32)
        for r in range(0, seq, rows_at):
            rows = slice(r, r + rows_at)
            low = probs[h, rows, :]
            up = upstream[rows, at]
            weight = low.astype(F32)
            product = weight * matmul_t(up, v)
            ds = product - weight * jnp.sum(product, axis=-1, keepdims=True)
            ds_low = ds.astype(BF16)
            d_query[rows, at] = (matmul(ds_low, k) * 0.125).astype(BF16)
            dk += t_matmul(ds_low, query[rows, at] * 0.125)
            dv += t_matmul(low, up)
            total += jnp.sum(ds, axis=0, keepdims=True)
            ds = ds * patch[rows, :]
            score[rows, :] = ds
            inside += jnp.sum(ds, axis=0, keepdims=True)
        d_key[:, at] = dk.astype(BF16)
        d_value[:, at] = dv.astype(BF16)
        wide[...] = jnp.zeros_like(wide)
        for r in range(G_HIGH):
            rows = slice(r * G_HIGH, (r + 1) * G_HIGH)
            off = (G_HIGH - 1 - r) * G_HIGH
            wide[:, off : off + CELLS] += score[rows, 0:CELLS]
        codes = code[...]
        flat = jnp.zeros((48, SPAN), F32)
        for a in range(G_HIGH):
            flat += jnp.where(codes == a + G_HIGH - 1, wide[a : a + 1, :], 0.0)
        high = flat.astype(BF16)
        rest = flat - high.astype(F32)
        middle = rest.astype(BF16)
        last = (rest - middle.astype(F32)).astype(BF16)
        for part in (high, middle, last):
            table += matmul_t(part, spread[h])
        outside = total - inside
        top = jnp.sum(jnp.where(column < CELLS, outside, 0.0), axis=1, keepdims=True)
        side = jnp.sum(jnp.where(column == CELLS, inside, 0.0), axis=1, keepdims=True)
        corner = jnp.sum(jnp.where(column == CELLS, outside, 0.0), axis=1, keepdims=True)
        for i, value in enumerate((top, side, corner)):
            edge += jnp.where(lane == h * 64 + i, value, 0.0)
    table = jnp.concatenate([table[0:40], jnp.where(lax.broadcasted_iota(jnp.int32, (8, 128), 0) == 7, edge, table[40:48])], axis=0)
    is_high = resolution[lax.axis_index("blk")] == 1
    d_table[0, 0] = jnp.where(is_high, 0.0, table)
    d_table[1, 0] = jnp.where(is_high, table, 0.0)


def attention_back(resolution, qkv, probs, upstream, patches, spread, code, output, partials, counts, vector, count):
    seq = qkv.shape[0]
    width = qkv.shape[1] // 3
    steps = width // 128
    column = lambda part: pl.BlockSpec((seq, 128), lambda h: (0, part * steps + h))
    flat = jax.ShapeDtypeStruct((seq, width), BF16)
    views = [g.reshape(2, 2, 2, g.shape[0] // 8, g.shape[1]) for g in partials]
    pairs = sum_plan([v.shape[3:] for v in views], counts)
    sums = [jax.ShapeDtypeStruct((g.shape[0] // 32, g.shape[1]), F32) for g in partials]
    more = [vector] if partials else []
    scratch = [pltpu.VMEM((seq, seq), F32), pltpu.VMEM((G_HIGH, SPAN), F32)] + Exchange(count).scratch()
    if partials:
        scratch += VectorSum(vector.shape[1]).scratch()
    result = pl.pallas_call(
        functools.partial(backward_kernel, (count, pairs, len(partials))),
        grid=(steps,),
        out_shape=[flat, flat, flat, jax.ShapeDtypeStruct((2, steps, 48, 128), F32)]
        + [jax.ShapeDtypeStruct(output.shape, BF16)]
        + sums
        + [jax.ShapeDtypeStruct(v.shape, F32) for v in more],
        in_specs=[
            SMEM,
            column(0),
            column(1),
            column(2),
            pl.BlockSpec((2, seq, seq), lambda h: (h, 0, 0)),
            column(0),
            whole(patches.shape),
            whole(spread.shape),
            whole(code.shape),
            ANY,
        ]
        + [ANY] * len(views)
        + [whole(v.shape) for v in more],
        out_specs=[
            column(0),
            column(0),
            column(0),
            pl.BlockSpec((2, 1, 48, 128), lambda h: (0, h, 0, 0)),
            ANY,
        ]
        + [whole(s.shape) for s in sums]
        + [whole(v.shape) for v in more],
        scratch_shapes=scratch + plan_scratch(pairs),
        compiler_params=pltpu.CompilerParams(
            collective_id=2, has_side_effects=True, vmem_limit_bytes=60 << 20
        ),
        name="attention_back",
    )(resolution, qkv, qkv, qkv, probs, upstream, patches, spread, code, output, *views, *more)
    return result[:5], result[5 : 5 + len(sums)], result[5 + len(sums) :]


MESH = pl.DeviceIdType.MESH


def place():
    b, z = lax.axis_index("batch"), lax.axis_index("blk")
    return b, z, lax.rem(b, 2), lax.rem(b // 2, 2), b // 4


def greet(partners):
    barrier = pltpu.get_barrier_semaphore()
    for partner in partners:
        pl.semaphore_signal(barrier, inc=1, device_id=partner, device_id_type=MESH)
    pl.semaphore_wait(barrier, len(partners))


def sum_partners():
    b, z, c, x, y = place()
    near = [(b + 1 - 2 * c, z), (b + 2 - 4 * x, z), (b + 4 - 8 * y, z)]
    return near + [(b, lax.rem(z + s, 4)) for s in (1, 2, 3)]


class Exchange:
    def __init__(self, count):
        self.count = count

    def scratch(self):
        sems = pltpu.SemaphoreType.DMA((self.count - 1,))
        return [sems, sems, pltpu.SemaphoreType.DMA]

    def bind(self, source, target, refs):
        self.source, self.target = source, target
        self.sent, self.come, self.own = refs
        return self

    def partners(self):
        b, z = lax.axis_index("batch"), lax.axis_index("blk")
        return [(b, lax.rem(z + s, self.count)) for s in range(1, self.count)]

    def local(self):
        z = lax.axis_index("blk")
        return pltpu.make_async_copy(self.source.at[z], self.target.at[z], self.own)

    def copy(self, i):
        device = self.partners()[i]
        return pltpu.make_async_remote_copy(
            src_ref=self.source.at[device[1]],
            dst_ref=self.target.at[lax.axis_index("blk")],
            send_sem=self.sent.at[i],
            recv_sem=self.come.at[i],
            device_id=device,
            device_id_type=MESH,
        )

    def start(self):
        for i in range(self.count - 1):
            self.copy(i).start()
        self.local().start()

    def finish(self):
        self.local().wait()
        for i in range(self.count - 1):
            self.copy(i).wait_recv()
        for i in range(self.count - 1):
            self.copy(i).wait_send()


class VectorSum:
    def __init__(self, size):
        self.size = size

    def scratch(self):
        part = pltpu.VMEM((self.size, 128), F32)
        sems = pltpu.SemaphoreType.DMA((7,))
        return [part] * 5 + [pltpu.VMEM((4, self.size, 128), F32), part, part, sems, sems]

    def bind(self, source, target, refs):
        self.source, self.target = source, target
        self.got0, self.sum1, self.got1, self.sum2, self.got2, self.got3, self.mine, self.other, self.sent, self.come = refs
        return self

    def copy(self, i):
        b, z, c, x, y = place()
        to = sum_partners()
        source, target, device = (
            (self.source.at[1 - c], self.got0, to[0]),
            (self.sum1, self.got1, to[1]),
            (self.sum2, self.got2, to[2]),
            (self.got3.at[z], self.got3.at[z], to[3]),
            (self.got3.at[z], self.got3.at[z], to[4]),
            (self.got3.at[z], self.got3.at[z], to[5]),
            (self.mine, self.other, to[0]),
        )[i]
        return pltpu.make_async_remote_copy(
            src_ref=source,
            dst_ref=target,
            send_sem=self.sent.at[i],
            recv_sem=self.come.at[i],
            device_id=device,
            device_id_type=MESH,
        )

    def stage(self, number):
        b, z, c, x, y = place()
        if number == 0:
            self.copy(0).start()
        elif number == 1:
            self.copy(0).wait_recv()
            self.sum1[...] = self.source[c] + self.got0[...]
            self.copy(1).start()
        elif number == 2:
            self.copy(1).wait_recv()
            self.sum2[...] = self.sum1[...] + self.got1[...]
            self.copy(2).start()
        elif number == 3:
            self.copy(2).wait_recv()
            self.got3[z] = self.sum2[...] + self.got2[...]
            for i in (3, 4, 5):
                self.copy(i).start()
        elif number == 4:
            for i in (3, 4, 5):
                self.copy(i).wait_recv()
            self.mine[...] = self.got3[0] + self.got3[1] + self.got3[2] + self.got3[3]
            self.copy(6).start()
        else:
            self.copy(6).wait_recv()
            self.target[c] = self.mine[...]
            self.target[1 - c] = self.other[...]
            for i in range(7):
                self.copy(i).wait_send()


def in_steps(rows, width, body):
    step = rows
    while step * width > 49152 and step % 32 == 0:
        step //= 2
    if step == rows:
        body(pl.ds(0, rows))
    else:

        def one(i, carry):
            body(pl.ds(pl.multiple_of(i * step, step), step))
            return carry

        lax.fori_loop(0, rows // step, one, 0)


class WeightSum:
    COPIES = 6

    def __init__(self, rows, at, width, flip):
        self.rows, self.at, self.width, self.flip = rows, at, width, flip
        self.fold = 2 if (rows // 4) % 16 else 1

    def scratch(self):
        r, w, f = self.rows, self.width, self.fold
        strip = (r // 4 * f, w // f)
        return [
            pltpu.VMEM((2, 2, r, w), BF16),
            pltpu.VMEM((2, 2, r, w), BF16),
            pltpu.VMEM((2, r, w), BF16),
            pltpu.VMEM((r, w), BF16),
            pltpu.VMEM((4,) + strip, BF16),
            pltpu.VMEM((3,) + strip, BF16),
            pltpu.SemaphoreType.DMA((self.COPIES,)),
            pltpu.SemaphoreType.DMA((self.COPIES,)),
            pltpu.SemaphoreType.DMA,
        ]

    def bind(self, grad, out, refs):
        self.grad, self.out = grad, out
        self.keep, self.got0, self.got1, self.got2, self.mine, self.got3, self.sent, self.come, self.own = refs
        return self

    def local(self):
        c = place()[2]
        return pltpu.make_async_copy(
            self.grad.at[:, :, c, :, pl.ds(self.at, self.width)], self.keep, self.own
        )

    def copy(self, i):
        b, z, c, x, y = place()
        to = sum_partners()
        if i == 0:
            source, target, device = self.grad.at[:, :, 1 - c, :, pl.ds(self.at, self.width)], self.got0, to[0]
        elif i == 1:
            source = self.keep.at[1 - y] if self.flip else self.keep.at[:, 1 - x]
            target, device = self.got1, to[2 if self.flip else 1]
        elif i == 2:
            source = self.keep.at[y, 1 - x] if self.flip else self.keep.at[1 - y, x]
            target, device = self.got2, to[1 if self.flip else 2]
        else:
            source, target, device = self.mine.at[lax.rem(z + i - 2, 4)], self.got3.at[i - 3], to[i]
        return pltpu.make_async_remote_copy(
            src_ref=source,
            dst_ref=target,
            send_sem=self.sent.at[i],
            recv_sem=self.come.at[i],
            device_id=device,
            device_id_type=MESH,
        )

    def add(self, target, source):
        def body(rows):
            target[rows, :] = (target[rows, :].astype(F32) + source[rows, :].astype(F32)).astype(BF16)

        in_steps(self.rows, self.width, body)

    def stage(self, number):
        b, z, c, x, y = place()
        keep, got0, got1 = self.keep, self.got0, self.got1
        if number == 0:
            self.local().start()
            self.copy(0).start()
        elif number == 1:
            self.local().wait()
            self.copy(0).wait_recv()
            spots = lambda k: [(k, 0), (k, 1)] if self.flip else [(0, k), (1, k)]
            mine = y if self.flip else x
            for i, j in spots(1 - mine):
                self.add(keep.at[i, j], got0.at[i, j])
            self.copy(1).start()
            for i, j in spots(mine):
                self.add(keep.at[i, j], got0.at[i, j])
        elif number == 2:
            self.copy(1).wait_recv()
            if self.flip:
                self.add(keep.at[y, 1 - x], got1.at[1 - x])
                self.copy(2).start()
                self.add(keep.at[y, x], got1.at[x])
            else:
                self.add(keep.at[1 - y, x], got1.at[1 - y])
                self.copy(2).start()
                self.add(keep.at[y, x], got1.at[y])
        elif number == 3:
            self.copy(2).wait_recv()
            r = self.rows // 4
            for k in range(4):
                rows = slice(k * r, k * r + r)
                value = keep[y, x, rows, :].astype(F32) + self.got2[rows, :].astype(F32)
                if self.fold == 2:
                    half = self.width // 2
                    value = jnp.concatenate([value[:, :half], value[:, half:]], axis=0)
                self.mine[k] = value.astype(BF16)
            for i in (3, 4, 5):
                self.copy(i).start()
        elif number == 4:
            for i in (3, 4, 5):
                self.copy(i).wait_recv()
            value = self.mine[z].astype(F32)
            for k in range(3):
                value += self.got3[k].astype(F32)
            r, half = self.rows // 4, self.width // 2
            if self.fold == 2:
                self.out[:, self.at : self.at + half] = value[:r]
                self.out[:, self.at + half : self.at + self.width] = value[r:]
            else:
                self.out[:, self.at : self.at + self.width] = value
        else:
            for i in range(self.COPIES):
                self.copy(i).wait_send()


def wave(count, depth):
    ticks = []
    for t in range(count + depth - 1):
        ticks.append([(t - s, s) for s in reversed(range(depth)) if 0 <= t - s < count])
    return ticks


def sum_plan(shapes, counts):
    pairs = []
    for n, ((rows, width), count) in enumerate(zip(shapes, counts)):
        unit = 256 if (rows // 4) % 16 else 128
        units = width // unit
        edges = [unit * (units * k // (2 * count)) for k in range(2 * count + 1)]
        for k in range(count):
            pairs.append([
                (n, WeightSum(rows, edges[2 * k + f], edges[2 * k + f + 1] - edges[2 * k + f], f == 1))
                for f in (0, 1)
            ])
    return pairs


def plan_scratch(pairs):
    return [s for pair in pairs for _, part in pair for s in part.scratch()]


def plan_ticks(pairs, grads, outs, scratch):
    parts, k = [], 0
    for pair in pairs:
        parts.append([])
        for n, part in pair:
            parts[-1].append(part.bind(grads[n], outs[n], scratch[9 * k : 9 * k + 9]))
            k += 1

    def tick(steps):
        for pair, stage in steps:
            for part in parts[pair]:
                part.stage(stage)

    def finish():
        for pair in parts:
            for part in pair:
                part.stage(5)

    return [functools.partial(tick, steps) for steps in wave(len(pairs), 5)] + [finish]


def final_kernel(setup, *refs):
    count, pairs, grads, vectors = setup
    refs = list(refs)
    take = lambda n: [refs.pop(0) for _ in range(n)]
    source = take(1)[0]
    partials, parts = take(grads), take(vectors)
    target = take(1)[0]
    sums, totals = take(grads), take(vectors)
    move = Exchange(count)
    move.bind(source, target, take(len(move.scratch())))
    greet(sum_partners() if grads else move.partners())
    small = []
    for part, total in zip(parts, totals):
        small.append(VectorSum(part.shape[1]))
        small[-1].bind(part, total, take(len(small[-1].scratch())))
    for k, tick in enumerate(plan_ticks(pairs, partials, sums, refs) if grads else []):
        if k < 6:
            for one in small:
                one.stage(k)
        tick()
        if k == 0:
            move.start()
    if not grads:
        move.start()
    move.finish()


def final(source, partials, counts, vectors, count):
    views = [g.reshape(2, 2, 2, g.shape[0] // 8, g.shape[1]) for g in partials]
    pairs = sum_plan([v.shape[3:] for v in views], counts)
    vmem = pl.BlockSpec(memory_space=pltpu.VMEM)
    scratch = Exchange(count).scratch()
    for v in vectors:
        scratch += VectorSum(v.shape[1]).scratch()
    result = pl.pallas_call(
        functools.partial(final_kernel, (count, pairs, len(partials), len(vectors))),
        out_shape=[jax.ShapeDtypeStruct(source.shape, BF16)]
        + [jax.ShapeDtypeStruct((g.shape[0] // 32, g.shape[1]), F32) for g in partials]
        + [jax.ShapeDtypeStruct(v.shape, F32) for v in vectors],
        in_specs=[ANY] + [ANY] * len(views) + [vmem] * len(vectors),
        out_specs=[ANY] + [vmem] * (len(views) + len(vectors)),
        scratch_shapes=scratch + plan_scratch(pairs),
        compiler_params=pltpu.CompilerParams(
            collective_id=3, has_side_effects=True, vmem_limit_bytes=56 << 20
        ),
        name="final",
    )(source, *views, *vectors)
    return result[0], result[1 : 1 + len(views)], result[1 + len(views) :]


def swap(value, axis, bit, count):
    return lax.ppermute(value, axis, [(i, i ^ bit) for i in range(count)])


def bits_of(count):
    return [1 << i for i in range(count.bit_length() - 1)]


def scatter_sum(grad, batch, blk):
    places = [("batch", bit, batch) for bit in bits_of(batch)][::-1]
    places += [("blk", bit, blk) for bit in bits_of(blk)][::-1]
    value = grad.reshape((2,) * len(places) + (grad.shape[0] >> len(places), grad.shape[1]))
    left = list(places)
    for spot in places:
        axis, bit, count = spot
        at = left.index(spot)
        left.remove(spot)
        mine = jnp.bitwise_and(lax.axis_index(axis) // bit, 1)
        sent = lax.dynamic_index_in_dim(value, 1 - mine, at, keepdims=False)
        kept = lax.dynamic_index_in_dim(value, mine, at, keepdims=False)
        got = swap(sent, axis, bit, count)
        value = kept.astype(F32) + got.astype(F32)
        if left:
            value = value.astype(BF16)
    return value


def total_sum(value, batch, blk):
    for bit in bits_of(batch):
        value = value + swap(value, "batch", bit, batch)
    for bit in bits_of(blk):
        value = value + swap(value, "blk", bit, blk)
    return value


def packed(parts):
    flat = jnp.concatenate([p.reshape(-1) for p in parts])
    size = flat.shape[0]
    rows = -(-size // 2048) * 8
    return jnp.pad(flat, (0, 2 * rows * 128 - size)).reshape(2, rows, 128)


def unpacked(value, shapes):
    flat = value.reshape(-1)
    result, at = [], 0
    for shape in shapes:
        size = int(np.prod(shape))
        result.append(flat[at : at + size].reshape(shape))
        at += size
    return result


def shards(
    batch,
    blk,
    tokens,
    resolution,
    positions,
    ln1_gain,
    ln1_bias,
    w_qkv,
    q_bias,
    v_bias,
    w_proj,
    proj_bias,
    gamma1,
    ln2_gain,
    ln2_bias,
    w_fc1,
    fc1_bias,
    w_fc2,
    fc2_bias,
    gamma2,
    rel_low,
    rel_high,
    grad_out,
):
    images, rows, width = tokens.shape
    seq = positions.shape[1]
    heads = rel_low.shape[1]
    assert images == blk and rows * blk == seq and width == heads * 64
    me = lax.axis_index("blk")

    direct = (batch, blk) == (8, 4)
    spread_np, code_np = lane_tables()
    spread = jnp.asarray(spread_np, BF16)
    code = jnp.asarray(code_np)
    patches = jnp.asarray(slot_tables(seq)[2].T, F32)
    bias, to_slot, raw = prepare(
        resolution, positions, rel_low, rel_high, spread, code, patches, tokens, blk
    )
    inputs = matmul(to_slot, raw.reshape(seq, width))

    gain1 = ln1_gain.astype(F32)
    gain2 = ln2_gain.astype(F32)
    scale1_layer = gamma1.astype(F32)
    scale2_layer = gamma2.astype(F32)
    normed1, factor1 = layer_stats(inputs)
    hidden1 = (normed1 * gain1 + ln1_bias.astype(F32)).astype(BF16)
    qkv_shift = jnp.concatenate([q_bias, jnp.zeros_like(q_bias), v_bias]).astype(F32)
    qkv = (matmul(hidden1, w_qkv) + qkv_shift).astype(BF16)
    probs, mixed, raw_up = attention(qkv, bias, grad_out, blk)
    attn = matmul(mixed, w_proj) + proj_bias.astype(F32)
    resid = inputs + scale1_layer * attn
    normed2, factor2 = layer_stats(resid)
    hidden2 = (normed2 * gain2 + ln2_bias.astype(F32)).astype(BF16)
    pre = matmul(hidden2, w_fc1) + fc1_bias.astype(F32)
    act = jax.nn.gelu(pre, approximate=False).astype(BF16)
    branch = matmul(act, w_fc2) + fc2_bias.astype(F32)
    out_slot = (resid + scale2_layer * branch).astype(BF16)
    out_blocks = t_matmul(to_slot, out_slot).astype(BF16).reshape(blk, rows, width)

    upstream = matmul(to_slot, raw_up.reshape(seq, width))
    d_gamma2 = jnp.sum(upstream * branch, axis=0)
    d_branch = (scale2_layer * upstream).astype(BF16)
    p_fc2 = t_matmul(act, d_branch).astype(BF16)
    d_fc2b = jnp.sum(d_branch.astype(F32), axis=0)
    d_pre = (matmul_t(d_branch, w_fc2) * gelu_slope(pre)).astype(BF16)
    p_fc1 = t_matmul(hidden2, d_pre).astype(BF16)
    d_fc1b = jnp.sum(d_pre.astype(F32), axis=0)
    d_hidden2 = matmul_t(d_pre, w_fc1)
    d_ln2g = jnp.sum(d_hidden2 * normed2, axis=0)
    d_ln2b = jnp.sum(d_hidden2, axis=0)
    d_resid = upstream + norm_back(d_hidden2, normed2, factor2, gain2)
    d_gamma1 = jnp.sum(d_resid * attn, axis=0)
    d_attn = (scale1_layer * d_resid).astype(BF16)
    p_proj = t_matmul(mixed, d_attn).astype(BF16)
    d_projb = jnp.sum(d_attn.astype(F32), axis=0)
    d_mixed = matmul_t(d_attn, w_proj).astype(BF16)
    early = [d_gamma2, d_fc2b, d_fc1b, d_ln2g, d_ln2b, d_gamma1, d_projb]
    early_pack = packed(early)
    first = [p_fc2, p_fc1, p_proj]
    (d_query, d_key, d_value, d_table, output), sums, more = attention_back(
        resolution,
        qkv,
        probs,
        d_mixed,
        patches,
        spread,
        code,
        out_blocks,
        first if direct else [],
        [3, 3, 1] if direct else [],
        early_pack,
        blk,
    )
    if direct:
        (g_fc2, g_fc1, g_proj), (early_sum,) = sums, more
    else:
        g_fc2, g_fc1, g_proj = [scatter_sum(g, batch, blk) for g in first]
        early_sum = total_sum(early_pack, batch, blk)
    d_qkv = jnp.concatenate([d_query, d_key, d_value], axis=1)
    p_qkv = t_matmul(hidden1, d_qkv).astype(BF16)
    d_qb = jnp.sum(d_query.astype(F32), axis=0)
    d_vb = jnp.sum(d_value.astype(F32), axis=0)
    d_hidden1 = matmul_t(d_qkv, w_qkv)
    d_ln1g = jnp.sum(d_hidden1 * normed1, axis=0)
    d_ln1b = jnp.sum(d_hidden1, axis=0)
    d_inputs = (d_resid + norm_back(d_hidden1, normed1, factor1, gain1)).astype(BF16)
    token_blocks = t_matmul(to_slot, d_inputs).astype(BF16).reshape(blk, rows, width)
    late = [d_ln1g, d_ln1b, d_qb, d_vb]
    vectors = [packed(late), d_table.reshape(2, -1, 128)]
    grad_tokens, sums, totals = final(
        token_blocks, [p_qkv] if direct else [], [2] if direct else [], vectors if direct else [], blk
    )
    if direct:
        g_qkv = sums[0]
    else:
        g_qkv = scatter_sum(p_qkv, batch, blk)
        totals = [total_sum(v, batch, blk) for v in vectors]
    late_sum, s_table = totals

    s_table = s_table.reshape(2, heads // 2, 48, 2, 64).transpose(0, 1, 3, 4, 2).reshape(2, heads, 64, 48)
    tops = s_table[:, :, 0:3, 47]
    offsets = s_table[:, :, SIDE - 1 :: -1, :SIDE]
    pad = G_HIGH - G_LOW
    small = offsets[0, :, pad : pad + SIDE_LOW, pad : pad + SIDE_LOW].reshape(heads, -1)
    s_low = jnp.concatenate([small, tops[0]], axis=1)
    s_high = jnp.concatenate([offsets[1].reshape(heads, -1), tops[1]], axis=1)

    s_gamma2, s_fc2b, s_fc1b, s_ln2g, s_ln2b, s_gamma1, s_projb = unpacked(
        early_sum, [p.shape for p in early]
    )
    s_ln1g, s_ln1b, s_qb, s_vb = unpacked(late_sum, [p.shape for p in late])
    return (
        output,
        grad_tokens,
        s_ln1g,
        s_ln1b,
        g_qkv,
        s_qb,
        s_vb,
        g_proj,
        s_projb,
        s_gamma1,
        s_ln2g,
        s_ln2b,
        g_fc1,
        s_fc1b,
        g_fc2,
        s_fc2b,
        s_gamma2,
        s_low.T,
        s_high.T,
    )


def solution(mesh):
    rows = P("batch", "blk", None)
    shared = P(("batch", "blk"), None)
    in_specs = (rows, P("batch"), P("batch", None)) + (P(),) * 17 + (rows,)
    out_specs = (
        (rows, rows, P(), P(), shared, P(), P(), shared)
        + (P(),) * 4
        + (shared, P(), shared)
        + (P(),) * 4
    )
    return jax.shard_map(
        functools.partial(shards, mesh.shape["batch"], mesh.shape["blk"]),
        mesh=mesh,
        in_specs=in_specs,
        out_specs=out_specs,
        check_vma=False,
    )
```

```python
import functools

import jax
import jax.numpy as jnp
import numpy as np
from jax import lax
from jax.experimental import pallas as pl
from jax.experimental.pallas import tpu as pltpu
from jax.sharding import PartitionSpec as P

G_LOW = 14
G_HIGH = 24
SIDE_LOW = 2 * G_LOW - 1
SIDE = 2 * G_HIGH - 1
CELLS = G_HIGH * G_HIGH
SPAN = 1152
F32 = jnp.float32
BF16 = jnp.bfloat16


def normalize(values):
    center = values - jnp.mean(values, axis=-1, keepdims=True)
    factor = lax.rsqrt(jnp.mean(center * center, axis=-1, keepdims=True) + 1e-06)
    return center * factor, factor


def norm_back(grad, normed, factor, gain):
    scaled = grad * gain
    return factor * (
        scaled
        - jnp.mean(scaled, axis=-1, keepdims=True)
        - normed * jnp.mean(scaled * normed, axis=-1, keepdims=True)
    )


def matmul(left, right):
    return jnp.dot(left, right, preferred_element_type=F32)


def matmul_t(left, right):
    return lax.dot_general(left, right, (((1,), (1,)), ((), ())), preferred_element_type=F32)


def t_matmul(left, right):
    return lax.dot_general(left, right, (((0,), (0,)), ((), ())), preferred_element_type=F32)


def slot_tables(seq):
    tokens = np.arange(seq)
    tables = []
    for grid in (G_LOW, G_HIGH):
        cells = np.arange(CELLS)
        used = (cells // G_HIGH < grid) & (cells % G_HIGH < grid)
        free = np.concatenate([cells[~used], np.arange(CELLS + 1, seq)])
        slot = np.full(seq, CELLS)
        slot[1 + grid * grid :] = free
        patch = np.concatenate([used, np.zeros(seq - CELLS, bool)])
        key = patch.copy()
        key[CELLS] = True
        tables.append((slot, (tokens >= 1) & (tokens < 1 + grid * grid), patch, key))
    return [np.stack(parts) for parts in zip(*tables)]


def lane_tables():
    lanes = np.arange(SPAN)
    spread = (lanes[None, :] // G_HIGH == np.arange(128)[:, None]) & (np.arange(128)[:, None] < SIDE)
    shift = G_HIGH - 1 - lanes % G_HIGH
    bits = (shift[None, :] >> np.arange(8)[:, None]) & 1
    return np.stack([spread, np.roll(spread, 64, axis=0)]), bits.astype(np.int32)


def slide(values, bits, down):
    for k in range(5):
        amount = 1 << k if down else 48 - (1 << k)
        values = jnp.where(bits[k : k + 1, :] > 0, pltpu.roll(values, amount, 0), values)
    return values


VMEM_LIMIT = 62 << 20


def whole(shape):
    return pl.BlockSpec(shape, lambda h: (0,) * len(shape))


ANY = pl.BlockSpec(memory_space=pl.ANY)
SMEM = pl.BlockSpec(memory_space=pltpu.SMEM)


def flat_row(ref):
    return ref[...].astype(F32).reshape(1, ref.shape[0])


def front_kernel(
    count, resolution, cells, low_t, high_t, spread, bits, slot_of, is_patch, patches, masks,
    ln1_gain, ln1_bias, q_bias, v_bias, w_qkv, tokens, grad_out,
    to_slot, inputs, qkv, probs, mixed, raw_up, bias, raw, inner_low, inner_high, wide, full, *refs,
):
    step = pl.program_id(0)
    me = lax.axis_index("blk")
    high = resolution[me] == 1
    seq = full.shape[0]
    heads = low_t.shape[0]
    width = inputs.shape[1]
    size = len(Exchange(count).scratch())
    move = Exchange(count).bind(tokens, raw, refs[:size])
    move_up = Exchange(count).bind(grad_out, raw_up, refs[size:])

    @pl.when(step == 0)
    def _():
        greet(move.partners())
        move.start()
        here = cells[pl.ds(me, 1), :]
        grid = jnp.where(high, G_HIGH, G_LOW)
        row = jnp.zeros_like(here)
        for k in range(1, G_HIGH):
            row += (here >= k * grid).astype(jnp.int32)
        at = row * G_HIGH + here - row * grid
        patch = jnp.where(high, is_patch[1:2, :], is_patch[0:1, :])
        other = jnp.where(high, slot_of[1:2, :], slot_of[0:1, :])
        slot = jnp.where(patch > 0, at, other)
        spots = lax.broadcasted_iota(jnp.int32, (seq, seq), 0)
        to_slot[...] = jnp.where(spots == slot, 1.0, 0.0).astype(BF16)
        inner_low[...] = jnp.zeros_like(inner_low)
        inner_high[...] = jnp.zeros_like(inner_high)
        low_f, high_f = low_t[...].astype(F32), high_t[...].astype(F32)
        pad = G_HIGH - G_LOW
        for j in range(SIDE):
            r = SIDE - 1 - j
            inner_high[j * 16 : j * 16 + heads, 0:SIDE] = high_f[:, r * SIDE : (r + 1) * SIDE]
            r -= pad
            if 0 <= r < SIDE_LOW:
                inner_low[j * 16 : j * 16 + heads, pad : pad + SIDE_LOW] = low_f[
                    :, r * SIDE_LOW : (r + 1) * SIDE_LOW
                ]

    @pl.when(step < heads)
    def _():
        rows = pl.ds(step, 48, stride=16)
        table = jnp.where(high, inner_high[rows, :], inner_low[rows, :]).astype(BF16)
        wide[...] = slide(t_matmul(table, spread[0, 0:48, :])[0:48], bits, False)[0:G_HIGH]
        for r in range(G_HIGH):
            at = (G_HIGH - 1 - r) * G_HIGH
            full[r * G_HIGH : (r + 1) * G_HIGH, 0:CELLS] = wide[:, at : at + CELLS]
        column = lax.broadcasted_iota(jnp.int32, (1, seq), 1)
        ends = [t[:, t.shape[1] - 3 : t.shape[1]].astype(F32) for t in (low_t, high_t)]
        special = jnp.where(high, ends[1], ends[0])
        here = lax.broadcasted_iota(jnp.int32, special.shape, 0) == step
        special = jnp.sum(jnp.where(here, special, 0.0), axis=0, keepdims=True)
        inner_row = jnp.where(column < CELLS, special[:, 0:1], special[:, 2:3])
        values = jnp.where(column < CELLS, full[...], special[:, 1:2])
        patch = jnp.where(high, patches[:, 1:2], patches[:, 0:1])
        mask = jnp.where(high, masks[1:2, :], masks[0:1, :])
        values = jnp.where(patch > 0.0, values, inner_row)
        bias[step] = (values + mask).astype(BF16)

    @pl.when(step == heads)
    def _():
        move.finish()
        move_up.start()
        value = matmul(to_slot[...], raw[...].reshape(seq, width))
        inputs[...] = value
        hidden = (normalize(value)[0] * flat_row(ln1_gain) + flat_row(ln1_bias)).astype(BF16)
        shifts = [flat_row(q_bias), 0.0, flat_row(v_bias)]
        for n in range(3):
            part = slice(n * width, (n + 1) * width)
            qkv[:, part] = (matmul(hidden, w_qkv[:, part]) + shifts[n]).astype(BF16)

    @pl.when(step >= heads)
    def _():
        pair = step - heads
        query, keys, values = [
            qkv[:, pl.ds(pl.multiple_of(n * width + pair * 128, 128), 128)] for n in range(3)
        ]
        for h in range(2):
            at = slice(h * 64, h * 64 + 64)
            scores = matmul_t(query[:, at] * 0.125, keys[:, at]) + bias[2 * pair + h].astype(F32)
            expo = jnp.exp(scores - jnp.max(scores, axis=-1, keepdims=True))
            low = (expo * (1.0 / jnp.sum(expo, axis=-1, keepdims=True))).astype(BF16)
            probs[h] = low
            mixed[:, at] = matmul(low, values[:, at]).astype(BF16)

    @pl.when(step == pl.num_programs(0) - 1)
    def _():
        move_up.finish()


def front(resolution, cells, rel_low, rel_high, spread, bits, patches, vectors, w_qkv, tokens, grad_out, count):
    heads = rel_low.shape[1]
    seq = cells.shape[1]
    width = w_qkv.shape[0]
    slot_np, token_np, _, key_np = slot_tables(seq)
    slot_of = jnp.asarray(slot_np, jnp.int32)
    is_patch = jnp.asarray(token_np, jnp.int32)
    masks = jnp.asarray(np.where(key_np, 0.0, -1e30), F32)
    operands = (rel_low.T, rel_high.T, spread, bits, slot_of, is_patch, patches, masks) + vectors + (w_qkv,)
    late = lambda i: jnp.maximum(i - heads, 0)
    return pl.pallas_call(
        functools.partial(front_kernel, count),
        grid=(heads + heads // 2,),
        out_shape=(
            jax.ShapeDtypeStruct((seq, seq), BF16),
            jax.ShapeDtypeStruct((seq, width), F32),
            jax.ShapeDtypeStruct((seq, 3 * width), BF16),
            jax.ShapeDtypeStruct((heads, seq, seq), BF16),
            jax.ShapeDtypeStruct((seq, width), BF16),
            jax.ShapeDtypeStruct(grad_out.shape, BF16),
        ),
        in_specs=[SMEM, whole(cells.shape)] + [whole(o.shape) for o in operands] + [ANY, ANY],
        out_specs=(
            whole((seq, seq)),
            whole((seq, width)),
            whole((seq, 3 * width)),
            pl.BlockSpec((2, seq, seq), lambda i: (late(i), 0, 0)),
            pl.BlockSpec((seq, 128), lambda i: (0, late(i))),
            ANY,
        ),
        scratch_shapes=[
            pltpu.VMEM((heads, seq, seq), BF16),
            pltpu.VMEM(tokens.shape, BF16),
            pltpu.VMEM((48 * 16, 128), F32),
            pltpu.VMEM((48 * 16, 128), F32),
            pltpu.VMEM((G_HIGH, SPAN), F32),
            pltpu.VMEM((seq, seq), F32),
        ]
        + Exchange(count).scratch()
        + Exchange(count).scratch(),
        compiler_params=pltpu.CompilerParams(
            collective_id=0, has_side_effects=True, vmem_limit_bytes=VMEM_LIMIT
        ),
        name="front",
    )(resolution, cells, *operands, tokens, grad_out)


def head_grads(query, keys, values, weights, up, patch, spread, bits, score, wide, lanes):
    ups = matmul_t(up, values)
    weight = weights.astype(F32)
    product = weight * ups
    ds = product - weight * jnp.sum(product, axis=-1, keepdims=True)
    ds_low = ds.astype(BF16)
    d_query = (matmul(ds_low, keys) * 0.125).astype(BF16)
    d_key = t_matmul(ds_low, query * 0.125).astype(BF16)
    d_value = t_matmul(weights, up).astype(BF16)
    total = jnp.sum(ds, axis=0, keepdims=True)
    ds = ds * patch
    score[...] = ds
    inside = jnp.sum(ds, axis=0, keepdims=True)
    wide[...] = jnp.zeros_like(wide)
    for r in range(G_HIGH):
        off = (G_HIGH - 1 - r) * G_HIGH
        wide[:, off : off + CELLS] += score[r * G_HIGH : (r + 1) * G_HIGH, 0:CELLS]
    flat = slide(jnp.concatenate([wide[...], jnp.zeros_like(wide)], axis=0), bits, True)
    first = flat.astype(BF16)
    rest = flat - first.astype(F32)
    second = rest.astype(BF16)
    third = (rest - second.astype(F32)).astype(BF16)
    table = matmul_t(first, spread) + matmul_t(second, spread) + matmul_t(third, spread)
    column = lax.broadcasted_iota(jnp.int32, total.shape, 1)
    lane = lax.broadcasted_iota(jnp.int32, (1, 128), 1)
    outside = total - inside
    edge = jnp.zeros((1, 128), F32)
    for i, value in enumerate((
        jnp.where(column < CELLS, outside, 0.0),
        jnp.where(column == CELLS, inside, 0.0),
        jnp.where(column == CELLS, outside, 0.0),
    )):
        edge += jnp.where(lane == lanes + i, jnp.sum(value, axis=1, keepdims=True), 0.0)
    return d_query, d_key, d_value, table, edge


def by_lanes(row):
    return jnp.concatenate([row[:, i : i + 128] for i in range(0, row.shape[1], 128)], axis=0)


def tail_kernel(setup, *refs):
    count, pairs, last_pairs, grads = setup
    direct = grads > 0
    refs = list(refs)
    take = lambda n: [refs.pop(0) for _ in range(n)]
    resolution, query, keys, values, probs, upstream, patches, spread, bits, ln1_gain, ln1_bias = take(11)
    output, *sources = take(5)
    partials = take(grads)
    early = take(1) if direct else []
    moved_output, moved_tokens, g_qkv = take(3)
    sums = take(grads)
    early_sum = take(1) if direct else []
    late_sum, table_sum = take(2)
    score, wide, d_qkv, table, tokens, late = take(6)
    loaded = take(4)
    load_sems = take(1)[0]
    size = len(Exchange(count).scratch())
    move_out = Exchange(count).bind(output, moved_output, take(size))
    move = Exchange(count).bind(tokens, moved_tokens, take(size))
    step = pl.program_id(0)
    steps = pl.num_programs(0) - 1
    seq, width = loaded[0].shape
    slots = [[] for _ in range(12)]
    closing = []
    if direct:
        grad = take(1)[0]
        tables, vectors, small = [VectorSum(v.shape[1:], low) for v, low in ((table, True), (late, False), (early[0], False))]
        tables.bind(table, table_sum, take(len(tables.scratch())))
        vectors.bind(late, late_sum, take(len(vectors.scratch())))
        small.bind(early[0], early_sum[0], take(len(small.scratch())))
        parts = []
        for pair in pairs:
            parts.append([])
            for n, part in pair:
                parts[-1].append(part.bind(partials[n], sums[n], take(len(part.scratch()))))
        last_parts = []
        for pair in last_pairs:
            last_parts.append([])
            for part in pair:
                last_parts[-1].append(part.bind(grad, g_qkv, take(len(part.scratch()))))
        for k in range(small.STAGES):
            slots[k].append(functools.partial(small.stage, k))
        for k, tick in enumerate(part_ticks(parts, 0, 4)):
            slots[k].append(tick)
        closing += part_ticks(parts, 4, 7)
        slots[11].append(closing.pop(0))
    slots[1].append(move_out.start)
    loads = [
        pltpu.make_async_copy(source, target, load_sems.at[i])
        for i, (source, target) in enumerate(zip(sources, loaded))
    ]

    @pl.when(step == 0)
    def _():
        greet(sum_partners() if direct else move.partners())
        for load in loads:
            load.start()

    high = resolution[lax.axis_index("blk")] == 1

    @pl.when(step < steps)
    def _():
        patch = jnp.where(high, patches[:, 1:2], patches[:, 0:1])
        total = jnp.zeros((48, 128), F32)
        edge = jnp.zeros((1, 128), F32)
        parts3 = [[], [], []]
        for h in range(2):
            for k in range(6):

                @pl.when(step == k)
                def _(at=2 * k + h):
                    for tick in slots[at]:
                        tick()

            at = slice(h * 64, h * 64 + 64)
            *heads3, part, ends = head_grads(
                query[:, at], keys[:, at], values[:, at], probs[h], upstream[:, at],
                patch, spread[h], bits, score, wide, h * 64,
            )
            total += part
            edge += ends
            for n in range(3):
                parts3[n].append(heads3[n])
        for n in range(3):
            at = pl.ds(pl.multiple_of(n * width + step * 128, 128), 128)
            d_qkv[:, at] = jnp.concatenate(parts3[n], axis=1)
        row = lax.broadcasted_iota(jnp.int32, (48, 128), 0)
        total = jnp.where(row == 47, edge, total)
        at = pl.ds(pl.multiple_of(step * 48, 16), 48)
        table[0, at, :] = jnp.where(high, 0.0, total)
        table[1, at, :] = jnp.where(high, total, 0.0)

    @pl.when(step == steps)
    def _():
        if direct:
            tables.stage(0)
        for load in loads:
            load.wait()
        inputs, d_resid, to_slot, w_qkv = loaded
        gain, shift = flat_row(ln1_gain), flat_row(ln1_bias)
        d_gain = d_shift = jnp.zeros((1, width), F32)
        lows = []
        for n, r in enumerate(range(0, seq, seq // 2)):
            rows = slice(r, r + seq // 2)
            back = matmul_t(d_qkv[rows, :], w_qkv[...])
            value, scale = normalize(inputs[rows, :])
            d_gain += row_sum(back * value)
            d_shift += row_sum(back)
            lows.append((d_resid[rows, :] + norm_back(back, value, scale, gain)).astype(BF16))
            if direct:
                tables.stage(n + 1)
        ordered = t_matmul(to_slot[...], jnp.concatenate(lows, axis=0)).astype(BF16)
        tokens[...] = ordered.reshape(tokens.shape)
        sums4 = [d_gain, d_shift] + [
            row_sum(d_qkv[:, n * width : (n + 1) * width].astype(F32)) for n in (0, 2)
        ]
        for n in range(2):
            both = [by_lanes(v) for v in sums4[2 * n : 2 * n + 2]] + [jnp.zeros((4, 128), F32)]
            late[n] = jnp.concatenate(both, axis=0)
        if direct:
            vectors.stage(0)
            vectors.stage(1)
        move.start()
        hidden = (normalize(inputs[...])[0] * gain + shift).astype(BF16)
        ticks = part_ticks(last_parts, 0, 7) if direct else []
        for n in range(3):
            part = slice(n * width, (n + 1) * width)
            partial = t_matmul(hidden, d_qkv[:, part]).astype(BF16)
            if direct:
                grad[:, :, :, :, part] = partial.reshape(2, 2, 2, width // 8, width)
                for _ in range((1, 2, 2)[n]):
                    ticks.pop(0)()
                if n == 0:
                    tables.stage(3)
                    vectors.stage(2)
                elif n == 1:
                    tables.stage(4)
                    vectors.stage(3)
            else:
                g_qkv[:, part] = partial
        if direct:
            tables.stage(5)
            ticks.pop(0)()
            vectors.stage(4)
            for tick in closing[:-1]:
                tick()
            for tick in ticks:
                tick()
            vectors.stage(5)
            closing[-1]()
        else:
            late_sum[...] = late[...]
            table_sum[...] = table[...]
        move_out.finish()
        move.finish()


def tail(resolution, qkv, probs, upstream, patches, spread, bits, vectors, output, inputs, d_resid, to_slot, w_qkv, partials, plan, early, count):
    seq, width = inputs.shape
    steps = width // 128
    direct = bool(partials)
    clip = lambda h: jnp.minimum(h, steps - 1)
    column = lambda part: pl.BlockSpec((seq, 128), lambda h: (0, part * steps + clip(h)))
    views = [g.reshape(2, 2, 2, g.shape[0] // 8, g.shape[1]) for g in partials]
    pairs = sum_plan([v.shape[3:] for v in views], plan)
    sums = [jax.ShapeDtypeStruct((g.shape[0] // 32, g.shape[1]), F32) for g in partials]
    last_pairs = []
    if direct:
        edges = list(range(0, 3 * width, 256)) + [3 * width]
        spans = list(zip(edges[:-1], edges[1:]))
        for k in range(0, len(spans), 2):
            last_pairs.append([
                WeightSum(width // 8, lo, hi - lo, f == 1, True) for f, (lo, hi) in enumerate(spans[k : k + 2])
            ])
    blocks = jax.ShapeDtypeStruct(output.shape, BF16)
    late, table = (2, 16, 128), (2, 48 * steps, 128)
    more = [early] if direct else []
    outs = sums + [jax.ShapeDtypeStruct(early.shape, F32) for _ in more]
    outs += [jax.ShapeDtypeStruct(late, F32), jax.ShapeDtypeStruct(table, F32)]
    g_qkv = (
        jax.ShapeDtypeStruct((width // 32, 3 * width), F32)
        if direct
        else jax.ShapeDtypeStruct((width, 3 * width), BF16)
    )
    held = (inputs, d_resid, to_slot, w_qkv)
    scratch = [
        pltpu.VMEM((seq, seq), F32),
        pltpu.VMEM((G_HIGH, SPAN), F32),
        pltpu.VMEM((seq, 3 * width), BF16),
        pltpu.VMEM(table, F32),
        pltpu.VMEM(output.shape, BF16),
        pltpu.VMEM(late, F32),
    ]
    scratch += [pltpu.VMEM(o.shape, o.dtype) for o in held] + [pltpu.SemaphoreType.DMA((4,))]
    scratch += Exchange(count).scratch() + Exchange(count).scratch()
    if direct:
        scratch.append(pltpu.VMEM((2, 2, 2, width // 8, 3 * width), BF16))
        scratch += VectorSum(table[1:], True).scratch() + VectorSum(late[1:]).scratch()
        scratch += VectorSum(early.shape[1:]).scratch()
        scratch += [s for pair in pairs for _, part in pair for s in part.scratch()]
        scratch += [s for pair in last_pairs for part in pair for s in part.scratch()]
    result = pl.pallas_call(
        functools.partial(tail_kernel, (count, pairs, last_pairs, len(partials))),
        grid=(steps + 1,),
        out_shape=[blocks, blocks, g_qkv] + outs,
        in_specs=[
            SMEM,
            column(0),
            column(1),
            column(2),
            pl.BlockSpec((2, seq, seq), lambda h: (clip(h), 0, 0)),
            column(0),
            whole(patches.shape),
            whole(spread.shape),
            whole(bits.shape),
        ]
        + [whole(v.shape) for v in vectors]
        + [ANY] * (5 + len(views))
        + [whole(v.shape) for v in more],
        out_specs=[ANY, ANY, whole(g_qkv.shape)] + [whole(o.shape) for o in outs],
        scratch_shapes=scratch,
        compiler_params=pltpu.CompilerParams(
            collective_id=2, has_side_effects=True, vmem_limit_bytes=VMEM_LIMIT
        ),
        name="tail",
    )(resolution, qkv, qkv, qkv, probs, upstream, patches, spread, bits, *vectors, output, *held, *views, *more)
    n = len(sums)
    return result[:3], result[3 : 3 + n], result[3 + n : -2], result[-2:]


MESH = pl.DeviceIdType.MESH


def place():
    b, z = lax.axis_index("batch"), lax.axis_index("blk")
    return b, z, lax.rem(b, 2), lax.rem(b // 2, 2), b // 4


def greet(partners):
    barrier = pltpu.get_barrier_semaphore()
    for partner in partners:
        pl.semaphore_signal(barrier, inc=1, device_id=partner, device_id_type=MESH)
    pl.semaphore_wait(barrier, len(partners))


def sum_partners():
    b, z, c, x, y = place()
    near = [(b + 1 - 2 * c, z), (b + 2 - 4 * x, z), (b + 4 - 8 * y, z)]
    return near + [(b, lax.rem(z + s, 4)) for s in (1, 2, 3)]


class Exchange:
    def __init__(self, count):
        self.count = count

    def scratch(self):
        sems = pltpu.SemaphoreType.DMA((self.count - 1,))
        return [sems, sems, pltpu.SemaphoreType.DMA]

    def bind(self, source, target, refs):
        self.source, self.target = source, target
        self.sent, self.come, self.own = refs
        return self

    def partners(self):
        b, z = lax.axis_index("batch"), lax.axis_index("blk")
        return [(b, lax.rem(z + s, self.count)) for s in range(1, self.count)]

    def local(self):
        z = lax.axis_index("blk")
        return pltpu.make_async_copy(self.source.at[z], self.target.at[z], self.own)

    def copy(self, i):
        device = self.partners()[i]
        return pltpu.make_async_remote_copy(
            src_ref=self.source.at[device[1]],
            dst_ref=self.target.at[lax.axis_index("blk")],
            send_sem=self.sent.at[i],
            recv_sem=self.come.at[i],
            device_id=device,
            device_id_type=MESH,
        )

    def start(self):
        for i in range(self.count - 1):
            self.copy(i).start()
        self.local().start()

    def finish(self):
        self.local().wait()
        for i in range(self.count - 1):
            self.copy(i).wait_recv()
        for i in range(self.count - 1):
            self.copy(i).wait_send()


class VectorSum:
    STAGES = 6

    def __init__(self, size, low=False):
        self.size, self.dtype = tuple(size), BF16 if low else F32

    def scratch(self):
        part = pltpu.VMEM(self.size, F32)
        sems = pltpu.SemaphoreType.DMA((7,))
        return [part] * 7 + [pltpu.VMEM((4,) + self.size, self.dtype), sems, sems]

    def bind(self, source, target, refs):
        self.source, self.target = source, target
        self.got0, self.sum1, self.got1, self.sum2, self.got2, self.mine, self.other, self.all = refs[:8]
        self.sent, self.come = refs[8:]
        return self

    def copy(self, i):
        b, z, c, x, y = place()
        near = sum_partners()
        source, target, device = (
            (self.source.at[1 - c], self.got0, near[0]),
            (self.all.at[z], self.all.at[z], near[3]),
            (self.all.at[z], self.all.at[z], near[4]),
            (self.all.at[z], self.all.at[z], near[5]),
            (self.sum1, self.got1, near[1]),
            (self.sum2, self.got2, near[2]),
            (self.mine, self.other, near[0]),
        )[i]
        return pltpu.make_async_remote_copy(
            src_ref=source,
            dst_ref=target,
            send_sem=self.sent.at[i],
            recv_sem=self.come.at[i],
            device_id=device,
            device_id_type=MESH,
        )

    def stage(self, number):
        b, z, c, x, y = place()
        if number == 0:
            self.copy(0).start()
        elif number == 1:
            self.copy(0).wait_recv()
            self.all[z] = (self.source[c] + self.got0[...]).astype(self.dtype)
            for i in (1, 2, 3):
                self.copy(i).start()
        elif number == 2:
            for i in (1, 2, 3):
                self.copy(i).wait_recv()
            value = [self.all[k].astype(F32) for k in range(4)]
            self.sum1[...] = value[0] + value[1] + value[2] + value[3]
            self.copy(4).start()
        elif number == 3:
            self.copy(4).wait_recv()
            self.sum2[...] = self.sum1[...] + self.got1[...]
            self.copy(5).start()
        elif number == 4:
            self.copy(5).wait_recv()
            self.mine[...] = self.sum2[...] + self.got2[...]
            self.copy(6).start()
        else:
            self.copy(6).wait_recv()
            self.target[c] = self.mine[...]
            self.target[1 - c] = self.other[...]
            for i in range(7):
                self.copy(i).wait_send()


def in_steps(rows, width, body):
    step = rows
    while step * width > 49152 and step % 32 == 0:
        step //= 2
    if step == rows:
        body(pl.ds(0, rows))
    else:

        def one(i, carry):
            body(pl.ds(pl.multiple_of(i * step, step), step))
            return carry

        lax.fori_loop(0, rows // step, one, 0)


class WeightSum:
    COPIES = 5

    def __init__(self, rows, at, width, flip, resident=False):
        self.rows, self.at, self.width, self.flip, self.resident = rows, at, width, flip, resident
        self.fold = 2 if (rows // 4) % 16 else 1

    def scratch(self):
        r, w, f = self.rows, self.width, self.fold
        strip = (r // 4 * f, w // f)
        own = [] if self.resident else [pltpu.VMEM((2, 2, r, w), BF16), pltpu.SemaphoreType.DMA]
        return own + [
            pltpu.VMEM((2, 2, r, w), BF16),
            pltpu.VMEM((2, r, w), BF16),
            pltpu.VMEM((r, w), BF16),
            pltpu.VMEM((2, 2) + strip, BF16),
            pltpu.VMEM((2,) + strip, BF16),
            pltpu.VMEM(strip, BF16),
            pltpu.SemaphoreType.DMA((self.COPIES,)),
            pltpu.SemaphoreType.DMA((self.COPIES,)),
        ]

    def bind(self, grad, out, refs, at=None):
        self.grad, self.out = grad, out
        self.source_at = self.at if at is None else at
        refs = list(refs)
        if not self.resident:
            self.kept, self.own = refs[:2]
            refs = refs[2:]
        self.got0, self.got1, self.got2, self.mine, self.got3, self.got4, self.sent, self.come = refs
        return self

    def columns(self):
        return pl.ds(self.source_at, self.width)

    def keep(self, i, j):
        if self.resident:
            return self.grad.at[i, j, place()[2], :, self.columns()]
        return self.kept.at[i, j]

    def local(self):
        c = place()[2]
        return pltpu.make_async_copy(self.grad.at[:, :, c, :, self.columns()], self.kept, self.own)

    def copy(self, i):
        b, z, c, x, y = place()
        to = sum_partners()
        every = slice(None)
        if i == 0:
            source, target, device = self.grad.at[:, :, 1 - c, :, self.columns()], self.got0, to[0]
        elif i == 1:
            source = self.keep(1 - y, every) if self.flip else self.keep(every, 1 - x)
            target, device = self.got1, to[2 if self.flip else 1]
        elif i == 2:
            source = self.keep(y, 1 - x) if self.flip else self.keep(1 - y, x)
            target, device = self.got2, to[1 if self.flip else 2]
        elif i == 3:
            z0 = lax.rem(z, 2)
            source, target, device = self.mine.at[:, 1 - z0], self.got3, (b, z + 1 - 2 * z0)
        else:
            z0, z1 = lax.rem(z, 2), z // 2
            source, target, device = self.mine.at[1 - z1, z0], self.got4, (b, z + 2 - 4 * z1)
        return pltpu.make_async_remote_copy(
            src_ref=source,
            dst_ref=target,
            send_sem=self.sent.at[i],
            recv_sem=self.come.at[i],
            device_id=device,
            device_id_type=MESH,
        )

    def add(self, target, source):
        def body(rows):
            target[rows, :] = (target[rows, :].astype(F32) + source[rows, :].astype(F32)).astype(BF16)

        in_steps(self.rows, self.width, body)

    def stage(self, number):
        b, z, c, x, y = place()
        keep, got0, got1 = self.keep, self.got0, self.got1
        if number == 0:
            if not self.resident:
                self.local().start()
            self.copy(0).start()
        elif number == 1:
            if not self.resident:
                self.local().wait()
            self.copy(0).wait_recv()
            spots = lambda k: [(k, 0), (k, 1)] if self.flip else [(0, k), (1, k)]
            mine = y if self.flip else x
            for i, j in spots(1 - mine):
                self.add(keep(i, j), got0.at[i, j])
            self.copy(1).start()
            for i, j in spots(mine):
                self.add(keep(i, j), got0.at[i, j])
        elif number == 2:
            self.copy(1).wait_recv()
            if self.flip:
                self.add(keep(y, 1 - x), got1.at[1 - x])
                self.copy(2).start()
                self.add(keep(y, x), got1.at[x])
            else:
                self.add(keep(1 - y, x), got1.at[1 - y])
                self.copy(2).start()
                self.add(keep(y, x), got1.at[y])
        elif number == 3:
            self.copy(2).wait_recv()
            r = self.rows // 4
            mine = keep(y, x)
            for k in range(4):
                rows = slice(k * r, k * r + r)
                value = mine[rows, :].astype(F32) + self.got2[rows, :].astype(F32)
                if self.fold == 2:
                    half = self.width // 2
                    value = jnp.concatenate([value[:, :half], value[:, half:]], axis=0)
                self.mine[k // 2, k % 2] = value.astype(BF16)
            self.copy(3).start()
        elif number == 4:
            self.copy(3).wait_recv()
            z0, z1 = lax.rem(z, 2), z // 2
            value = self.mine[1 - z1, z0].astype(F32) + self.got3[1 - z1].astype(F32)
            self.mine[1 - z1, z0] = value.astype(BF16)
            self.copy(4).start()
        elif number == 5:
            self.copy(4).wait_recv()
            z0, z1 = lax.rem(z, 2), z // 2
            value = self.mine[z1, z0].astype(F32) + self.got3[z1].astype(F32) + self.got4[...].astype(F32)
            r, half = self.rows // 4, self.width // 2
            if self.fold == 2:
                self.out[:, self.at : self.at + half] = value[:r]
                self.out[:, self.at + half : self.at + self.width] = value[r:]
            else:
                self.out[:, self.at : self.at + self.width] = value
        else:
            for i in range(self.COPIES):
                self.copy(i).wait_send()


def wave(count, depth):
    ticks = []
    for t in range(count + depth - 1):
        ticks.append([(t - s, s) for s in reversed(range(depth)) if 0 <= t - s < count])
    return ticks


def sum_plan(shapes, counts):
    pairs = []
    for n, ((rows, width), count) in enumerate(zip(shapes, counts)):
        unit = 256 if (rows // 4) % 16 else 128
        units = width // unit
        edges = [unit * (units * k // (2 * count)) for k in range(2 * count + 1)]
        for k in range(count):
            pairs.append([
                (n, WeightSum(rows, edges[2 * k + f], edges[2 * k + f + 1] - edges[2 * k + f], f == 1))
                for f in (0, 1)
            ])
    return pairs


def part_ticks(parts, first, last):
    def tick(steps):
        for pair, stage in steps:
            for part in parts[pair]:
                part.stage(first + stage)

    return [functools.partial(tick, steps) for steps in wave(len(parts), last - first)]


def row_sum(values):
    return jnp.sum(values, axis=0, keepdims=True)


MLP_ROWS = 320
MLP_CHUNK = 512
EARLY = 4


def mlp_kernel(setup, *refs):
    direct, pairs = setup
    refs = list(refs)
    take = lambda n: [refs.pop(0) for _ in range(n)]
    inputs, mixed, raw_up, to_slot, w_proj, *vectors = take(11)
    w1, b1, w2 = take(3)
    out_rows, d_resid, d_mixed, p_proj, p_fc1, p_fc2, vector = take(7)
    g_fc1 = take(1) if direct else []
    hidden, d_branch, upstream, attn, resid, branch, d_hidden, act, d_pre, d_bias = take(10)
    step = pl.program_id(0)
    seq, width = inputs.shape
    chunk = w1.shape[1]
    steps = w_proj.shape[0] * 4 // chunk
    proj_bias, gain1, gain2, shift2, fc2_bias, gain_out = [flat_row(v) for v in vectors]
    blocks = [slice(r, r + MLP_ROWS) for r in range(0, seq, MLP_ROWS)]
    ticks = []
    if direct:
        grads = take(len(pairs))
        parts = []
        for grad, pair in zip(grads, pairs):
            parts.append([])
            for part in pair:
                size = len(part.scratch())
                parts[-1].append(part.bind(grad, g_fc1[0], take(size), at=part.at % chunk))
        ticks = part_ticks(parts, 0, 7)

    @pl.when(step == 0)
    def _():
        if direct:
            greet(sum_partners())
        for rows in blocks:
            up = matmul(to_slot[rows, :], raw_up[...])
            upstream[rows, :] = up
            d_branch[rows, :] = (gain_out * up).astype(BF16)
            value = matmul(mixed[rows, :], w_proj[...]) + proj_bias
            attn[rows, :] = value
            value = inputs[rows, :] + gain1 * value
            resid[rows, :] = value
            hidden[rows, :] = (normalize(value)[0] * gain2 + shift2).astype(BF16)
        branch[...] = jnp.zeros_like(branch)
        d_hidden[...] = jnp.zeros_like(d_hidden)

    bias_sum = jnp.zeros((1, chunk), F32)
    bias_here = flat_row(b1)
    for rows in blocks:
        pre = matmul(hidden[rows, :], w1[...]) + bias_here
        half = 0.5 * (1.0 + lax.erf(pre * 0.7071067811865476))
        slope = half + pre * jnp.exp(-0.5 * pre * pre) * 0.3989422804014327
        low = (pre * half).astype(BF16)
        act[rows, :] = low
        branch[rows, :] += matmul(low, w2[...])
        back = (matmul_t(d_branch[rows, :], w2[...]) * slope).astype(BF16)
        d_pre[rows, :] = back
        bias_sum += row_sum(back.astype(F32))
        d_hidden[rows, :] += matmul_t(back, w1[...])
    d_bias[:, pl.ds(pl.multiple_of(step * chunk, chunk), chunk)] = bias_sum
    p_fc2[...] = t_matmul(act[...], d_branch[...]).astype(BF16)
    partial = t_matmul(hidden[...], d_pre[...]).astype(BF16)
    p_fc1[...] = partial
    if direct:
        for k in range(steps):

            @pl.when(step == k)
            def _(k=k):
                if k < len(pairs):
                    grads[k][...] = partial.reshape(grads[k].shape)
                ticks[k]()

    @pl.when(step == steps - 1)
    def _():
        for tick in ticks[steps : steps + 1]:
            tick()
        d_gamma2 = d_fc2b = d_ln2g = d_ln2b = d_gamma1 = d_projb = jnp.zeros((1, width), F32)
        for rows in blocks:
            mlp = branch[rows, :] + fc2_bias
            up = upstream[rows, :]
            d_gamma2 += row_sum(up * mlp)
            d_fc2b += row_sum(d_branch[rows, :].astype(F32))
            normed, factor = normalize(resid[rows, :])
            hidden[rows, :] = (resid[rows, :] + gain_out * mlp).astype(BF16)
            grad = d_hidden[rows, :]
            d_ln2g += row_sum(grad * normed)
            d_ln2b += row_sum(grad)
            grad = up + norm_back(grad, normed, factor, gain2)
            d_resid[rows, :] = grad
            d_gamma1 += row_sum(grad * attn[rows, :])
            grad = (gain1 * grad).astype(BF16)
            d_branch[rows, :] = grad
            d_projb += row_sum(grad.astype(F32))
            d_mixed[rows, :] = matmul_t(grad, w_proj[...]).astype(BF16)
        for tick in ticks[steps + 1 : steps + 2]:
            tick()
        out_rows[...] = t_matmul(to_slot[...], hidden[...]).astype(BF16)
        p_proj[...] = t_matmul(mixed[...], d_branch[...]).astype(BF16)
        zero = jnp.zeros((2, width), F32)
        vector[0] = jnp.concatenate([d_gamma2, d_fc2b, d_ln2g, d_ln2b, d_gamma1, d_projb, zero], axis=0)
        pieces = [d_bias[:, i * width : (i + 1) * width] for i in range(4)]
        vector[1] = jnp.concatenate(pieces + [zero, zero], axis=0)
        for tick in ticks[steps + 2 :]:
            tick()


def mlp(inputs, mixed, raw_up, to_slot, w_proj, vectors, w1, b1, w2, direct):
    seq, width = inputs.shape
    hidden = w1.shape[1]
    chunk = MLP_CHUNK
    steps = hidden // chunk
    early = EARLY if direct else 0
    half = chunk // 2
    pairs = [
        [WeightSum(width // 8, k * chunk + f * half, half, f == 1, True) for f in (0, 1)] for k in range(early)
    ]
    flat = lambda dtype: jax.ShapeDtypeStruct((seq, width), dtype)
    vmem = lambda dtype: pltpu.VMEM((seq, width), dtype)
    return pl.pallas_call(
        functools.partial(mlp_kernel, (direct, pairs)),
        grid=(steps,),
        out_shape=[
            flat(BF16),
            flat(F32),
            flat(BF16),
            jax.ShapeDtypeStruct((width, width), BF16),
            jax.ShapeDtypeStruct((width, hidden - early * chunk), BF16),
            jax.ShapeDtypeStruct((hidden, width), BF16),
            jax.ShapeDtypeStruct((2, 8, width), F32),
        ]
        + ([jax.ShapeDtypeStruct((width // 32, early * chunk), F32)] if direct else []),
        in_specs=[
            whole(inputs.shape),
            whole(mixed.shape),
            whole(raw_up.shape),
            whole(to_slot.shape),
            whole(w_proj.shape),
        ]
        + [whole(v.shape) for v in vectors]
        + [
            pl.BlockSpec((width, chunk), lambda k: (0, k)),
            pl.BlockSpec((chunk,), lambda k: (k,)),
            pl.BlockSpec((chunk, width), lambda k: (k, 0)),
        ],
        out_specs=[
            whole((seq, width)),
            whole((seq, width)),
            whole((seq, width)),
            whole((width, width)),
            pl.BlockSpec((width, chunk), lambda k: (0, jnp.maximum(k - early, 0))),
            pl.BlockSpec((chunk, width), lambda k: (k, 0)),
            whole((2, 8, width)),
        ]
        + ([whole((width // 32, early * chunk))] if direct else []),
        scratch_shapes=[
            vmem(BF16), vmem(BF16), vmem(F32), vmem(F32), vmem(F32), vmem(F32), vmem(F32),
            pltpu.VMEM((seq, chunk), BF16), pltpu.VMEM((seq, chunk), BF16), pltpu.VMEM((1, hidden), F32),
        ]
        + [pltpu.VMEM((2, 2, 2, width // 8, chunk), BF16) for _ in pairs]
        + [s for pair in pairs for part in pair for s in part.scratch()],
        compiler_params=pltpu.CompilerParams(
            collective_id=1 if direct else None, has_side_effects=direct, vmem_limit_bytes=VMEM_LIMIT
        ),
        name="mlp",
    )(inputs, mixed, raw_up, to_slot, w_proj, *vectors, w1, b1, w2)


def unpack_kernel(plan, early, late, table, *refs):
    refs = list(refs)
    take = lambda n: [refs.pop(0) for _ in range(n)]
    sources = [take(n) for n in plan]
    vectors = take(11)
    out_low, out_high = take(2)
    targets = take(len(plan))
    turned = take(1)[0]
    for group, target in zip(sources, targets):
        at = 0
        for source in group:
            size = source.shape[-1]
            target[..., at : at + size] = source[...]
            at += size
    for i in range(6):
        vectors[i][...] = early[0, i : i + 1, :].reshape(vectors[i].shape)
    for n in range(2):
        for i in range(2):
            rows = [late[n, 6 * i + k : 6 * i + k + 1, :] for k in range(6)]
            out = vectors[6 + 2 * n + i]
            out[...] = jnp.concatenate(rows, axis=1).reshape(out.shape)
    rows = [early[1, i : i + 1, :] for i in range(4)]
    vectors[10][...] = jnp.concatenate(rows, axis=1).reshape(vectors[10].shape)
    heads = out_low.shape[0]
    for n, (out, side, pad) in enumerate(((out_low, SIDE_LOW, G_HIGH - G_LOW), (out_high, SIDE, 0))):
        value = jnp.concatenate([table[n, k * 48 : (k + 1) * 48, :] for k in range(heads // 2)], axis=1)
        turned[n] = jnp.concatenate([value, jnp.zeros((80, 64 * heads), F32)], axis=0).T
        here = turned.at[n]
        for r in range(side):
            rows = pl.ds(SIDE - 1 - r - pad, heads, stride=64)
            out[:, r * side : (r + 1) * side] = here[rows, :][:, pad : pad + side]
        for i in range(3):
            out[:, side * side + i : side * side + i + 1] = here[pl.ds(i, heads, stride=64), :][:, 47:48]


def unpack(early, late, table, groups, width, hidden, heads):
    outs = [jax.ShapeDtypeStruct((width,), F32)] * 10 + [jax.ShapeDtypeStruct((hidden,), F32)]
    outs += [jax.ShapeDtypeStruct((heads, side * side + 3), F32) for side in (SIDE_LOW, SIDE)]
    outs += [
        jax.ShapeDtypeStruct(g[0].shape[:-1] + (sum(p.shape[-1] for p in g),), g[0].dtype) for g in groups
    ]
    pieces = [p for g in groups for p in g]
    vmem = pl.BlockSpec(memory_space=pltpu.VMEM)
    result = pl.pallas_call(
        functools.partial(unpack_kernel, [len(g) for g in groups]),
        out_shape=outs,
        in_specs=[vmem] * (3 + len(pieces)),
        out_specs=[vmem] * (13 + len(groups)),
        scratch_shapes=[pltpu.VMEM((2, 64 * heads, 128), F32)],
        compiler_params=pltpu.CompilerParams(vmem_limit_bytes=VMEM_LIMIT),
        name="unpack",
    )(early, late, table, *pieces)
    return result[:11], result[11].T, result[12].T, result[13:]


def swap(value, axis, bit, count):
    return lax.ppermute(value, axis, [(i, i ^ bit) for i in range(count)])


def bits_of(count):
    return [1 << i for i in range(count.bit_length() - 1)]


def scatter_sum(grad, batch, blk):
    places = [("batch", bit, batch) for bit in bits_of(batch)][::-1]
    places += [("blk", bit, blk) for bit in bits_of(blk)][::-1]
    value = grad.reshape((2,) * len(places) + (grad.shape[0] >> len(places), grad.shape[1]))
    left = list(places)
    for spot in places:
        axis, bit, count = spot
        at = left.index(spot)
        left.remove(spot)
        mine = jnp.bitwise_and(lax.axis_index(axis) // bit, 1)
        sent = lax.dynamic_index_in_dim(value, 1 - mine, at, keepdims=False)
        kept = lax.dynamic_index_in_dim(value, mine, at, keepdims=False)
        got = swap(sent, axis, bit, count)
        value = kept.astype(F32) + got.astype(F32)
        if left:
            value = value.astype(BF16)
    return value


def total_sum(value, batch, blk):
    for bit in bits_of(batch):
        value = value + swap(value, "batch", bit, batch)
    for bit in bits_of(blk):
        value = value + swap(value, "blk", bit, blk)
    return value


def shards(
    batch,
    blk,
    tokens,
    resolution,
    positions,
    ln1_gain,
    ln1_bias,
    w_qkv,
    q_bias,
    v_bias,
    w_proj,
    proj_bias,
    gamma1,
    ln2_gain,
    ln2_bias,
    w_fc1,
    fc1_bias,
    w_fc2,
    fc2_bias,
    gamma2,
    rel_low,
    rel_high,
    grad_out,
):
    images, rows, width = tokens.shape
    seq = positions.shape[1]
    heads = rel_low.shape[1]
    assert images == blk and rows * blk == seq and width == heads * 64
    direct = (batch, blk) == (8, 4)
    spread_np, bits_np = lane_tables()
    spread = jnp.asarray(spread_np, BF16)
    bits = jnp.asarray(bits_np)
    patches = jnp.asarray(slot_tables(seq)[2].T, F32)
    to_slot, inputs, qkv, probs, mixed, raw_up = front(
        resolution,
        positions,
        rel_low,
        rel_high,
        spread,
        bits,
        patches,
        (ln1_gain, ln1_bias, q_bias, v_bias),
        w_qkv,
        tokens,
        grad_out,
        blk,
    )
    out_rows, d_resid, d_mixed, p_proj, p_fc1, p_fc2, early, *g_fc1 = mlp(
        inputs,
        mixed,
        raw_up.reshape(seq, width),
        to_slot,
        w_proj,
        (proj_bias, gamma1, ln2_gain, ln2_bias, fc2_bias, gamma2),
        w_fc1,
        fc1_bias,
        w_fc2,
        direct,
    )
    partials = [p_fc1, p_fc2, p_proj]
    (output, grad_tokens, g_qkv), sums, early_sum, (late, d_table) = tail(
        resolution,
        qkv,
        probs,
        d_mixed,
        patches,
        spread,
        bits,
        (ln1_gain, ln1_bias),
        out_rows.reshape(blk, rows, width),
        inputs,
        d_resid,
        to_slot,
        w_qkv,
        partials if direct else [],
        [1, 3, 1],
        early,
        blk,
    )
    if direct:
        early = early_sum[0]
        groups = [[output], [grad_tokens], [g_fc1[0], sums[0]], [sums[1]], [sums[2]], [g_qkv]]
    else:
        g_fc1, g_fc2, g_proj, g_qkv = [scatter_sum(g, batch, blk) for g in partials + [g_qkv]]
        early, late, d_table = [total_sum(v, batch, blk) for v in (early, late, d_table)]
        groups = [[output], [grad_tokens]]
    vectors, s_low, s_high, rest = unpack(early, late, d_table, groups, width, w_fc1.shape[1], heads)
    s_gamma2, s_fc2b, s_ln2g, s_ln2b, s_gamma1, s_projb, s_ln1g, s_ln1b, s_qb, s_vb, s_fc1b = vectors
    output, grad_tokens = rest[:2]
    if direct:
        g_fc1, g_fc2, g_proj, g_qkv = rest[2:]
    return (
        output,
        grad_tokens,
        s_ln1g,
        s_ln1b,
        g_qkv,
        s_qb,
        s_vb,
        g_proj,
        s_projb,
        s_gamma1,
        s_ln2g,
        s_ln2b,
        g_fc1,
        s_fc1b,
        g_fc2,
        s_fc2b,
        s_gamma2,
        s_low,
        s_high,
    )


def solution(mesh):
    rows = P("batch", "blk", None)
    shared = P(("batch", "blk"), None)
    in_specs = (rows, P("batch"), P("batch", None)) + (P(),) * 17 + (rows,)
    out_specs = (
        (rows, rows, P(), P(), shared, P(), P(), shared)
        + (P(),) * 4
        + (shared, P(), shared)
        + (P(),) * 4
    )
    return jax.shard_map(
        functools.partial(shards, mesh.shape["batch"], mesh.shape["blk"]),
        mesh=mesh,
        in_specs=in_specs,
        out_specs=out_specs,
        check_vma=False,
    )
```

```python
import functools

import jax
import jax.numpy as jnp
import numpy as np
from jax import lax
from jax.experimental import pallas as pl
from jax.experimental.pallas import tpu as pltpu
from jax.sharding import PartitionSpec as P

G_LOW = 14
G_HIGH = 24
SIDE_LOW = 2 * G_LOW - 1
SIDE = 2 * G_HIGH - 1
CELLS = G_HIGH * G_HIGH
SPAN = 1152
F32 = jnp.float32
BF16 = jnp.bfloat16


def normalize(values):
    center = values - jnp.mean(values, axis=-1, keepdims=True)
    factor = lax.rsqrt(jnp.mean(center * center, axis=-1, keepdims=True) + 1e-06)
    return center * factor, factor


def norm_back(grad, normed, factor, gain):
    scaled = grad * gain
    return factor * (
        scaled
        - jnp.mean(scaled, axis=-1, keepdims=True)
        - normed * jnp.mean(scaled * normed, axis=-1, keepdims=True)
    )


def matmul(left, right):
    return jnp.dot(left, right, preferred_element_type=F32)


def matmul_t(left, right):
    return lax.dot_general(left, right, (((1,), (1,)), ((), ())), preferred_element_type=F32)


def t_matmul(left, right):
    return lax.dot_general(left, right, (((0,), (0,)), ((), ())), preferred_element_type=F32)


def slot_tables(seq):
    tokens = np.arange(seq)
    tables = []
    for grid in (G_LOW, G_HIGH):
        cells = np.arange(CELLS)
        used = (cells // G_HIGH < grid) & (cells % G_HIGH < grid)
        free = np.concatenate([cells[~used], np.arange(CELLS + 1, seq)])
        slot = np.full(seq, CELLS)
        slot[1 + grid * grid :] = free
        patch = np.concatenate([used, np.zeros(seq - CELLS, bool)])
        key = patch.copy()
        key[CELLS] = True
        tables.append((slot, (tokens >= 1) & (tokens < 1 + grid * grid), patch, key))
    return [np.stack(parts) for parts in zip(*tables)]


def lane_tables():
    lanes = np.arange(SPAN)
    spread = (lanes[None, :] // G_HIGH == np.arange(128)[:, None]) & (np.arange(128)[:, None] < SIDE)
    shift = G_HIGH - 1 - lanes % G_HIGH
    bits = (shift[None, :] >> np.arange(8)[:, None]) & 1
    return np.stack([spread, np.roll(spread, 64, axis=0)]), bits.astype(np.int32)


def slide(values, bits, down):
    for k in range(5):
        amount = 1 << k if down else 48 - (1 << k)
        values = jnp.where(bits[k : k + 1, :] > 0, pltpu.roll(values, amount, 0), values)
    return values


VMEM_LIMIT = 62 << 20


def whole(shape):
    return pl.BlockSpec(shape, lambda h: (0,) * len(shape))


ANY = pl.BlockSpec(memory_space=pl.ANY)
SMEM = pl.BlockSpec(memory_space=pltpu.SMEM)


def flat_row(ref):
    return ref[...].astype(F32).reshape(1, ref.shape[0])


def front_kernel(
    count, resolution, cells, low_t, high_t, spread, bits, slot_of, is_patch, patches, masks,
    ln1_gain, ln1_bias, q_bias, v_bias, w_qkv, tokens, grad_out,
    to_slot, inputs, qkv, probs, mixed, raw_up, bias, raw, inner_low, inner_high, wide, full, *refs,
):
    step = pl.program_id(0)
    me = lax.axis_index("blk")
    high = resolution[me] == 1
    seq = full.shape[0]
    heads = low_t.shape[0]
    width = inputs.shape[1]
    size = len(Exchange(count).scratch())
    move = Exchange(count).bind(tokens, raw, refs[:size])
    move_up = Exchange(count).bind(grad_out, raw_up, refs[size:])

    @pl.when(step == 0)
    def _():
        greet(move.partners())
        move.start()
        here = cells[pl.ds(me, 1), :]
        grid = jnp.where(high, G_HIGH, G_LOW)
        row = jnp.zeros_like(here)
        for k in range(1, G_HIGH):
            row += (here >= k * grid).astype(jnp.int32)
        at = row * G_HIGH + here - row * grid
        patch = jnp.where(high, is_patch[1:2, :], is_patch[0:1, :])
        other = jnp.where(high, slot_of[1:2, :], slot_of[0:1, :])
        slot = jnp.where(patch > 0, at, other)
        spots = lax.broadcasted_iota(jnp.int32, (seq, seq), 0)
        to_slot[...] = jnp.where(spots == slot, 1.0, 0.0).astype(BF16)
        inner_low[...] = jnp.zeros_like(inner_low)
        inner_high[...] = jnp.zeros_like(inner_high)
        low_f, high_f = low_t[...].astype(F32), high_t[...].astype(F32)
        pad = G_HIGH - G_LOW
        for j in range(SIDE):
            r = SIDE - 1 - j
            inner_high[j * 16 : j * 16 + heads, 0:SIDE] = high_f[:, r * SIDE : (r + 1) * SIDE]
            r -= pad
            if 0 <= r < SIDE_LOW:
                inner_low[j * 16 : j * 16 + heads, pad : pad + SIDE_LOW] = low_f[
                    :, r * SIDE_LOW : (r + 1) * SIDE_LOW
                ]

    @pl.when(step < heads)
    def _():
        rows = pl.ds(step, 48, stride=16)
        table = jnp.where(high, inner_high[rows, :], inner_low[rows, :]).astype(BF16)
        wide[...] = slide(t_matmul(table, spread[0, 0:48, :])[0:48], bits, False)[0:G_HIGH]
        for r in range(G_HIGH):
            at = (G_HIGH - 1 - r) * G_HIGH
            full[r * G_HIGH : (r + 1) * G_HIGH, 0:CELLS] = wide[:, at : at + CELLS]
        column = lax.broadcasted_iota(jnp.int32, (1, seq), 1)
        ends = [t[:, t.shape[1] - 3 : t.shape[1]].astype(F32) for t in (low_t, high_t)]
        special = jnp.where(high, ends[1], ends[0])
        here = lax.broadcasted_iota(jnp.int32, special.shape, 0) == step
        special = jnp.sum(jnp.where(here, special, 0.0), axis=0, keepdims=True)
        inner_row = jnp.where(column < CELLS, special[:, 0:1], special[:, 2:3])
        values = jnp.where(column < CELLS, full[...], special[:, 1:2])
        patch = jnp.where(high, patches[:, 1:2], patches[:, 0:1])
        mask = jnp.where(high, masks[1:2, :], masks[0:1, :])
        values = jnp.where(patch > 0.0, values, inner_row)
        bias[step] = (values + mask).astype(BF16)

    @pl.when(step == heads)
    def _():
        move.finish()
        move_up.start()
        value = matmul(to_slot[...], raw[...].reshape(seq, width))
        inputs[...] = value
        hidden = (normalize(value)[0] * flat_row(ln1_gain) + flat_row(ln1_bias)).astype(BF16)
        shifts = [flat_row(q_bias), 0.0, flat_row(v_bias)]
        for n in range(3):
            part = slice(n * width, (n + 1) * width)
            qkv[:, part] = (matmul(hidden, w_qkv[:, part]) + shifts[n]).astype(BF16)

    @pl.when(step >= heads)
    def _():
        pair = step - heads
        query, keys, values = [
            qkv[:, pl.ds(pl.multiple_of(n * width + pair * 128, 128), 128)] for n in range(3)
        ]
        for h in range(2):
            at = slice(h * 64, h * 64 + 64)
            scores = matmul_t(query[:, at] * 0.125, keys[:, at]) + bias[2 * pair + h].astype(F32)
            expo = jnp.exp(scores - jnp.max(scores, axis=-1, keepdims=True))
            low = (expo * (1.0 / jnp.sum(expo, axis=-1, keepdims=True))).astype(BF16)
            probs[h] = low
            mixed[:, at] = matmul(low, values[:, at]).astype(BF16)

    @pl.when(step == pl.num_programs(0) - 1)
    def _():
        move_up.finish()


def front(resolution, cells, rel_low, rel_high, spread, bits, patches, vectors, w_qkv, tokens, grad_out, count):
    heads = rel_low.shape[1]
    seq = cells.shape[1]
    width = w_qkv.shape[0]
    slot_np, token_np, _, key_np = slot_tables(seq)
    slot_of = jnp.asarray(slot_np, jnp.int32)
    is_patch = jnp.asarray(token_np, jnp.int32)
    masks = jnp.asarray(np.where(key_np, 0.0, -1e30), F32)
    operands = (rel_low.T, rel_high.T, spread, bits, slot_of, is_patch, patches, masks) + vectors + (w_qkv,)
    late = lambda i: jnp.maximum(i - heads, 0)
    return pl.pallas_call(
        functools.partial(front_kernel, count),
        grid=(heads + heads // 2,),
        out_shape=(
            jax.ShapeDtypeStruct((seq, seq), BF16),
            jax.ShapeDtypeStruct((seq, width), F32),
            jax.ShapeDtypeStruct((seq, 3 * width), BF16),
            jax.ShapeDtypeStruct((heads, seq, seq), BF16),
            jax.ShapeDtypeStruct((seq, width), BF16),
            jax.ShapeDtypeStruct(grad_out.shape, BF16),
        ),
        in_specs=[SMEM, whole(cells.shape)] + [whole(o.shape) for o in operands] + [ANY, ANY],
        out_specs=(
            whole((seq, seq)),
            whole((seq, width)),
            whole((seq, 3 * width)),
            pl.BlockSpec((2, seq, seq), lambda i: (late(i), 0, 0)),
            pl.BlockSpec((seq, 128), lambda i: (0, late(i))),
            ANY,
        ),
        scratch_shapes=[
            pltpu.VMEM((heads, seq, seq), BF16),
            pltpu.VMEM(tokens.shape, BF16),
            pltpu.VMEM((48 * 16, 128), F32),
            pltpu.VMEM((48 * 16, 128), F32),
            pltpu.VMEM((G_HIGH, SPAN), F32),
            pltpu.VMEM((seq, seq), F32),
        ]
        + Exchange(count).scratch()
        + Exchange(count).scratch(),
        compiler_params=pltpu.CompilerParams(
            collective_id=0, has_side_effects=True, vmem_limit_bytes=VMEM_LIMIT
        ),
        name="front",
    )(resolution, cells, *operands, tokens, grad_out)


def head_grads(query, keys, values, weights, up, patch, spread, bits, score, wide, lanes):
    ups = matmul_t(up, values)
    weight = weights.astype(F32)
    product = weight * ups
    ds = product - weight * jnp.sum(product, axis=-1, keepdims=True)
    ds_low = ds.astype(BF16)
    d_query = (matmul(ds_low, keys) * 0.125).astype(BF16)
    d_key = t_matmul(ds_low, query * 0.125).astype(BF16)
    d_value = t_matmul(weights, up).astype(BF16)
    total = jnp.sum(ds, axis=0, keepdims=True)
    ds = ds * patch
    score[...] = ds
    inside = jnp.sum(ds, axis=0, keepdims=True)
    wide[...] = jnp.zeros_like(wide)
    for r in range(G_HIGH):
        off = (G_HIGH - 1 - r) * G_HIGH
        wide[:, off : off + CELLS] += score[r * G_HIGH : (r + 1) * G_HIGH, 0:CELLS]
    flat = slide(jnp.concatenate([wide[...], jnp.zeros_like(wide)], axis=0), bits, True)
    first = flat.astype(BF16)
    rest = flat - first.astype(F32)
    second = rest.astype(BF16)
    third = (rest - second.astype(F32)).astype(BF16)
    table = matmul_t(first, spread) + matmul_t(second, spread) + matmul_t(third, spread)
    column = lax.broadcasted_iota(jnp.int32, total.shape, 1)
    lane = lax.broadcasted_iota(jnp.int32, (1, 128), 1)
    outside = total - inside
    edge = jnp.zeros((1, 128), F32)
    for i, value in enumerate((
        jnp.where(column < CELLS, outside, 0.0),
        jnp.where(column == CELLS, inside, 0.0),
        jnp.where(column == CELLS, outside, 0.0),
    )):
        edge += jnp.where(lane == lanes + i, jnp.sum(value, axis=1, keepdims=True), 0.0)
    return d_query, d_key, d_value, table, edge


def by_lanes(row):
    return jnp.concatenate([row[:, i : i + 128] for i in range(0, row.shape[1], 128)], axis=0)


FC1_SPANS = (2048, 1024)
FC1_SLOTS = ((0, 2, 8, 12, 14, 20, 26), (0, 3, 9, 12, 15, 20, 26))
PROJ_SLOTS = ((8, 10, 13, 16, 21, 22, 26),)
QKV_SLOTS = (
    (8, 10, 13, 16, 21, 22, 26),
    (9, 11, 16, 17, 21, 22, 26),
    (12, 13, 17, 18, 21, 22, 26),
)
FC2_SLOTS = ((0, 4, 7, 18, 26), (0, 5, 8, 18, 26))
EARLY_SLOTS = (0, 1, 3, 5, 7, 9)
TABLE_SLOTS = ((8, 9, 11, 16, 17, 18), (12, 13, 16, 17, 18, 19))
LATE_SLOTS = (15, 15, 16, 17, 18, 19)
TABLE_PAIRS = 4


def tail_kernel(setup, *refs):
    count, groups, grads = setup
    direct = grads > 0
    fc1_pairs, proj_pairs, fc2_second, qkv_groups = groups
    refs = list(refs)
    take = lambda n: [refs.pop(0) for _ in range(n)]
    resolution, query, keys, values, probs, upstream, patches, spread, bits, ln1_gain, ln1_bias = take(11)
    sources = take(4)
    partials = take(grads)
    early, *p_fc2 = take(1 + len(fc2_second)) if direct else [None]
    moved, g_qkv = take(2)
    g_fc1, g_proj, g_fc2, early_sum = take(4) if direct else [None] * 4
    late_sum, table_sum = take(2)
    score, wide, d_qkv, hidden, table_a, table_b, tokens, late = take(8)
    loaded = take(4)
    load_sems = take(1)[0]
    move = Exchange(count)
    move.bind(tokens, moved, take(len(move.scratch())))
    step = pl.program_id(0)
    steps = pl.num_programs(0) - 1
    seq, width = loaded[0].shape
    first_rows = table_a.shape[1]
    slots = [[] for _ in range(28)]

    def run(slot):
        for tick in slots[slot]:
            tick()

    if direct:
        grad = take(1)[0]
        scratch_of = lambda part: take(len(part.scratch()))

        def plan(bound, own, numbers=range(7)):
            for number, slot in zip(numbers, own):
                slots[slot].append(functools.partial(run_stage, bound, number))

        small = VectorSum(early.shape[1:])
        plan([small.bind(early, early_sum, scratch_of(small))], EARLY_SLOTS)
        for ref, at, own in zip((table_a, table_b), (0, first_rows), TABLE_SLOTS):
            part = VectorSum(ref.shape[1:], True)
            plan([part.bind(ref, table_sum, scratch_of(part), at)], own)
        part = VectorSum(late.shape[1:])
        plan([part.bind(late, late_sum, scratch_of(part))], LATE_SLOTS)
        for pair, own, source in zip(fc2_second, FC2_SLOTS, p_fc2):
            bound = [part.bind(source.at[f], g_fc2, scratch_of(part)) for f, part in enumerate(pair)]
            plan(bound, own, (2, 3, 4, 5, 6))
        for pairs, own, n, out in ((fc1_pairs, FC1_SLOTS, 0, g_fc1), (proj_pairs, PROJ_SLOTS, 1, g_proj)):
            for pair, spots in zip(pairs, own):
                plan([part.bind(partials[n], out, scratch_of(part)) for part in pair], spots)
        for group, spots in zip(qkv_groups, QKV_SLOTS):
            plan([part.bind(grad, g_qkv, scratch_of(part)) for part in group], spots)

    loads = [
        pltpu.make_async_copy(source, target, load_sems.at[i])
        for i, (source, target) in enumerate(zip(sources, loaded))
    ]
    inputs, d_resid, to_slot, w_qkv = loaded

    @pl.when(step == 0)
    def _():
        greet(sum_partners() if direct else move.partners())
        for load in loads:
            load.start()

    high = resolution[lax.axis_index("blk")] == 1

    @pl.when(step < steps)
    def _():
        patch = jnp.where(high, patches[:, 1:2], patches[:, 0:1])
        total = jnp.zeros((48, 128), F32)
        edge = jnp.zeros((1, 128), F32)
        parts3 = [[], [], []]
        for h in range(2):
            for k in range(6):
                if slots[2 * k + h]:
                    pl.when(step == k)(functools.partial(run, 2 * k + h))

            at = slice(h * 64, h * 64 + 64)
            *heads3, part, ends = head_grads(
                query[:, at], keys[:, at], values[:, at], probs[h], upstream[:, at],
                patch, spread[h], bits, score, wide, h * 64,
            )
            total += part
            edge += ends
            for n in range(3):
                parts3[n].append(heads3[n])
        for n in range(3):
            at = pl.ds(pl.multiple_of(n * width + step * 128, 128), 128)
            d_qkv[:, at] = jnp.concatenate(parts3[n], axis=1)
        row = lax.broadcasted_iota(jnp.int32, (48, 128), 0)
        total = jnp.where(row == 47, edge, total)
        for k in range(6):

            @pl.when(step == k)
            def _(k=k):
                ref, at = (table_a, k) if k < TABLE_PAIRS else (table_b, k - TABLE_PAIRS)
                ref[0, at * 48 : at * 48 + 48, :] = jnp.where(high, 0.0, total)
                ref[1, at * 48 : at * 48 + 48, :] = jnp.where(high, total, 0.0)

    @pl.when(step == 1)
    def _():
        loads[0].wait()
        hidden[...] = (normalize(inputs[...])[0] * flat_row(ln1_gain) + flat_row(ln1_bias)).astype(BF16)

    for k in range(3):

        @pl.when(step == 2 * k + 1)
        def _(k=k):
            for n in range(3):
                at = slice(n * width + k * 256, n * width + k * 256 + 256)
                partial = t_matmul(hidden[...], d_qkv[:, at]).astype(BF16)
                if direct:
                    grad[:, :, :, :, at] = partial.reshape(2, 2, 2, width // 8, 256)
                else:
                    g_qkv[:, at] = partial

    @pl.when(step == steps)
    def _():
        run(12)
        for load in loads[1:]:
            load.wait()
        gain = flat_row(ln1_gain)
        d_gain = d_shift = jnp.zeros((1, width), F32)
        lows = []
        for n, r in enumerate(range(0, seq, seq // 2)):
            rows = slice(r, r + seq // 2)
            back = matmul_t(d_qkv[rows, :], w_qkv[...])
            value, scale = normalize(inputs[rows, :])
            d_gain += row_sum(back * value)
            d_shift += row_sum(back)
            lows.append((d_resid[rows, :] + norm_back(back, value, scale, gain)).astype(BF16))
            run(13 + n)
        ordered = t_matmul(to_slot[...], jnp.concatenate(lows, axis=0)).astype(BF16)
        tokens[...] = ordered.reshape(tokens.shape)
        sums4 = [d_gain, d_shift] + [
            row_sum(d_qkv[:, n * width : (n + 1) * width].astype(F32)) for n in (0, 2)
        ]
        for n in range(2):
            both = [by_lanes(v) for v in sums4[2 * n : 2 * n + 2]] + [jnp.zeros((4, 128), F32)]
            late[n] = jnp.concatenate(both, axis=0)
        run(15)
        move.start()
        if direct:
            for slot in range(16, 28):
                run(slot)
        else:
            late_sum[...] = late[...]
            table_sum[:, 0:first_rows] = table_a[...]
            table_sum[:, first_rows:] = table_b[...]
        move.finish()


def tail(resolution, qkv, probs, upstream, patches, spread, bits, vectors, inputs, d_resid, to_slot, w_qkv, partials, p_fc2, early, count, direct):
    seq, width = inputs.shape
    steps = width // 128
    clip = lambda h: jnp.minimum(h, steps - 1)
    column = lambda part: pl.BlockSpec((seq, 128), lambda h: (0, part * steps + clip(h)))
    blocks = jax.ShapeDtypeStruct((count, seq // count, width), BF16)
    late, table = (2, 16, 128), (2, 48 * steps, 128)
    tables = [(2, 48 * TABLE_PAIRS, 128), (2, 48 * (steps - TABLE_PAIRS), 128)]
    groups, views, more, outs = ((), (), (), ()), [], [], []
    g_qkv = jax.ShapeDtypeStruct((width, 3 * width), BF16)
    if direct:
        views = [g.reshape(2, 2, 2, g.shape[0] // 8, g.shape[1]) for g in partials]
        more = [early, *p_fc2]
        hidden = partials[0].shape[1]
        share = lambda columns, rows=width: jax.ShapeDtypeStruct((rows // 32, columns), F32)
        outs = [share(hidden), share(width), share(width, hidden), jax.ShapeDtypeStruct(early.shape, F32)]
        g_qkv = share(3 * width)
        fc1_pairs, at = [], 0
        for span in FC1_SPANS:
            part = span // 2
            fc1_pairs.append([WeightSum(width // 8, at + f * part, part, f == 1) for f in (0, 1)])
            at += span
        proj_pairs = [[WeightSum(width // 8, 0, 256, False), WeightSum(width // 8, 256, 512, True)]]
        fc2_second = fc2_pairs(hidden, "second")
        qkv_groups = [
            [WeightSum(width // 8, n * width + k * 256, 256, (n + k) % 2 == 1, True) for n in range(3)]
            for k in range(3)
        ]
        groups = (fc1_pairs, proj_pairs, fc2_second, qkv_groups)
    outs = list(outs) + [jax.ShapeDtypeStruct(late, F32), jax.ShapeDtypeStruct(table, F32)]
    held = (inputs, d_resid, to_slot, w_qkv)
    scratch = [
        pltpu.VMEM((seq, seq), F32),
        pltpu.VMEM((G_HIGH, SPAN), F32),
        pltpu.VMEM((seq, 3 * width), BF16),
        pltpu.VMEM((seq, width), BF16),
        pltpu.VMEM(tables[0], F32),
        pltpu.VMEM(tables[1], F32),
        pltpu.VMEM(blocks.shape, BF16),
        pltpu.VMEM(late, F32),
    ]
    scratch += [pltpu.VMEM(o.shape, o.dtype) for o in held] + [pltpu.SemaphoreType.DMA((4,))]
    scratch += Exchange(count).scratch()
    if direct:
        scratch.append(pltpu.VMEM((2, 2, 2, width // 8, 3 * width), BF16))
        parts = [VectorSum(early.shape[1:])] + [VectorSum(t[1:], True) for t in tables] + [VectorSum(late[1:])]
        parts += [part for pair in fc2_second + fc1_pairs + proj_pairs + qkv_groups for part in pair]
        scratch += [s for part in parts for s in part.scratch()]
    return pl.pallas_call(
        functools.partial(tail_kernel, (count, groups, len(views))),
        grid=(steps + 1,),
        out_shape=[blocks, g_qkv] + outs,
        in_specs=[
            SMEM,
            column(0),
            column(1),
            column(2),
            pl.BlockSpec((2, seq, seq), lambda h: (clip(h), 0, 0)),
            column(0),
            whole(patches.shape),
            whole(spread.shape),
            whole(bits.shape),
        ]
        + [whole(v.shape) for v in vectors]
        + [ANY] * (4 + len(views))
        + [whole(v.shape) for v in more],
        out_specs=[ANY, whole(g_qkv.shape)] + [whole(o.shape) for o in outs],
        scratch_shapes=scratch,
        compiler_params=pltpu.CompilerParams(
            collective_id=2, has_side_effects=True, vmem_limit_bytes=VMEM_LIMIT
        ),
        name="tail",
    )(resolution, qkv, qkv, qkv, probs, upstream, patches, spread, bits, *vectors, *held, *views, *more)


MESH = pl.DeviceIdType.MESH


def place():
    b, z = lax.axis_index("batch"), lax.axis_index("blk")
    return b, z, lax.rem(b, 2), lax.rem(b // 2, 2), b // 4


def greet(partners):
    barrier = pltpu.get_barrier_semaphore()
    for partner in partners:
        pl.semaphore_signal(barrier, inc=1, device_id=partner, device_id_type=MESH)
    pl.semaphore_wait(barrier, len(partners))


def sum_partners():
    b, z, c, x, y = place()
    near = [(b + 1 - 2 * c, z), (b + 2 - 4 * x, z), (b + 4 - 8 * y, z)]
    return near + [(b, lax.rem(z + s, 4)) for s in (1, 2, 3)]


class Exchange:
    def __init__(self, count):
        self.count = count

    def scratch(self):
        sems = pltpu.SemaphoreType.DMA((self.count - 1,))
        return [sems, sems, pltpu.SemaphoreType.DMA]

    def bind(self, source, target, refs):
        self.source, self.target = source, target
        self.sent, self.come, self.own = refs
        return self

    def partners(self):
        b, z = lax.axis_index("batch"), lax.axis_index("blk")
        return [(b, lax.rem(z + s, self.count)) for s in range(1, self.count)]

    def local(self):
        z = lax.axis_index("blk")
        return pltpu.make_async_copy(self.source.at[z], self.target.at[z], self.own)

    def copy(self, i):
        device = self.partners()[i]
        return pltpu.make_async_remote_copy(
            src_ref=self.source.at[device[1]],
            dst_ref=self.target.at[lax.axis_index("blk")],
            send_sem=self.sent.at[i],
            recv_sem=self.come.at[i],
            device_id=device,
            device_id_type=MESH,
        )

    def start(self):
        for i in range(self.count - 1):
            self.copy(i).start()
        self.local().start()

    def finish(self):
        self.local().wait()
        for i in range(self.count - 1):
            self.copy(i).wait_recv()
        for i in range(self.count - 1):
            self.copy(i).wait_send()


class VectorSum:
    STAGES = 6

    def __init__(self, size, low=False):
        self.size, self.dtype = tuple(size), BF16 if low else F32

    def scratch(self):
        part = pltpu.VMEM(self.size, F32)
        sems = pltpu.SemaphoreType.DMA((7,))
        return [part] * 7 + [pltpu.VMEM((4,) + self.size, self.dtype), sems, sems]

    def bind(self, source, target, refs, at=0):
        self.source, self.target, self.at = source, target, at
        self.got0, self.sum1, self.got1, self.sum2, self.got2, self.mine, self.other, self.all = refs[:8]
        self.sent, self.come = refs[8:]
        return self

    def copy(self, i):
        b, z, c, x, y = place()
        near = sum_partners()
        source, target, device = (
            (self.source.at[1 - c], self.got0, near[0]),
            (self.all.at[z], self.all.at[z], near[3]),
            (self.all.at[z], self.all.at[z], near[4]),
            (self.all.at[z], self.all.at[z], near[5]),
            (self.sum1, self.got1, near[1]),
            (self.sum2, self.got2, near[2]),
            (self.mine, self.other, near[0]),
        )[i]
        return pltpu.make_async_remote_copy(
            src_ref=source,
            dst_ref=target,
            send_sem=self.sent.at[i],
            recv_sem=self.come.at[i],
            device_id=device,
            device_id_type=MESH,
        )

    def stage(self, number):
        b, z, c, x, y = place()
        if number == 0:
            self.copy(0).start()
        elif number == 1:
            self.copy(0).wait_recv()
            self.all[z] = (self.source[c] + self.got0[...]).astype(self.dtype)
            for i in (1, 2, 3):
                self.copy(i).start()
        elif number == 2:
            for i in (1, 2, 3):
                self.copy(i).wait_recv()
            value = [self.all[k].astype(F32) for k in range(4)]
            self.sum1[...] = value[0] + value[1] + value[2] + value[3]
            self.copy(4).start()
        elif number == 3:
            self.copy(4).wait_recv()
            self.sum2[...] = self.sum1[...] + self.got1[...]
            self.copy(5).start()
        elif number == 4:
            self.copy(5).wait_recv()
            self.mine[...] = self.sum2[...] + self.got2[...]
            self.copy(6).start()
        else:
            self.copy(6).wait_recv()
            rows = slice(self.at, self.at + self.size[0])
            self.target[c, rows] = self.mine[...]
            self.target[1 - c, rows] = self.other[...]
            for i in range(7):
                self.copy(i).wait_send()


def in_steps(rows, width, body):
    step = rows
    while step * width > 49152 and step % 32 == 0:
        step //= 2
    if step == rows:
        body(pl.ds(0, rows))
    else:

        def one(i, carry):
            body(pl.ds(pl.multiple_of(i * step, step), step))
            return carry

        lax.fori_loop(0, rows // step, one, 0)


class WeightSum:
    COPIES = 5

    def __init__(self, rows, at, width, flip, resident=False, half=""):
        self.rows, self.at, self.width, self.flip, self.resident = rows, at, width, flip, resident
        self.half = half
        self.fold = 2 if (rows // 4) % 16 else 1

    def strip(self):
        return (self.rows // 4 * self.fold, self.width // self.fold)

    def scratch(self):
        r, w = self.rows, self.width
        strip = self.strip()
        refs = [pltpu.SemaphoreType.DMA((self.COPIES,))] * 2
        if self.half != "first":
            refs += [pltpu.VMEM((2, 2) + strip, BF16), pltpu.VMEM((2,) + strip, BF16), pltpu.VMEM(strip, BF16)]
            refs += [pltpu.VMEM((r, w), BF16)]
        if self.half != "second":
            refs += [pltpu.VMEM((2, 2, r, w), BF16), pltpu.VMEM((2, r, w), BF16)]
            if not self.resident:
                refs += [pltpu.VMEM((2, 2, r, w), BF16), pltpu.SemaphoreType.DMA]
        return refs

    def bind(self, grad, out, refs, at=None):
        self.grad, self.out = grad, out
        self.source_at = self.at if at is None else at
        refs = list(refs)
        take = lambda n: [refs.pop(0) for _ in range(n)]
        self.sent, self.come = take(2)
        if self.half != "first":
            self.mine, self.got3, self.got4, self.got2 = take(4)
        if self.half != "second":
            self.got0, self.got1 = take(2)
            if not self.resident:
                self.kept, self.own = take(2)
        return self

    def columns(self):
        return pl.ds(self.source_at, self.width)

    def keep(self, i, j):
        if self.half == "second":
            return self.grad.at[j if self.flip else i]
        if self.resident:
            return self.grad.at[i, j, place()[2], :, self.columns()]
        return self.kept.at[i, j]

    def local(self):
        c = place()[2]
        return pltpu.make_async_copy(self.grad.at[:, :, c, :, self.columns()], self.kept, self.own)

    def copy(self, i):
        b, z, c, x, y = place()
        to = sum_partners()
        every = slice(None)
        if i == 0:
            source, target, device = self.grad.at[:, :, 1 - c, :, self.columns()], self.got0, to[0]
        elif i == 1:
            source = self.keep(1 - y, every) if self.flip else self.keep(every, 1 - x)
            target, device = self.got1, to[2 if self.flip else 1]
        elif i == 2:
            source = self.keep(y, 1 - x) if self.flip else self.keep(1 - y, x)
            target, device = self.got2, to[1 if self.flip else 2]
        elif i == 3:
            z0 = lax.rem(z, 2)
            source, target, device = self.mine.at[:, 1 - z0], self.got3, (b, z + 1 - 2 * z0)
        else:
            z0, z1 = lax.rem(z, 2), z // 2
            source, target, device = self.mine.at[1 - z1, z0], self.got4, (b, z + 2 - 4 * z1)
        return pltpu.make_async_remote_copy(
            src_ref=source,
            dst_ref=target,
            send_sem=self.sent.at[i],
            recv_sem=self.come.at[i],
            device_id=device,
            device_id_type=MESH,
        )

    def add(self, target, source):
        self.put(target, target, source)

    def put(self, target, first, second):
        def body(rows):
            target[rows, :] = first[rows, :] + second[rows, :]

        in_steps(self.rows, self.width, body)

    def stage(self, number):
        b, z, c, x, y = place()
        keep = self.keep
        if self.half != "second":
            got0, got1 = self.got0, self.got1
        if self.half == "second" and number == 2:
            self.copy(2).start()
            return
        if self.half == "first" and number == 2:
            self.copy(1).wait_recv()
            for k in range(2):
                self.put(self.out.at[k], keep(y, k) if self.flip else keep(k, x), got1.at[k])
            return
        if number == 0:
            if not self.resident:
                self.local().start()
            self.copy(0).start()
        elif number == 1:
            if not self.resident:
                self.local().wait()
            self.copy(0).wait_recv()
            spots = lambda k: [(k, 0), (k, 1)] if self.flip else [(0, k), (1, k)]
            mine = y if self.flip else x
            for i, j in spots(1 - mine):
                self.add(keep(i, j), got0.at[i, j])
            self.copy(1).start()
            for i, j in spots(mine):
                self.add(keep(i, j), got0.at[i, j])
        elif number == 2:
            self.copy(1).wait_recv()
            if self.flip:
                self.add(keep(y, 1 - x), got1.at[1 - x])
                self.copy(2).start()
                self.add(keep(y, x), got1.at[x])
            else:
                self.add(keep(1 - y, x), got1.at[1 - y])
                self.copy(2).start()
                self.add(keep(y, x), got1.at[y])
        elif number == 3:
            self.copy(2).wait_recv()
            r = self.rows // 4
            mine = keep(y, x)
            for k in range(4):
                rows = slice(k * r, k * r + r)
                value = mine[rows, :].astype(F32) + self.got2[rows, :].astype(F32)
                if self.fold == 2:
                    half = self.width // 2
                    value = jnp.concatenate([value[:, :half], value[:, half:]], axis=0)
                self.mine[k // 2, k % 2] = value.astype(BF16)
            self.copy(3).start()
        elif number == 4:
            self.copy(3).wait_recv()
            z0, z1 = lax.rem(z, 2), z // 2
            self.mine[1 - z1, z0] = self.mine[1 - z1, z0] + self.got3[1 - z1]
            self.copy(4).start()
        elif number == 5:
            self.copy(4).wait_recv()
            z0, z1 = lax.rem(z, 2), z // 2
            value = self.mine[z1, z0].astype(F32) + self.got3[z1].astype(F32) + self.got4[...].astype(F32)
            r, half = self.rows // 4, self.width // 2
            if self.fold == 2:
                self.out[:, self.at : self.at + half] = value[:r]
                self.out[:, self.at + half : self.at + self.width] = value[r:]
            else:
                self.out[:, self.at : self.at + self.width] = value
        else:
            for i in {"": range(5), "first": range(2), "second": range(2, 5)}[self.half]:
                self.copy(i).wait_send()


def run_stage(pair, number):
    for part in pair:
        part.stage(number)


def row_sum(values):
    return jnp.sum(values, axis=0, keepdims=True)


MLP_ROWS = 320
MLP_CHUNK = 512
FC2_SPANS = (512, 256)
MLP_SLOTS = (
    (0, 4, 20, 21),
    (3, 6, 21, 21),
)


def mlp_kernel(setup, *refs):
    count, direct, pairs = setup
    refs = list(refs)
    take = lambda n: [refs.pop(0) for _ in range(n)]
    inputs, mixed, raw_up, to_slot, w_proj, *vectors = take(11)
    w1, b1, w2 = take(3)
    output, d_resid, d_mixed, p_proj, p_fc1, vector, *p_fc2 = take(6 + (len(pairs) or 1))
    hidden, d_branch, upstream, attn, resid, branch, d_hidden, act, slope, d_pre, d_bias, blocks_out = take(12)
    move = Exchange(count)
    move.bind(blocks_out, output, take(len(move.scratch())))
    step = pl.program_id(0)
    seq, width = inputs.shape
    chunk = w1.shape[1]
    steps = act.shape[1] // chunk
    proj_bias, gain1, gain2, shift2, fc2_bias, gain_out = [flat_row(v) for v in vectors]
    blocks = [slice(r, r + MLP_ROWS) for r in range(0, seq, MLP_ROWS)]
    slots = [[] for _ in range(3 * steps + 4)]
    at_chunk = pl.ds(pl.multiple_of(lax.rem(step, steps) * chunk, chunk), chunk)
    grads = []

    def run(slot):
        for tick in slots[slot]:
            tick()

    def run_here(spot):
        for k in range(steps):
            if slots[3 * k + spot]:
                pl.when(step == steps + k)(functools.partial(run, 3 * k + spot))

    if direct:
        grads = take(len(pairs))
        for n, (grad, pair) in enumerate(zip(grads, pairs)):
            bound = [
                part.bind(grad, p_fc2[n].at[f], take(len(part.scratch())), at=f * part.width)
                for f, part in enumerate(pair)
            ]
            for number, slot in zip((0, 1, 2, 6), MLP_SLOTS[n]):
                slots[slot].append(functools.partial(run_stage, bound, number))

    @pl.when(step == 0)
    def _():
        greet(sum_partners() if direct else move.partners())
        for rows in blocks:
            up = matmul(to_slot[rows, :], raw_up[...])
            upstream[rows, :] = up
            d_branch[rows, :] = (gain_out * up).astype(BF16)
            value = matmul(mixed[rows, :], w_proj[...]) + proj_bias
            attn[rows, :] = value
            value = inputs[rows, :] + gain1 * value
            resid[rows, :] = value
            hidden[rows, :] = (normalize(value)[0] * gain2 + shift2).astype(BF16)
        branch[...] = jnp.zeros_like(branch)
        d_hidden[...] = jnp.zeros_like(d_hidden)

    @pl.when(step < steps)
    def _():
        bias_here = flat_row(b1)
        for rows in blocks:
            pre = matmul(hidden[rows, :], w1[...]) + bias_here
            half = 0.5 * (1.0 + lax.erf(pre * 0.7071067811865476))
            slope[rows, at_chunk] = (half + pre * jnp.exp(-0.5 * pre * pre) * 0.3989422804014327).astype(BF16)
            low = (pre * half).astype(BF16)
            act[rows, at_chunk] = low
            branch[rows, :] += matmul(low, w2[...])

    @pl.when(step == steps)
    def _():
        d_gamma2 = jnp.zeros((1, width), F32)
        lows = []
        for rows in blocks:
            mlp = branch[rows, :] + fc2_bias
            d_gamma2 += row_sum(upstream[rows, :] * mlp)
            lows.append((resid[rows, :] + gain_out * mlp).astype(BF16))
        vector[0, 0:1, :] = d_gamma2
        ordered = t_matmul(to_slot[...], jnp.concatenate(lows, axis=0)).astype(BF16)
        blocks_out[...] = ordered.reshape(blocks_out.shape)
        move.start()

    if direct:
        for k in range(len(grads)):

            @pl.when(step == steps + k)
            def _(k=k):
                at = sum(FC2_SPANS[:k])
                partial = t_matmul(act[...], d_branch[:, at : at + FC2_SPANS[k]]).astype(BF16)
                grads[k][...] = partial.reshape(grads[k].shape)
    else:

        @pl.when(step == steps)
        def _():
            p_fc2[0][...] = t_matmul(act[...], d_branch[...]).astype(BF16)

    run_here(0)

    @pl.when(step >= steps)
    def _():
        bias_sum = jnp.zeros((1, chunk), F32)
        for n, rows in enumerate(blocks):
            if n == 1:
                run_here(1)
            back = (matmul_t(d_branch[rows, :], w2[...]) * slope[rows, at_chunk].astype(F32)).astype(BF16)
            d_pre[rows, :] = back
            bias_sum += row_sum(back.astype(F32))
            d_hidden[rows, :] += matmul_t(back, w1[...])
        d_bias[:, at_chunk] = bias_sum
        run_here(2)
        p_fc1[...] = t_matmul(hidden[...], d_pre[...]).astype(BF16)

    @pl.when(step == 2 * steps - 1)
    def _():
        run(3 * steps)
        d_fc2b = d_ln2g = d_ln2b = d_gamma1 = d_projb = jnp.zeros((1, width), F32)
        for n, rows in enumerate(blocks):
            d_fc2b += row_sum(d_branch[rows, :].astype(F32))
            normed, factor = normalize(resid[rows, :])
            grad = d_hidden[rows, :]
            d_ln2g += row_sum(grad * normed)
            d_ln2b += row_sum(grad)
            grad = upstream[rows, :] + norm_back(grad, normed, factor, gain2)
            d_resid[rows, :] = grad
            d_gamma1 += row_sum(grad * attn[rows, :])
            grad = (gain1 * grad).astype(BF16)
            d_branch[rows, :] = grad
            d_projb += row_sum(grad.astype(F32))
            d_mixed[rows, :] = matmul_t(grad, w_proj[...]).astype(BF16)
            run(3 * steps + 1 + n)
        p_proj[...] = t_matmul(mixed[...], d_branch[...]).astype(BF16)
        zero = jnp.zeros((2, width), F32)
        vector[0, 1:8, :] = jnp.concatenate([d_fc2b, d_ln2g, d_ln2b, d_gamma1, d_projb, zero], axis=0)
        pieces = [d_bias[:, i * width : (i + 1) * width] for i in range(4)]
        vector[1] = jnp.concatenate(pieces + [zero, zero], axis=0)
        run(3 * steps + 3)
        move.finish()


def fc2_pairs(hidden, half):
    pairs, at = [], 0
    for span in FC2_SPANS:
        part = span // 2
        pairs.append([WeightSum(hidden // 8, at + f * part, part, f == 1, True, half) for f in (0, 1)])
        at += span
    return pairs


def mlp(inputs, mixed, raw_up, to_slot, w_proj, vectors, w1, b1, w2, count, direct):
    seq, width = inputs.shape
    hidden = w1.shape[1]
    chunk = MLP_CHUNK
    steps = hidden // chunk
    pairs = fc2_pairs(hidden, "first") if direct else []
    flat = lambda dtype: jax.ShapeDtypeStruct((seq, width), dtype)
    vmem = lambda dtype: pltpu.VMEM((seq, width), dtype)
    parts = [(2, 2, hidden // 8, span // 2) for span in FC2_SPANS] if direct else [(hidden, width)]
    turn = lambda k: lax.rem(k, steps)
    blocks = (count, seq // count, width)
    return pl.pallas_call(
        functools.partial(mlp_kernel, (count, direct, pairs)),
        grid=(2 * steps,),
        out_shape=[
            jax.ShapeDtypeStruct(blocks, BF16),
            flat(F32),
            flat(BF16),
            jax.ShapeDtypeStruct((width, width), BF16),
            jax.ShapeDtypeStruct((width, hidden), BF16),
            jax.ShapeDtypeStruct((2, 8, width), F32),
        ]
        + [jax.ShapeDtypeStruct(p, BF16) for p in parts],
        in_specs=[
            whole(inputs.shape),
            whole(mixed.shape),
            whole(raw_up.shape),
            whole(to_slot.shape),
            whole(w_proj.shape),
        ]
        + [whole(v.shape) for v in vectors]
        + [
            pl.BlockSpec((width, chunk), lambda k: (0, turn(k))),
            pl.BlockSpec((chunk,), lambda k: (turn(k),)),
            pl.BlockSpec((chunk, width), lambda k: (turn(k), 0)),
        ],
        out_specs=[
            ANY,
            whole((seq, width)),
            whole((seq, width)),
            whole((width, width)),
            pl.BlockSpec((width, chunk), lambda k: (0, jnp.maximum(k - steps, 0))),
            whole((2, 8, width)),
        ]
        + [whole(p) for p in parts],
        scratch_shapes=[
            vmem(BF16), vmem(BF16), vmem(F32), vmem(F32), vmem(F32), vmem(F32), vmem(F32),
            pltpu.VMEM((seq, hidden), BF16), pltpu.VMEM((seq, hidden), BF16),
            pltpu.VMEM((seq, chunk), BF16), pltpu.VMEM((1, hidden), F32), pltpu.VMEM(blocks, BF16),
        ]
        + Exchange(count).scratch()
        + [pltpu.VMEM((2, 2, 2, hidden // 8, span), BF16) for span in FC2_SPANS[: len(pairs)]]
        + [s for pair in pairs for part in pair for s in part.scratch()],
        compiler_params=pltpu.CompilerParams(
            collective_id=1, has_side_effects=True, vmem_limit_bytes=VMEM_LIMIT
        ),
        name="mlp",
    )(inputs, mixed, raw_up, to_slot, w_proj, *vectors, w1, b1, w2)


def swap(value, axis, bit, count):
    return lax.ppermute(value, axis, [(i, i ^ bit) for i in range(count)])


def bits_of(count):
    return [1 << i for i in range(count.bit_length() - 1)]


def scatter_sum(grad, batch, blk):
    places = [("batch", bit, batch) for bit in bits_of(batch)][::-1]
    places += [("blk", bit, blk) for bit in bits_of(blk)][::-1]
    value = grad.reshape((2,) * len(places) + (grad.shape[0] >> len(places), grad.shape[1]))
    left = list(places)
    for spot in places:
        axis, bit, count = spot
        at = left.index(spot)
        left.remove(spot)
        mine = jnp.bitwise_and(lax.axis_index(axis) // bit, 1)
        sent = lax.dynamic_index_in_dim(value, 1 - mine, at, keepdims=False)
        kept = lax.dynamic_index_in_dim(value, mine, at, keepdims=False)
        got = swap(sent, axis, bit, count)
        value = kept.astype(F32) + got.astype(F32)
        if left:
            value = value.astype(BF16)
    return value


def total_sum(value, batch, blk):
    for bit in bits_of(batch):
        value = value + swap(value, "batch", bit, batch)
    for bit in bits_of(blk):
        value = value + swap(value, "blk", bit, blk)
    return value


def unpack_kernel(plan, early, late, table, *refs):
    refs = list(refs)
    take = lambda n: [refs.pop(0) for _ in range(n)]
    sources = [take(n) for n in plan]
    vectors = take(11)
    out_low, out_high = take(2)
    targets = take(len(plan))
    turned = take(1)[0]
    for group, target in zip(sources, targets):
        at = 0
        for source in group:
            size = source.shape[-1]
            target[..., at : at + size] = source[...]
            at += size
    for i in range(6):
        vectors[i][...] = early[0, i : i + 1, :].reshape(vectors[i].shape)
    for n in range(2):
        for i in range(2):
            rows = [late[n, 6 * i + k : 6 * i + k + 1, :] for k in range(6)]
            out = vectors[6 + 2 * n + i]
            out[...] = jnp.concatenate(rows, axis=1).reshape(out.shape)
    rows = [early[1, i : i + 1, :] for i in range(4)]
    vectors[10][...] = jnp.concatenate(rows, axis=1).reshape(vectors[10].shape)
    heads = out_low.shape[0]
    for n, (out, side, pad) in enumerate(((out_low, SIDE_LOW, G_HIGH - G_LOW), (out_high, SIDE, 0))):
        value = jnp.concatenate([table[n, k * 48 : (k + 1) * 48, :] for k in range(heads // 2)], axis=1)
        turned[n] = jnp.concatenate([value, jnp.zeros((80, 64 * heads), F32)], axis=0).T
        here = turned.at[n]
        for r in range(side):
            rows = pl.ds(SIDE - 1 - r - pad, heads, stride=64)
            out[:, r * side : (r + 1) * side] = here[rows, :][:, pad : pad + side]
        for i in range(3):
            out[:, side * side + i : side * side + i + 1] = here[pl.ds(i, heads, stride=64), :][:, 47:48]


def unpack(early, late, table, groups, width, hidden, heads):
    outs = [jax.ShapeDtypeStruct((width,), F32)] * 10 + [jax.ShapeDtypeStruct((hidden,), F32)]
    outs += [jax.ShapeDtypeStruct((heads, side * side + 3), F32) for side in (SIDE_LOW, SIDE)]
    outs += [
        jax.ShapeDtypeStruct(g[0].shape[:-1] + (sum(p.shape[-1] for p in g),), g[0].dtype) for g in groups
    ]
    pieces = [p for g in groups for p in g]
    vmem = pl.BlockSpec(memory_space=pltpu.VMEM)
    result = pl.pallas_call(
        functools.partial(unpack_kernel, [len(g) for g in groups]),
        out_shape=outs,
        in_specs=[vmem] * (3 + len(pieces)),
        out_specs=[vmem] * (13 + len(groups)),
        scratch_shapes=[pltpu.VMEM((2, 64 * heads, 128), F32)],
        compiler_params=pltpu.CompilerParams(vmem_limit_bytes=VMEM_LIMIT),
        name="unpack",
    )(early, late, table, *pieces)
    return result[:11], result[11].T, result[12].T, result[13:]


def swap(value, axis, bit, count):
    return lax.ppermute(value, axis, [(i, i ^ bit) for i in range(count)])


def bits_of(count):
    return [1 << i for i in range(count.bit_length() - 1)]


def scatter_sum(grad, batch, blk):
    places = [("batch", bit, batch) for bit in bits_of(batch)][::-1]
    places += [("blk", bit, blk) for bit in bits_of(blk)][::-1]
    value = grad.reshape((2,) * len(places) + (grad.shape[0] >> len(places), grad.shape[1]))
    left = list(places)
    for spot in places:
        axis, bit, count = spot
        at = left.index(spot)
        left.remove(spot)
        mine = jnp.bitwise_and(lax.axis_index(axis) // bit, 1)
        sent = lax.dynamic_index_in_dim(value, 1 - mine, at, keepdims=False)
        kept = lax.dynamic_index_in_dim(value, mine, at, keepdims=False)
        got = swap(sent, axis, bit, count)
        value = kept.astype(F32) + got.astype(F32)
        if left:
            value = value.astype(BF16)
    return value


def total_sum(value, batch, blk):
    for bit in bits_of(batch):
        value = value + swap(value, "batch", bit, batch)
    for bit in bits_of(blk):
        value = value + swap(value, "blk", bit, blk)
    return value


def shards(
    batch,
    blk,
    tokens,
    resolution,
    positions,
    ln1_gain,
    ln1_bias,
    w_qkv,
    q_bias,
    v_bias,
    w_proj,
    proj_bias,
    gamma1,
    ln2_gain,
    ln2_bias,
    w_fc1,
    fc1_bias,
    w_fc2,
    fc2_bias,
    gamma2,
    rel_low,
    rel_high,
    grad_out,
):
    images, rows, width = tokens.shape
    seq = positions.shape[1]
    heads = rel_low.shape[1]
    assert images == blk and rows * blk == seq and width == heads * 64
    direct = (batch, blk) == (8, 4)
    spread_np, bits_np = lane_tables()
    spread = jnp.asarray(spread_np, BF16)
    bits = jnp.asarray(bits_np)
    patches = jnp.asarray(slot_tables(seq)[2].T, F32)
    to_slot, inputs, qkv, probs, mixed, raw_up = front(
        resolution,
        positions,
        rel_low,
        rel_high,
        spread,
        bits,
        patches,
        (ln1_gain, ln1_bias, q_bias, v_bias),
        w_qkv,
        tokens,
        grad_out,
        blk,
    )
    output, d_resid, d_mixed, p_proj, p_fc1, early, *p_fc2 = mlp(
        inputs,
        mixed,
        raw_up.reshape(seq, width),
        to_slot,
        w_proj,
        (proj_bias, gamma1, ln2_gain, ln2_bias, fc2_bias, gamma2),
        w_fc1,
        fc1_bias,
        w_fc2,
        blk,
        direct,
    )
    grad_tokens, g_qkv, *sums, late, d_table = tail(
        resolution,
        qkv,
        probs,
        d_mixed,
        patches,
        spread,
        bits,
        (ln1_gain, ln1_bias),
        inputs,
        d_resid,
        to_slot,
        w_qkv,
        (p_fc1, p_proj),
        p_fc2,
        early,
        blk,
        direct,
    )
    groups = [[output], [grad_tokens]]
    if direct:
        g_fc1, g_proj, g_fc2, early = sums
        groups += [[g] for g in (g_fc1, g_fc2, g_proj, g_qkv)]
    else:
        g_fc1, g_fc2, g_proj, g_qkv = [scatter_sum(g, batch, blk) for g in (p_fc1, *p_fc2, p_proj, g_qkv)]
        early, late, d_table = [total_sum(v, batch, blk) for v in (early, late, d_table)]
    vectors, s_low, s_high, rest = unpack(early, late, d_table, groups, width, w_fc1.shape[1], heads)
    s_gamma2, s_fc2b, s_ln2g, s_ln2b, s_gamma1, s_projb, s_ln1g, s_ln1b, s_qb, s_vb, s_fc1b = vectors
    output, grad_tokens = rest[:2]
    if direct:
        g_fc1, g_fc2, g_proj, g_qkv = rest[2:]
    return (
        output,
        grad_tokens,
        s_ln1g,
        s_ln1b,
        g_qkv,
        s_qb,
        s_vb,
        g_proj,
        s_projb,
        s_gamma1,
        s_ln2g,
        s_ln2b,
        g_fc1,
        s_fc1b,
        g_fc2,
        s_fc2b,
        s_gamma2,
        s_low,
        s_high,
    )


def solution(mesh):
    rows = P("batch", "blk", None)
    shared = P(("batch", "blk"), None)
    in_specs = (rows, P("batch"), P("batch", None)) + (P(),) * 17 + (rows,)
    out_specs = (
        (rows, rows, P(), P(), shared, P(), P(), shared)
        + (P(),) * 4
        + (shared, P(), shared)
        + (P(),) * 4
    )
    return jax.shard_map(
        functools.partial(shards, mesh.shape["batch"], mesh.shape["blk"]),
        mesh=mesh,
        in_specs=in_specs,
        out_specs=out_specs,
        check_vma=False,
    )
```

```python
import functools

import jax
import jax.numpy as jnp
import numpy as np
from jax import lax
from jax.experimental import pallas as pl
from jax.experimental.pallas import tpu as pltpu
from jax.sharding import PartitionSpec as P

G_LOW = 14
G_HIGH = 24
SIDE_LOW = 2 * G_LOW - 1
SIDE = 2 * G_HIGH - 1
CELLS = G_HIGH * G_HIGH
SPAN = 1152
F32 = jnp.float32
BF16 = jnp.bfloat16


def normalize(values):
    center = values - jnp.mean(values, axis=-1, keepdims=True)
    factor = lax.rsqrt(jnp.mean(center * center, axis=-1, keepdims=True) + 1e-06)
    return center * factor, factor


def norm_back(grad, normed, factor, gain):
    scaled = grad * gain
    return factor * (
        scaled
        - jnp.mean(scaled, axis=-1, keepdims=True)
        - normed * jnp.mean(scaled * normed, axis=-1, keepdims=True)
    )


def matmul(left, right):
    return jnp.dot(left, right, preferred_element_type=F32)


def matmul_t(left, right):
    return lax.dot_general(left, right, (((1,), (1,)), ((), ())), preferred_element_type=F32)


def t_matmul(left, right):
    return lax.dot_general(left, right, (((0,), (0,)), ((), ())), preferred_element_type=F32)


def slot_tables(seq):
    tokens = np.arange(seq)
    tables = []
    for grid in (G_LOW, G_HIGH):
        cells = np.arange(CELLS)
        used = (cells // G_HIGH < grid) & (cells % G_HIGH < grid)
        free = np.concatenate([cells[~used], np.arange(CELLS + 1, seq)])
        slot = np.full(seq, CELLS)
        slot[1 + grid * grid :] = free
        patch = np.concatenate([used, np.zeros(seq - CELLS, bool)])
        key = patch.copy()
        key[CELLS] = True
        tables.append((slot, (tokens >= 1) & (tokens < 1 + grid * grid), patch, key))
    return [np.stack(parts) for parts in zip(*tables)]


def lane_tables():
    lanes = np.arange(SPAN)
    shift = G_HIGH - 1 - lanes % G_HIGH
    bits = (shift[None, :] >> np.arange(8)[:, None]) & 1
    return bits.astype(np.int32)


def spread_of(rows, first):
    row = (lax.broadcasted_iota(jnp.int32, (rows, SPAN), 0) - first) * G_HIGH
    lane = lax.broadcasted_iota(jnp.int32, (rows, SPAN), 1) - row
    inside = (lane >= 0) & (lane < G_HIGH) & (row >= 0) & (row < SIDE * G_HIGH)
    return jnp.where(inside, 1.0, 0.0).astype(BF16)


def slide(values, bits, down):
    for k in range(5):
        amount = 1 << k if down else 48 - (1 << k)
        values = jnp.where(bits[k : k + 1, :] > 0, pltpu.roll(values, amount, 0), values)
    return values


VMEM_LIMIT = 62 << 20


def whole(shape):
    return pl.BlockSpec(shape, lambda h: (0,) * len(shape))


def once(shape):
    return pl.BlockSpec(shape, lambda h: (0,) * len(shape), pipeline_mode=pl.Buffered(1))


ANY = pl.BlockSpec(memory_space=pl.ANY)
SMEM = pl.BlockSpec(memory_space=pltpu.SMEM)


def flat_row(ref):
    return ref[...].astype(F32).reshape(1, ref.shape[0])


def front_kernel(
    count, resolution, cells, low_t, high_t, bits, slot_of, is_patch, patches, masks,
    ln1_gain, ln1_bias, q_bias, v_bias, w_qkv, tokens, grad_out,
    to_slot, inputs, qkv, probs, mixed, raw_up, bias, raw, landed, inner_low, inner_high, wide, full, spread, *refs,
):
    step = pl.program_id(0)
    me = lax.axis_index("blk")
    high = resolution[me] == 1
    seq = full.shape[0]
    heads = low_t.shape[0]
    width = inputs.shape[1]
    size = len(Exchange(count).scratch())
    move = Exchange(count).bind(tokens, raw, refs[:size])
    move_up = Exchange(count).bind(grad_out, landed, refs[size:])

    @pl.when(step == 0)
    def _():
        greet(move.partners())
        move.start()
        here = cells[pl.ds(me, 1), :]
        grid = jnp.where(high, G_HIGH, G_LOW)
        row = jnp.zeros_like(here)
        for k in range(1, G_HIGH):
            row += (here >= k * grid).astype(jnp.int32)
        at = row * G_HIGH + here - row * grid
        patch = jnp.where(high, is_patch[1:2, :], is_patch[0:1, :])
        other = jnp.where(high, slot_of[1:2, :], slot_of[0:1, :])
        slot = jnp.where(patch > 0, at, other)
        spots = lax.broadcasted_iota(jnp.int32, (seq, seq), 0)
        to_slot[...] = jnp.where(spots == slot, 1.0, 0.0).astype(BF16)
        spread[...] = spread_of(48, 0)
        inner_low[...] = jnp.zeros_like(inner_low)
        inner_high[...] = jnp.zeros_like(inner_high)
        low_f, high_f = low_t[...].astype(F32), high_t[...].astype(F32)
        pad = G_HIGH - G_LOW
        for j in range(SIDE):
            r = SIDE - 1 - j
            inner_high[j * 16 : j * 16 + heads, 0:SIDE] = high_f[:, r * SIDE : (r + 1) * SIDE]
            r -= pad
            if 0 <= r < SIDE_LOW:
                inner_low[j * 16 : j * 16 + heads, pad : pad + SIDE_LOW] = low_f[
                    :, r * SIDE_LOW : (r + 1) * SIDE_LOW
                ]

    @pl.when(step < heads)
    def _():
        rows = pl.ds(step, 48, stride=16)
        table = jnp.where(high, inner_high[rows, :], inner_low[rows, :]).astype(BF16)
        wide[...] = slide(t_matmul(table, spread[...])[0:48], bits, False)[0:G_HIGH]
        for r in range(G_HIGH):
            at = (G_HIGH - 1 - r) * G_HIGH
            full[r * G_HIGH : (r + 1) * G_HIGH, 0:CELLS] = wide[:, at : at + CELLS]
        column = lax.broadcasted_iota(jnp.int32, (1, seq), 1)
        ends = [t[:, t.shape[1] - 3 : t.shape[1]].astype(F32) for t in (low_t, high_t)]
        special = jnp.where(high, ends[1], ends[0])
        here = lax.broadcasted_iota(jnp.int32, special.shape, 0) == step
        special = jnp.sum(jnp.where(here, special, 0.0), axis=0, keepdims=True)
        inner_row = jnp.where(column < CELLS, special[:, 0:1], special[:, 2:3])
        values = jnp.where(column < CELLS, full[...], special[:, 1:2])
        patch = jnp.where(high, patches[:, 1:2], patches[:, 0:1])
        mask = jnp.where(high, masks[1:2, :], masks[0:1, :])
        values = jnp.where(patch > 0.0, values, inner_row)
        bias[step] = (values + mask).astype(BF16)

    @pl.when(step == heads)
    def _():
        move.finish()
        move_up.start()
        value = matmul(to_slot[...], raw[...].reshape(seq, width))
        inputs[...] = value
        hidden = (normalize(value)[0] * flat_row(ln1_gain) + flat_row(ln1_bias)).astype(BF16)
        shifts = [flat_row(q_bias), 0.0, flat_row(v_bias)]
        for n in range(3):
            part = slice(n * width, (n + 1) * width)
            qkv[:, part] = (matmul(hidden, w_qkv[:, part]) + shifts[n]).astype(BF16)

    @pl.when(step >= heads)
    def _():
        pair = step - heads
        query, keys, values = [
            qkv[:, pl.ds(pl.multiple_of(n * width + pair * 128, 128), 128)] for n in range(3)
        ]
        for h in range(2):
            at = slice(h * 64, h * 64 + 64)
            scores = matmul_t(query[:, at] * 0.125, keys[:, at]) + bias[2 * pair + h].astype(F32)
            expo = jnp.exp(scores - jnp.max(scores, axis=-1, keepdims=True))
            low = (expo * (1.0 / jnp.sum(expo, axis=-1, keepdims=True))).astype(BF16)
            probs[h] = low
            mixed[:, at] = matmul(low, values[:, at]).astype(BF16)

    @pl.when(step == pl.num_programs(0) - 1)
    def _():
        move_up.finish()
        raw_up[...] = landed[...]


def front(resolution, cells, rel_low, rel_high, bits, patches, vectors, w_qkv, tokens, grad_out, count):
    heads = rel_low.shape[1]
    seq = cells.shape[1]
    width = w_qkv.shape[0]
    slot_np, token_np, _, key_np = slot_tables(seq)
    slot_of = jnp.asarray(slot_np, jnp.int32)
    is_patch = jnp.asarray(token_np, jnp.int32)
    masks = jnp.asarray(np.where(key_np, 0.0, -1e30), F32)
    operands = (rel_low.T, rel_high.T, bits, slot_of, is_patch, patches, masks) + vectors + (w_qkv,)
    late = lambda i: jnp.maximum(i - heads, 0)
    return pl.pallas_call(
        functools.partial(front_kernel, count),
        grid=(heads + heads // 2,),
        out_shape=(
            jax.ShapeDtypeStruct((seq, seq), BF16),
            jax.ShapeDtypeStruct((seq, width), F32),
            jax.ShapeDtypeStruct((seq, 3 * width), BF16),
            jax.ShapeDtypeStruct((heads, seq, seq), BF16),
            jax.ShapeDtypeStruct((seq, width), BF16),
            jax.ShapeDtypeStruct(grad_out.shape, BF16),
        ),
        in_specs=[SMEM, whole(cells.shape)] + [whole(o.shape) for o in operands] + [ANY, ANY],
        out_specs=(
            whole((seq, seq)),
            whole((seq, width)),
            whole((seq, 3 * width)),
            pl.BlockSpec((2, seq, seq), lambda i: (late(i), 0, 0)),
            pl.BlockSpec((seq, 128), lambda i: (0, late(i))),
            once(grad_out.shape),
        ),
        scratch_shapes=[
            pltpu.VMEM((heads, seq, seq), BF16),
            pltpu.VMEM(tokens.shape, BF16),
            pltpu.VMEM(grad_out.shape, BF16),
            pltpu.VMEM((48 * 16, 128), F32),
            pltpu.VMEM((48 * 16, 128), F32),
            pltpu.VMEM((G_HIGH, SPAN), F32),
            pltpu.VMEM((seq, seq), F32),
            pltpu.VMEM((48, SPAN), BF16),
        ]
        + Exchange(count).scratch()
        + Exchange(count).scratch(),
        compiler_params=pltpu.CompilerParams(
            collective_id=0, has_side_effects=True, vmem_limit_bytes=VMEM_LIMIT
        ),
        name="front",
    )(resolution, cells, *operands, tokens, grad_out)


def head_grads(query, keys, values, weights, up, patch, spread, bits, score, wide, lanes):
    ups = matmul_t(up, values)
    weight = weights.astype(F32)
    product = weight * ups
    ds = product - weight * jnp.sum(product, axis=-1, keepdims=True)
    ds_low = ds.astype(BF16)
    d_query = (matmul(ds_low, keys) * 0.125).astype(BF16)
    d_key = t_matmul(ds_low, query * 0.125).astype(BF16)
    d_value = t_matmul(weights, up).astype(BF16)
    total = jnp.sum(ds, axis=0, keepdims=True)
    ds = ds * patch
    score[...] = ds
    inside = jnp.sum(ds, axis=0, keepdims=True)
    wide[...] = jnp.zeros_like(wide)
    for r in range(G_HIGH):
        off = (G_HIGH - 1 - r) * G_HIGH
        wide[:, off : off + CELLS] += score[r * G_HIGH : (r + 1) * G_HIGH, 0:CELLS]
    flat = slide(jnp.concatenate([wide[...], jnp.zeros_like(wide)], axis=0), bits, True)
    first = flat.astype(BF16)
    rest = flat - first.astype(F32)
    second = rest.astype(BF16)
    third = (rest - second.astype(F32)).astype(BF16)
    table = matmul_t(first, spread) + matmul_t(second, spread) + matmul_t(third, spread)
    column = lax.broadcasted_iota(jnp.int32, total.shape, 1)
    lane = lax.broadcasted_iota(jnp.int32, (1, 128), 1)
    outside = total - inside
    edge = jnp.zeros((1, 128), F32)
    for i, value in enumerate((
        jnp.where(column < CELLS, outside, 0.0),
        jnp.where(column == CELLS, inside, 0.0),
        jnp.where(column == CELLS, outside, 0.0),
    )):
        edge += jnp.where(lane == lanes + i, jnp.sum(value, axis=1, keepdims=True), 0.0)
    return d_query, d_key, d_value, table, edge


def by_lanes(row):
    return jnp.concatenate([row[:, i : i + 128] for i in range(0, row.shape[1], 128)], axis=0)


FC1_SLOTS = ((0, 2, 6, 10, 13, 20, 26), (0, 3, 8, 11, 13, 20, 26), (1, 3, 9, 12, 14, 20, 26))
PROJ_SLOTS = ((8, 10, 13, 16, 21, 22, 26),)
QKV_SLOTS = (
    (8, 10, 13, 16, 21, 22, 26),
    (9, 11, 16, 17, 21, 22, 26),
    (12, 13, 17, 18, 21, 22, 26),
)
FC2_SLOTS = ((0, 4, 7, 18, 26), (0, 5, 8, 18, 26))
EARLY_SLOTS = (0, 1, 3, 5, 7, 9)
TABLE_SLOTS = ((8, 9, 11, 16, 17, 18), (12, 13, 16, 17, 18, 19))
LATE_SLOTS = (15, 15, 16, 17, 18, 19)
TABLE_PAIRS = 4


def tail_kernel(setup, *refs):
    count, groups, grads = setup
    direct = grads > 0
    fc1_pairs, proj_pairs, fc2_second, qkv_groups = groups
    refs = list(refs)
    take = lambda n: [refs.pop(0) for _ in range(n)]
    resolution, query, keys, values, probs, upstream, patches, bits, ln1_gain, ln1_bias = take(10)
    sources = take(4)
    partials = take(grads)
    early, *p_fc2 = take(1 + len(fc2_second)) if direct else [None]
    moved, g_qkv = take(2)
    g_fc1, g_proj, g_fc2, early_sum = take(4) if direct else [None] * 4
    late_sum, table_sum = take(2)
    score, wide, d_qkv, hidden, table_a, table_b, tokens, landed, late, spread = take(10)
    loaded = take(4)
    load_sems = take(1)[0]
    move = Exchange(count)
    move.bind(tokens, landed, take(len(move.scratch())))
    step = pl.program_id(0)
    steps = pl.num_programs(0) - 1
    seq, width = loaded[0].shape
    first_rows = table_a.shape[1]
    slots = [[] for _ in range(28)]

    def run(slot):
        for tick in slots[slot]:
            tick()

    if direct:
        grad = take(1)[0]
        scratch_of = lambda part: take(len(part.scratch()))

        def plan(bound, own, numbers=range(7)):
            for number, slot in zip(numbers, own):
                slots[slot].append(functools.partial(run_stage, bound, number))

        small = VectorSum(early.shape[1:])
        plan([small.bind(early, early_sum, scratch_of(small))], EARLY_SLOTS)
        for ref, at, own in zip((table_a, table_b), (0, first_rows), TABLE_SLOTS):
            part = VectorSum(ref.shape[1:], True)
            plan([part.bind(ref, table_sum, scratch_of(part), at)], own)
        part = VectorSum(late.shape, split=False)
        plan([part.bind(late, late_sum, scratch_of(part))], LATE_SLOTS)
        for pair, own, source in zip(fc2_second, FC2_SLOTS, p_fc2):
            bound = [part.bind(source.at[f], g_fc2, scratch_of(part)) for f, part in enumerate(pair)]
            plan(bound, own, (2, 3, 4, 5, 6))
        for k, (pair, spots) in enumerate(zip(fc1_pairs, FC1_SLOTS)):
            plan([part.bind(partials[0].at[2 * k + f], g_fc1, scratch_of(part), 0) for f, part in enumerate(pair)], spots)
        for pair, spots in zip(proj_pairs, PROJ_SLOTS):
            plan([part.bind(partials[1], g_proj, scratch_of(part)) for part in pair], spots)
        for group, spots in zip(qkv_groups, QKV_SLOTS):
            plan([part.bind(grad, g_qkv, scratch_of(part)) for part in group], spots)

    loads = [
        pltpu.make_async_copy(source, target, load_sems.at[i])
        for i, (source, target) in enumerate(zip(sources, loaded))
    ]
    inputs, d_resid, to_slot, w_qkv = loaded

    @pl.when(step == 0)
    def _():
        greet(sum_partners() if direct else move.partners())
        for load in loads:
            load.start()
        for h in range(2):
            spread[h] = spread_of(128, 64 * h)

    high = resolution[lax.axis_index("blk")] == 1

    @pl.when(step < steps)
    def _():
        patch = jnp.where(high, patches[:, 1:2], patches[:, 0:1])
        total = jnp.zeros((48, 128), F32)
        edge = jnp.zeros((1, 128), F32)
        parts3 = [[], [], []]
        for h in range(2):
            for k in range(6):
                if slots[2 * k + h]:
                    pl.when(step == k)(functools.partial(run, 2 * k + h))

            at = slice(h * 64, h * 64 + 64)
            *heads3, part, ends = head_grads(
                query[:, at], keys[:, at], values[:, at], probs[h], upstream[:, at],
                patch, spread[h], bits, score, wide, h * 64,
            )
            total += part
            edge += ends
            for n in range(3):
                parts3[n].append(heads3[n])
        for n in range(3):
            at = pl.ds(pl.multiple_of(n * width + step * 128, 128), 128)
            d_qkv[:, at] = jnp.concatenate(parts3[n], axis=1)
        row = lax.broadcasted_iota(jnp.int32, (48, 128), 0)
        total = jnp.where(row == 47, edge, total)
        for k in range(6):

            @pl.when(step == k)
            def _(k=k):
                ref, at = (table_a, k) if k < TABLE_PAIRS else (table_b, k - TABLE_PAIRS)
                ref[0, at * 48 : at * 48 + 48, :] = jnp.where(high, 0.0, total)
                ref[1, at * 48 : at * 48 + 48, :] = jnp.where(high, total, 0.0)

    @pl.when(step == 1)
    def _():
        loads[0].wait()
        hidden[...] = (normalize(inputs[...])[0] * flat_row(ln1_gain) + flat_row(ln1_bias)).astype(BF16)

    for k in range(3):

        @pl.when(step == 2 * k + 1)
        def _(k=k):
            for n in range(3):
                at = slice(n * width + k * 256, n * width + k * 256 + 256)
                partial = t_matmul(hidden[...], d_qkv[:, at]).astype(BF16)
                if direct:
                    grad[:, :, :, :, at] = partial.reshape(2, 2, 2, width // 8, 256)
                else:
                    g_qkv[:, at] = partial

    @pl.when(step == steps)
    def _():
        run(12)
        for load in loads[1:]:
            load.wait()
        gain = flat_row(ln1_gain)
        def enter(rows, totals):
            d_gain, d_shift = totals
            back = matmul_t(d_qkv[rows, :], w_qkv[...])
            value, scale = normalize(inputs[rows, :])
            hidden[rows, :] = (d_resid[rows, :] + norm_back(back, value, scale, gain)).astype(BF16)
            return d_gain + row_sum(back * value), d_shift + row_sum(back)

        d_gain, d_shift = row_blocks(seq, seq // 2, enter, (jnp.zeros((1, width), F32),) * 2)
        run(13)
        run(14)
        ordered = t_matmul(to_slot[...], hidden[...]).astype(BF16)
        tokens[...] = ordered.reshape(tokens.shape)
        sums4 = [d_gain, d_shift] + [
            row_sum(d_qkv[:, n * width : (n + 1) * width].astype(F32)) for n in (0, 2)
        ]
        late[...] = jnp.concatenate([by_lanes(v) for v in sums4], axis=0)
        run(15)
        move.start()
        if direct:
            for slot in range(16, 28):
                run(slot)
        else:
            late_sum[...] = late[...]
            table_sum[:, 0:first_rows] = table_a[...]
            table_sum[:, first_rows:] = table_b[...]
        move.finish()
        moved[...] = landed[...]


def tail(resolution, qkv, probs, upstream, patches, bits, vectors, inputs, d_resid, to_slot, w_qkv, partials, p_fc2, early, count, direct):
    seq, width = inputs.shape
    steps = width // 128
    clip = lambda h: jnp.minimum(h, steps - 1)
    column = lambda part: pl.BlockSpec((seq, 128), lambda h: (0, part * steps + clip(h)))
    blocks = jax.ShapeDtypeStruct((count, seq // count, width), BF16)
    late, table = (24, 128), (2, 48 * steps, 128)
    tables = [(2, 48 * TABLE_PAIRS, 128), (2, 48 * (steps - TABLE_PAIRS), 128)]
    groups, views, more, outs = ((), (), (), ()), [], [], []
    g_qkv = jax.ShapeDtypeStruct((width, 3 * width), BF16)
    if direct:
        views = [g.reshape(*g.shape[:-2], 2, 2, 2, g.shape[-2] // 8, g.shape[-1]) for g in partials]
        more = [early, *p_fc2]
        chunks, _, chunk = partials[0].shape
        hidden = chunks * chunk
        share = lambda columns, rows=width: jax.ShapeDtypeStruct((rows // 32, columns), F32)
        outs = [share(hidden), share(width), share(width, hidden), jax.ShapeDtypeStruct(early.shape, F32)]
        g_qkv = share(3 * width)
        fc1_pairs = [
            [WeightSum(width // 8, (2 * k + f) * chunk, chunk, f == 1) for f in (0, 1)] for k in range(chunks // 2)
        ]
        proj_pairs = [[WeightSum(width // 8, 0, 256, False), WeightSum(width // 8, 256, 512, True)]]
        fc2_second = fc2_pairs(hidden, "second")
        qkv_groups = [
            [WeightSum(width // 8, n * width + k * 256, 256, (n + k) % 2 == 1, True) for n in range(3)]
            for k in range(3)
        ]
        groups = (fc1_pairs, proj_pairs, fc2_second, qkv_groups)
    outs = list(outs) + [jax.ShapeDtypeStruct(late, F32), jax.ShapeDtypeStruct(table, F32)]
    held = (inputs, d_resid, to_slot, w_qkv)
    scratch = [
        pltpu.VMEM((seq, seq), F32),
        pltpu.VMEM((G_HIGH, SPAN), F32),
        pltpu.VMEM((seq, 3 * width), BF16),
        pltpu.VMEM((seq, width), BF16),
        pltpu.VMEM(tables[0], F32),
        pltpu.VMEM(tables[1], F32),
        pltpu.VMEM(blocks.shape, BF16),
        pltpu.VMEM(blocks.shape, BF16),
        pltpu.VMEM(late, F32),
        pltpu.VMEM((2, 128, SPAN), BF16),
    ]
    scratch += [pltpu.VMEM(o.shape, o.dtype) for o in held] + [pltpu.SemaphoreType.DMA((4,))]
    scratch += Exchange(count).scratch()
    if direct:
        scratch.append(pltpu.VMEM((2, 2, 2, width // 8, 3 * width), BF16))
        parts = [VectorSum(early.shape[1:])] + [VectorSum(t[1:], True) for t in tables] + [VectorSum(late, split=False)]
        parts += [part for pair in fc2_second + fc1_pairs + proj_pairs + qkv_groups for part in pair]
        scratch += [s for part in parts for s in part.scratch()]
    return pl.pallas_call(
        functools.partial(tail_kernel, (count, groups, len(views))),
        grid=(steps + 1,),
        out_shape=[blocks, g_qkv] + outs,
        in_specs=[
            SMEM,
            column(0),
            column(1),
            column(2),
            pl.BlockSpec((2, seq, seq), lambda h: (clip(h), 0, 0)),
            column(0),
            whole(patches.shape),
            whole(bits.shape),
        ]
        + [whole(v.shape) for v in vectors]
        + [ANY] * (4 + len(views))
        + [whole(v.shape) for v in more],
        out_specs=[once(blocks.shape), whole(g_qkv.shape)] + [whole(o.shape) for o in outs],
        scratch_shapes=scratch,
        compiler_params=pltpu.CompilerParams(
            collective_id=2, has_side_effects=True, vmem_limit_bytes=VMEM_LIMIT
        ),
        name="tail",
    )(resolution, qkv, qkv, qkv, probs, upstream, patches, bits, *vectors, *held, *views, *more)


MESH = pl.DeviceIdType.MESH


def place():
    b, z = lax.axis_index("batch"), lax.axis_index("blk")
    return b, z, lax.rem(b, 2), lax.rem(b // 2, 2), b // 4


def greet(partners):
    barrier = pltpu.get_barrier_semaphore()
    for partner in partners:
        pl.semaphore_signal(barrier, inc=1, device_id=partner, device_id_type=MESH)
    pl.semaphore_wait(barrier, len(partners))


def sum_partners():
    b, z, c, x, y = place()
    near = [(b + 1 - 2 * c, z), (b + 2 - 4 * x, z), (b + 4 - 8 * y, z)]
    return near + [(b, lax.rem(z + s, 4)) for s in (1, 2, 3)]


class Exchange:
    def __init__(self, count):
        self.count = count

    def scratch(self):
        sems = pltpu.SemaphoreType.DMA((self.count - 1,))
        return [sems, sems, pltpu.SemaphoreType.DMA]

    def bind(self, source, target, refs):
        self.source, self.target = source, target
        self.sent, self.come, self.own = refs
        return self

    def partners(self):
        b, z = lax.axis_index("batch"), lax.axis_index("blk")
        return [(b, lax.rem(z + s, self.count)) for s in range(1, self.count)]

    def local(self):
        z = lax.axis_index("blk")
        return pltpu.make_async_copy(self.source.at[z], self.target.at[z], self.own)

    def copy(self, i):
        device = self.partners()[i]
        return pltpu.make_async_remote_copy(
            src_ref=self.source.at[device[1]],
            dst_ref=self.target.at[lax.axis_index("blk")],
            send_sem=self.sent.at[i],
            recv_sem=self.come.at[i],
            device_id=device,
            device_id_type=MESH,
        )

    def start(self):
        for i in range(self.count - 1):
            self.copy(i).start()
        self.local().start()

    def finish(self):
        self.local().wait()
        for i in range(self.count - 1):
            self.copy(i).wait_recv()
        for i in range(self.count - 1):
            self.copy(i).wait_send()


class VectorSum:
    STAGES = 6

    def __init__(self, size, low=False, split=True):
        self.size, self.dtype, self.split = tuple(size), BF16 if low else F32, split

    def scratch(self):
        part = pltpu.VMEM(self.size, F32)
        sems = pltpu.SemaphoreType.DMA((7,))
        return [part] * 7 + [pltpu.VMEM((4,) + self.size, self.dtype), sems, sems]

    def bind(self, source, target, refs, at=0):
        self.source, self.target, self.at = source, target, at
        self.got0, self.sum1, self.got1, self.sum2, self.got2, self.mine, self.other, self.all = refs[:8]
        self.sent, self.come = refs[8:]
        return self

    def copy(self, i):
        b, z, c, x, y = place()
        near = sum_partners()
        source, target, device = (
            (self.source.at[1 - c] if self.split else None, self.got0, near[0]),
            (self.all.at[z], self.all.at[z], near[3]),
            (self.all.at[z], self.all.at[z], near[4]),
            (self.all.at[z], self.all.at[z], near[5]),
            (self.sum1, self.got1, near[1]),
            (self.sum2, self.got2, near[2]),
            (self.mine, self.other, near[0]),
        )[i]
        return pltpu.make_async_remote_copy(
            src_ref=source,
            dst_ref=target,
            send_sem=self.sent.at[i],
            recv_sem=self.come.at[i],
            device_id=device,
            device_id_type=MESH,
        )

    def stage(self, number):
        b, z, c, x, y = place()
        if number == 0:
            if self.split:
                self.copy(0).start()
        elif number == 1:
            if self.split:
                self.copy(0).wait_recv()
                self.all[z] = (self.source[c] + self.got0[...]).astype(self.dtype)
            else:
                self.all[z] = self.source[...].astype(self.dtype)
            for i in (1, 2, 3):
                self.copy(i).start()
        elif number == 2:
            for i in (1, 2, 3):
                self.copy(i).wait_recv()
            value = [self.all[k].astype(F32) for k in range(4)]
            self.sum1[...] = value[0] + value[1] + value[2] + value[3]
            self.copy(4).start()
        elif number == 3:
            self.copy(4).wait_recv()
            self.sum2[...] = self.sum1[...] + self.got1[...]
            self.copy(5).start()
        elif number == 4:
            self.copy(5).wait_recv()
            self.mine[...] = self.sum2[...] + self.got2[...]
            self.copy(6).start()
        else:
            self.copy(6).wait_recv()
            if self.split:
                rows = slice(self.at, self.at + self.size[0])
                self.target[c, rows] = self.mine[...]
                self.target[1 - c, rows] = self.other[...]
            else:
                self.target[...] = self.mine[...] + self.other[...]
            for i in range(0 if self.split else 1, 7):
                self.copy(i).wait_send()


def in_steps(rows, width, body):
    step = rows
    while step * width > 49152 and step % 32 == 0:
        step //= 2
    if step == rows:
        body(pl.ds(0, rows))
    else:

        def one(i, carry):
            body(pl.ds(pl.multiple_of(i * step, step), step))
            return carry

        lax.fori_loop(0, rows // step, one, 0)


class WeightSum:
    COPIES = 5

    def __init__(self, rows, at, width, flip, resident=False, half=""):
        self.rows, self.at, self.width, self.flip, self.resident = rows, at, width, flip, resident
        self.half = half
        self.fold = 2 if (rows // 4) % 16 else 1

    def strip(self):
        return (self.rows // 4 * self.fold, self.width // self.fold)

    def scratch(self):
        r, w = self.rows, self.width
        strip = self.strip()
        refs = [pltpu.SemaphoreType.DMA((self.COPIES,))] * 2
        if self.half != "first":
            refs += [pltpu.VMEM((2, 2) + strip, BF16), pltpu.VMEM((2,) + strip, BF16), pltpu.VMEM(strip, BF16)]
            refs += [pltpu.VMEM((r, w), BF16)]
        if self.half != "second":
            refs += [pltpu.VMEM((2, 2, r, w), BF16), pltpu.VMEM((2, r, w), BF16)]
            if not self.resident:
                refs += [pltpu.VMEM((2, 2, r, w), BF16), pltpu.SemaphoreType.DMA]
        return refs

    def bind(self, grad, out, refs, at=None):
        self.grad, self.out = grad, out
        self.source_at = self.at if at is None else at
        refs = list(refs)
        take = lambda n: [refs.pop(0) for _ in range(n)]
        self.sent, self.come = take(2)
        if self.half != "first":
            self.mine, self.got3, self.got4, self.got2 = take(4)
        if self.half != "second":
            self.got0, self.got1 = take(2)
            if not self.resident:
                self.kept, self.own = take(2)
        return self

    def columns(self):
        return pl.ds(self.source_at, self.width)

    def keep(self, i, j):
        if self.half == "second":
            return self.grad.at[j if self.flip else i]
        if self.resident:
            return self.grad.at[i, j, place()[2], :, self.columns()]
        return self.kept.at[i, j]

    def local(self):
        c = place()[2]
        return pltpu.make_async_copy(self.grad.at[:, :, c, :, self.columns()], self.kept, self.own)

    def copy(self, i):
        b, z, c, x, y = place()
        to = sum_partners()
        every = slice(None)
        if i == 0:
            source, target, device = self.grad.at[:, :, 1 - c, :, self.columns()], self.got0, to[0]
        elif i == 1:
            source = self.keep(1 - y, every) if self.flip else self.keep(every, 1 - x)
            target, device = self.got1, to[2 if self.flip else 1]
        elif i == 2:
            source = self.keep(y, 1 - x) if self.flip else self.keep(1 - y, x)
            target, device = self.got2, to[1 if self.flip else 2]
        elif i == 3:
            z0 = lax.rem(z, 2)
            source, target, device = self.mine.at[:, 1 - z0], self.got3, (b, z + 1 - 2 * z0)
        else:
            z0, z1 = lax.rem(z, 2), z // 2
            source, target, device = self.mine.at[1 - z1, z0], self.got4, (b, z + 2 - 4 * z1)
        return pltpu.make_async_remote_copy(
            src_ref=source,
            dst_ref=target,
            send_sem=self.sent.at[i],
            recv_sem=self.come.at[i],
            device_id=device,
            device_id_type=MESH,
        )

    def add(self, target, source):
        self.put(target, target, source)

    def put(self, target, first, second):
        def body(rows):
            target[rows, :] = first[rows, :] + second[rows, :]

        in_steps(self.rows, self.width, body)

    def stage(self, number):
        b, z, c, x, y = place()
        keep = self.keep
        if self.half != "second":
            got0, got1 = self.got0, self.got1
        if self.half == "second" and number == 2:
            self.copy(2).start()
            return
        if self.half == "first" and number == 2:
            self.copy(1).wait_recv()
            for k in range(2):
                self.put(self.out.at[k], keep(y, k) if self.flip else keep(k, x), got1.at[k])
            return
        if number == 0:
            if not self.resident:
                self.local().start()
            self.copy(0).start()
        elif number == 1:
            if not self.resident:
                self.local().wait()
            self.copy(0).wait_recv()
            spots = lambda k: [(k, 0), (k, 1)] if self.flip else [(0, k), (1, k)]
            mine = y if self.flip else x
            for i, j in spots(1 - mine):
                self.add(keep(i, j), got0.at[i, j])
            self.copy(1).start()
            for i, j in spots(mine):
                self.add(keep(i, j), got0.at[i, j])
        elif number == 2:
            self.copy(1).wait_recv()
            if self.flip:
                self.add(keep(y, 1 - x), got1.at[1 - x])
                self.copy(2).start()
                self.add(keep(y, x), got1.at[x])
            else:
                self.add(keep(1 - y, x), got1.at[1 - y])
                self.copy(2).start()
                self.add(keep(y, x), got1.at[y])
        elif number == 3:
            self.copy(2).wait_recv()
            r = self.rows // 4
            mine = keep(y, x)
            for k in range(4):
                rows = slice(k * r, k * r + r)
                value = mine[rows, :].astype(F32) + self.got2[rows, :].astype(F32)
                if self.fold == 2:
                    half = self.width // 2
                    value = jnp.concatenate([value[:, :half], value[:, half:]], axis=0)
                self.mine[k // 2, k % 2] = value.astype(BF16)
            self.copy(3).start()
        elif number == 4:
            self.copy(3).wait_recv()
            z0, z1 = lax.rem(z, 2), z // 2
            self.mine[1 - z1, z0] = self.mine[1 - z1, z0] + self.got3[1 - z1]
            self.copy(4).start()
        elif number == 5:
            self.copy(4).wait_recv()
            z0, z1 = lax.rem(z, 2), z // 2
            value = self.mine[z1, z0].astype(F32) + self.got3[z1].astype(F32) + self.got4[...].astype(F32)
            r, half = self.rows // 4, self.width // 2
            if self.fold == 2:
                self.out[:, self.at : self.at + half] = value[:r]
                self.out[:, self.at + half : self.at + self.width] = value[r:]
            else:
                self.out[:, self.at : self.at + self.width] = value
        else:
            for i in {"": range(5), "first": range(2), "second": range(2, 5)}[self.half]:
                self.copy(i).wait_send()


def run_stage(pair, number):
    for part in pair:
        part.stage(number)


def row_blocks(rows, size, body, carry):
    return lax.fori_loop(
        0, rows // size, lambda i, c: body(pl.ds(pl.multiple_of(i * size, size), size), c), carry
    )


def row_sum(values):
    return jnp.sum(values, axis=0, keepdims=True)


MLP_ROWS = 320
MLP_CHUNK = 512
FC2_SPANS = (512, 256)
MLP_SLOTS = (
    (0, 5, 20, 21),
    (3, 6, 21, 21),
)


def mlp_kernel(setup, *refs):
    count, direct, pairs = setup
    refs = list(refs)
    take = lambda n: [refs.pop(0) for _ in range(n)]
    inputs, mixed, raw_up, to_slot, w_proj, *vectors = take(11)
    b1, w1_all, w2_all = take(3)
    output, d_resid, d_mixed, p_proj, p_fc1, vector, *p_fc2 = take(6 + (len(pairs) or 1))
    hidden, d_branch, upstream, attn, resid, branch, d_hidden, act, slope, d_pre, d_bias, blocks_out, landed = take(13)
    held1, held2, load_sems = take(3)
    move = Exchange(count)
    move.bind(blocks_out, landed, take(len(move.scratch())))
    step = pl.program_id(0)
    seq, width = inputs.shape
    steps, _, chunk = held1.shape
    w1, w2 = held1.at[lax.rem(step, steps)], held2.at[lax.rem(step, steps)]
    proj_bias, gain1, gain2, shift2, fc2_bias, gain_out = [flat_row(v) for v in vectors]
    slots = [[] for _ in range(3 * steps + 4)]
    at_chunk = pl.ds(pl.multiple_of(lax.rem(step, steps) * chunk, chunk), chunk)
    grads = []

    def run(slot):
        for tick in slots[slot]:
            tick()

    def run_here(spot):
        for k in range(steps):
            if slots[3 * k + spot]:
                pl.when(step == steps + k)(functools.partial(run, 3 * k + spot))

    if direct:
        grads = take(len(pairs))
        for n, (grad, pair) in enumerate(zip(grads, pairs)):
            bound = [
                part.bind(grad, p_fc2[n].at[f], take(len(part.scratch())), at=f * part.width)
                for f, part in enumerate(pair)
            ]
            for number, slot in zip((0, 1, 2, 6), MLP_SLOTS[n]):
                slots[slot].append(functools.partial(run_stage, bound, number))

    def load(k):
        at = slice(k * chunk, (k + 1) * chunk)
        return [
            pltpu.make_async_copy(w1_all.at[:, at], held1.at[k], load_sems.at[2 * k]),
            pltpu.make_async_copy(w2_all.at[at, :], held2.at[k], load_sems.at[2 * k + 1]),
        ]

    @pl.when(step == 0)
    def _():
        for k in range(steps):
            for copy in load(k):
                copy.start()
        greet(sum_partners() if direct else move.partners())
        d_bias[...] = flat_row(b1)

        def enter(rows, carry):
            up = matmul(to_slot[rows, :], raw_up[...])
            upstream[rows, :] = up
            d_branch[rows, :] = (gain_out * up).astype(BF16)
            value = matmul(mixed[rows, :], w_proj[...]) + proj_bias
            attn[rows, :] = value
            value = inputs[rows, :] + gain1 * value
            resid[rows, :] = value
            hidden[rows, :] = (normalize(value)[0] * gain2 + shift2).astype(BF16)
            return carry

        row_blocks(seq, MLP_ROWS, enter, 0)
        branch[...] = jnp.zeros_like(branch)
        d_hidden[...] = jnp.zeros_like(d_hidden)

    for k in range(steps):

        @pl.when(step == k)
        def _(k=k):
            for copy in load(k):
                copy.wait()

    @pl.when(step < steps)
    def _():
        bias_here = d_bias[:, at_chunk]

        def forward(rows, carry):
            pre = matmul(hidden[rows, :], w1[...]) + bias_here
            half = 0.5 * (1.0 + lax.erf(pre * 0.7071067811865476))
            slope[rows, at_chunk] = (half + pre * jnp.exp(-0.5 * pre * pre) * 0.3989422804014327).astype(BF16)
            low = (pre * half).astype(BF16)
            act[rows, at_chunk] = low
            branch[rows, :] += matmul(low, w2[...])
            return carry

        row_blocks(seq, MLP_ROWS, forward, 0)

    @pl.when(step == steps)
    def _():
        def finish(rows, total):
            mlp = branch[rows, :] + fc2_bias
            d_mixed[rows, :] = (resid[rows, :] + gain_out * mlp).astype(BF16)
            return total + row_sum(upstream[rows, :] * mlp)

        vector[0, 0:1, :] = row_blocks(seq, MLP_ROWS, finish, jnp.zeros((1, width), F32))
        ordered = t_matmul(to_slot[...], d_mixed[...]).astype(BF16)
        blocks_out[...] = ordered.reshape(blocks_out.shape)
        move.start()

    if direct:
        for k in range(len(grads)):

            @pl.when(step == steps + k)
            def _(k=k):
                at = sum(FC2_SPANS[:k])
                partial = t_matmul(act[...], d_branch[:, at : at + FC2_SPANS[k]]).astype(BF16)
                grads[k][...] = partial.reshape(grads[k].shape)
    else:

        @pl.when(step == steps)
        def _():
            p_fc2[0][...] = t_matmul(act[...], d_branch[...]).astype(BF16)

    run_here(0)

    @pl.when(step >= steps)
    def _():
        def backward(rows, total):
            back = (matmul_t(d_branch[rows, :], w2[...]) * slope[rows, at_chunk].astype(F32)).astype(BF16)
            d_pre[rows, :] = back
            d_hidden[rows, :] += matmul_t(back, w1[...])
            return total + row_sum(back.astype(F32))

        bias_sum = row_blocks(seq, MLP_ROWS, backward, jnp.zeros((1, chunk), F32))
        d_bias[:, at_chunk] = bias_sum
        run_here(2)
        p_fc1[0] = t_matmul(hidden[...], d_pre[...]).astype(BF16)

    @pl.when(step == 2 * steps - 1)
    def _():
        run(3 * steps)

        def leave(rows, totals):
            d_fc2b, d_ln2g, d_ln2b, d_gamma1, d_projb = totals
            d_fc2b += row_sum(d_branch[rows, :].astype(F32))
            normed, factor = normalize(resid[rows, :])
            grad = d_hidden[rows, :]
            d_ln2g += row_sum(grad * normed)
            d_ln2b += row_sum(grad)
            grad = upstream[rows, :] + norm_back(grad, normed, factor, gain2)
            d_resid[rows, :] = grad
            d_gamma1 += row_sum(grad * attn[rows, :])
            grad = (gain1 * grad).astype(BF16)
            d_branch[rows, :] = grad
            d_projb += row_sum(grad.astype(F32))
            d_mixed[rows, :] = matmul_t(grad, w_proj[...]).astype(BF16)
            return d_fc2b, d_ln2g, d_ln2b, d_gamma1, d_projb

        totals = row_blocks(seq, MLP_ROWS, leave, (jnp.zeros((1, width), F32),) * 5)
        run(3 * steps + 1)
        run(3 * steps + 2)
        p_proj[...] = t_matmul(mixed[...], d_branch[...]).astype(BF16)
        zero = jnp.zeros((2, width), F32)
        vector[0, 1:8, :] = jnp.concatenate([*totals, zero], axis=0)
        pieces = [d_bias[:, i * width : (i + 1) * width] for i in range(4)]
        vector[1] = jnp.concatenate(pieces + [zero, zero], axis=0)
        run(3 * steps + 3)
        move.finish()
        output[...] = landed[...]


def fc2_pairs(hidden, half):
    pairs, at = [], 0
    for span in FC2_SPANS:
        part = span // 2
        pairs.append([WeightSum(hidden // 8, at + f * part, part, f == 1, True, half) for f in (0, 1)])
        at += span
    return pairs


def mlp(inputs, mixed, raw_up, to_slot, w_proj, vectors, w1, b1, w2, count, direct):
    seq, width = inputs.shape
    hidden = w1.shape[1]
    chunk = MLP_CHUNK
    steps = hidden // chunk
    pairs = fc2_pairs(hidden, "first") if direct else []
    flat = lambda dtype: jax.ShapeDtypeStruct((seq, width), dtype)
    vmem = lambda dtype: pltpu.VMEM((seq, width), dtype)
    parts = [(2, 2, hidden // 8, span // 2) for span in FC2_SPANS] if direct else [(hidden, width)]
    turn = lambda k: lax.rem(k, steps)
    blocks = (count, seq // count, width)
    return pl.pallas_call(
        functools.partial(mlp_kernel, (count, direct, pairs)),
        grid=(2 * steps,),
        out_shape=[
            jax.ShapeDtypeStruct(blocks, BF16),
            flat(F32),
            flat(BF16),
            jax.ShapeDtypeStruct((width, width), BF16),
            jax.ShapeDtypeStruct((steps, width, chunk), BF16),
            jax.ShapeDtypeStruct((2, 8, width), F32),
        ]
        + [jax.ShapeDtypeStruct(p, BF16) for p in parts],
        in_specs=[
            once(inputs.shape),
            once(mixed.shape),
            once(raw_up.shape),
            once(to_slot.shape),
            once(w_proj.shape),
        ]
        + [whole(v.shape) for v in vectors]
        + [whole(b1.shape), ANY, ANY],
        out_specs=[
            once(blocks),
            once((seq, width)),
            once((seq, width)),
            once((width, width)),
            pl.BlockSpec((1, width, chunk), lambda k: (jnp.maximum(k - steps, 0), 0, 0)),
            whole((2, 8, width)),
        ]
        + [once(p) for p in parts],
        scratch_shapes=[
            vmem(BF16), vmem(BF16), vmem(F32), vmem(F32), vmem(F32), vmem(F32), vmem(F32),
            pltpu.VMEM((seq, hidden), BF16), pltpu.VMEM((seq, hidden), BF16),
            pltpu.VMEM((seq, chunk), BF16), pltpu.VMEM((1, hidden), F32), pltpu.VMEM(blocks, BF16),
            pltpu.VMEM(blocks, BF16),
            pltpu.VMEM((steps, width, chunk), BF16), pltpu.VMEM((steps, chunk, width), BF16),
            pltpu.SemaphoreType.DMA((2 * steps,)),
        ]
        + Exchange(count).scratch()
        + [pltpu.VMEM((2, 2, 2, hidden // 8, span), BF16) for span in FC2_SPANS[: len(pairs)]]
        + [s for pair in pairs for part in pair for s in part.scratch()],
        compiler_params=pltpu.CompilerParams(
            collective_id=1, has_side_effects=True, vmem_limit_bytes=VMEM_LIMIT
        ),
        name="mlp",
    )(inputs, mixed, raw_up, to_slot, w_proj, *vectors, b1, w1, w2)


def swap(value, axis, bit, count):
    return lax.ppermute(value, axis, [(i, i ^ bit) for i in range(count)])


def bits_of(count):
    return [1 << i for i in range(count.bit_length() - 1)]


def scatter_sum(grad, batch, blk):
    places = [("batch", bit, batch) for bit in bits_of(batch)][::-1]
    places += [("blk", bit, blk) for bit in bits_of(blk)][::-1]
    value = grad.reshape((2,) * len(places) + (grad.shape[0] >> len(places), grad.shape[1]))
    left = list(places)
    for spot in places:
        axis, bit, count = spot
        at = left.index(spot)
        left.remove(spot)
        mine = jnp.bitwise_and(lax.axis_index(axis) // bit, 1)
        sent = lax.dynamic_index_in_dim(value, 1 - mine, at, keepdims=False)
        kept = lax.dynamic_index_in_dim(value, mine, at, keepdims=False)
        got = swap(sent, axis, bit, count)
        value = kept.astype(F32) + got.astype(F32)
        if left:
            value = value.astype(BF16)
    return value


def total_sum(value, batch, blk):
    for bit in bits_of(batch):
        value = value + swap(value, "batch", bit, batch)
    for bit in bits_of(blk):
        value = value + swap(value, "blk", bit, blk)
    return value


def unpack_kernel(plan, early, late, table, *refs):
    refs = list(refs)
    take = lambda n: [refs.pop(0) for _ in range(n)]
    sources = [take(n) for n in plan]
    vectors = take(11)
    out_low, out_high = take(2)
    targets = take(len(plan))
    turned = take(1)[0]
    for group, target in zip(sources, targets):
        at = 0
        for source in group:
            size = source.shape[-1]
            target[..., at : at + size] = source[...]
            at += size
    for i in range(6):
        vectors[i][...] = early[0, i : i + 1, :].reshape(vectors[i].shape)
    for n in range(4):
        rows = [late[6 * n + k : 6 * n + k + 1, :] for k in range(6)]
        vectors[6 + n][...] = jnp.concatenate(rows, axis=1).reshape(vectors[6 + n].shape)
    rows = [early[1, i : i + 1, :] for i in range(4)]
    vectors[10][...] = jnp.concatenate(rows, axis=1).reshape(vectors[10].shape)
    heads = out_low.shape[0]
    for n, (out, side, pad) in enumerate(((out_low, SIDE_LOW, G_HIGH - G_LOW), (out_high, SIDE, 0))):
        value = jnp.concatenate([table[n, k * 48 : (k + 1) * 48, :] for k in range(heads // 2)], axis=1)
        turned[n] = jnp.concatenate([value, jnp.zeros((80, 64 * heads), F32)], axis=0).T
        here = turned.at[n]
        for r in range(side):
            rows = pl.ds(SIDE - 1 - r - pad, heads, stride=64)
            out[:, r * side : (r + 1) * side] = here[rows, :][:, pad : pad + side]
        for i in range(3):
            out[:, side * side + i : side * side + i + 1] = here[pl.ds(i, heads, stride=64), :][:, 47:48]


def unpack(early, late, table, groups, width, hidden, heads):
    outs = [jax.ShapeDtypeStruct((width,), F32)] * 10 + [jax.ShapeDtypeStruct((hidden,), F32)]
    outs += [jax.ShapeDtypeStruct((heads, side * side + 3), F32) for side in (SIDE_LOW, SIDE)]
    outs += [
        jax.ShapeDtypeStruct(g[0].shape[:-1] + (sum(p.shape[-1] for p in g),), g[0].dtype) for g in groups
    ]
    pieces = [p for g in groups for p in g]
    vmem = pl.BlockSpec(memory_space=pltpu.VMEM)
    result = pl.pallas_call(
        functools.partial(unpack_kernel, [len(g) for g in groups]),
        out_shape=outs,
        in_specs=[vmem] * (3 + len(pieces)),
        out_specs=[vmem] * (13 + len(groups)),
        scratch_shapes=[pltpu.VMEM((2, 64 * heads, 128), F32)],
        compiler_params=pltpu.CompilerParams(vmem_limit_bytes=VMEM_LIMIT),
        name="unpack",
    )(early, late, table, *pieces)
    return result[:11], result[11].T, result[12].T, result[13:]


def swap(value, axis, bit, count):
    return lax.ppermute(value, axis, [(i, i ^ bit) for i in range(count)])


def bits_of(count):
    return [1 << i for i in range(count.bit_length() - 1)]


def scatter_sum(grad, batch, blk):
    places = [("batch", bit, batch) for bit in bits_of(batch)][::-1]
    places += [("blk", bit, blk) for bit in bits_of(blk)][::-1]
    value = grad.reshape((2,) * len(places) + (grad.shape[0] >> len(places), grad.shape[1]))
    left = list(places)
    for spot in places:
        axis, bit, count = spot
        at = left.index(spot)
        left.remove(spot)
        mine = jnp.bitwise_and(lax.axis_index(axis) // bit, 1)
        sent = lax.dynamic_index_in_dim(value, 1 - mine, at, keepdims=False)
        kept = lax.dynamic_index_in_dim(value, mine, at, keepdims=False)
        got = swap(sent, axis, bit, count)
        value = kept.astype(F32) + got.astype(F32)
        if left:
            value = value.astype(BF16)
    return value


def total_sum(value, batch, blk):
    for bit in bits_of(batch):
        value = value + swap(value, "batch", bit, batch)
    for bit in bits_of(blk):
        value = value + swap(value, "blk", bit, blk)
    return value


def shards(
    batch,
    blk,
    tokens,
    resolution,
    positions,
    ln1_gain,
    ln1_bias,
    w_qkv,
    q_bias,
    v_bias,
    w_proj,
    proj_bias,
    gamma1,
    ln2_gain,
    ln2_bias,
    w_fc1,
    fc1_bias,
    w_fc2,
    fc2_bias,
    gamma2,
    rel_low,
    rel_high,
    grad_out,
):
    images, rows, width = tokens.shape
    seq = positions.shape[1]
    heads = rel_low.shape[1]
    assert images == blk and rows * blk == seq and width == heads * 64
    direct = (batch, blk) == (8, 4)
    bits = jnp.asarray(lane_tables())
    patches = jnp.asarray(slot_tables(seq)[2].T, F32)
    to_slot, inputs, qkv, probs, mixed, raw_up = front(
        resolution,
        positions,
        rel_low,
        rel_high,
        bits,
        patches,
        (ln1_gain, ln1_bias, q_bias, v_bias),
        w_qkv,
        tokens,
        grad_out,
        blk,
    )
    output, d_resid, d_mixed, p_proj, p_fc1, early, *p_fc2 = mlp(
        inputs,
        mixed,
        raw_up.reshape(seq, width),
        to_slot,
        w_proj,
        (proj_bias, gamma1, ln2_gain, ln2_bias, fc2_bias, gamma2),
        w_fc1,
        fc1_bias,
        w_fc2,
        blk,
        direct,
    )
    grad_tokens, g_qkv, *sums, late, d_table = tail(
        resolution,
        qkv,
        probs,
        d_mixed,
        patches,
        bits,
        (ln1_gain, ln1_bias),
        inputs,
        d_resid,
        to_slot,
        w_qkv,
        (p_fc1, p_proj),
        p_fc2,
        early,
        blk,
        direct,
    )
    groups = [[output], [grad_tokens]]
    if direct:
        g_fc1, g_proj, g_fc2, early = sums
        groups += [[g] for g in (g_fc1, g_fc2, g_proj, g_qkv)]
    else:
        g_fc1, g_fc2, g_proj, g_qkv = [scatter_sum(g, batch, blk) for g in (p_fc1.transpose(1, 0, 2).reshape(width, -1), *p_fc2, p_proj, g_qkv)]
        early, late, d_table = [total_sum(v, batch, blk) for v in (early, late, d_table)]
    vectors, s_low, s_high, rest = unpack(early, late, d_table, groups, width, w_fc1.shape[1], heads)
    s_gamma2, s_fc2b, s_ln2g, s_ln2b, s_gamma1, s_projb, s_ln1g, s_ln1b, s_qb, s_vb, s_fc1b = vectors
    output, grad_tokens = rest[:2]
    if direct:
        g_fc1, g_fc2, g_proj, g_qkv = rest[2:]
    return (
        output,
        grad_tokens,
        s_ln1g,
        s_ln1b,
        g_qkv,
        s_qb,
        s_vb,
        g_proj,
        s_projb,
        s_gamma1,
        s_ln2g,
        s_ln2b,
        g_fc1,
        s_fc1b,
        g_fc2,
        s_fc2b,
        s_gamma2,
        s_low,
        s_high,
    )


def solution(mesh):
    rows = P("batch", "blk", None)
    shared = P(("batch", "blk"), None)
    in_specs = (rows, P("batch"), P("batch", None)) + (P(),) * 17 + (rows,)
    out_specs = (
        (rows, rows, P(), P(), shared, P(), P(), shared)
        + (P(),) * 4
        + (shared, P(), shared)
        + (P(),) * 4
    )
    return jax.shard_map(
        functools.partial(shards, mesh.shape["batch"], mesh.shape["blk"]),
        mesh=mesh,
        in_specs=in_specs,
        out_specs=out_specs,
        check_vma=False,
    )
```

```python
import functools

import jax
import jax.numpy as jnp
import numpy as np
from jax import lax
from jax.experimental import pallas as pl
from jax.experimental.pallas import tpu as pltpu
from jax.sharding import PartitionSpec as P

G_LOW = 14
G_HIGH = 24
SIDE_LOW = 2 * G_LOW - 1
SIDE = 2 * G_HIGH - 1
CELLS = G_HIGH * G_HIGH
SPAN = 1152
F32 = jnp.float32
BF16 = jnp.bfloat16


def normalize(values):
    center = values - jnp.mean(values, axis=-1, keepdims=True)
    factor = lax.rsqrt(jnp.mean(center * center, axis=-1, keepdims=True) + 1e-06)
    return center * factor, factor


def norm_back(grad, normed, factor, gain):
    scaled = grad * gain
    return factor * (
        scaled
        - jnp.mean(scaled, axis=-1, keepdims=True)
        - normed * jnp.mean(scaled * normed, axis=-1, keepdims=True)
    )


def matmul(left, right):
    return jnp.dot(left, right, preferred_element_type=F32)


def matmul_t(left, right):
    return lax.dot_general(left, right, (((1,), (1,)), ((), ())), preferred_element_type=F32)


def t_matmul(left, right):
    return lax.dot_general(left, right, (((0,), (0,)), ((), ())), preferred_element_type=F32)


def slot_tables(seq):
    tokens = np.arange(seq)
    tables = []
    for grid in (G_LOW, G_HIGH):
        cells = np.arange(CELLS)
        used = (cells // G_HIGH < grid) & (cells % G_HIGH < grid)
        free = np.concatenate([cells[~used], np.arange(CELLS + 1, seq)])
        slot = np.full(seq, CELLS)
        slot[1 + grid * grid :] = free
        patch = np.concatenate([used, np.zeros(seq - CELLS, bool)])
        key = patch.copy()
        key[CELLS] = True
        tables.append((slot, (tokens >= 1) & (tokens < 1 + grid * grid), patch, key))
    return [np.stack(parts) for parts in zip(*tables)]


def lane_tables():
    lanes = np.arange(SPAN)
    shift = G_HIGH - 1 - lanes % G_HIGH
    bits = (shift[None, :] >> np.arange(8)[:, None]) & 1
    return bits.astype(np.int32)


def spread_of(rows, first):
    row = (lax.broadcasted_iota(jnp.int32, (rows, SPAN), 0) - first) * G_HIGH
    lane = lax.broadcasted_iota(jnp.int32, (rows, SPAN), 1) - row
    inside = (lane >= 0) & (lane < G_HIGH) & (row >= 0) & (row < SIDE * G_HIGH)
    return jnp.where(inside, 1.0, 0.0).astype(BF16)


def slide(values, bits, down):
    for k in range(5):
        amount = 1 << k if down else 48 - (1 << k)
        values = jnp.where(bits[k : k + 1, :] > 0, pltpu.roll(values, amount, 0), values)
    return values


VMEM_LIMIT = 62 << 20


def whole(shape):
    return pl.BlockSpec(shape, lambda h: (0,) * len(shape))


def once(shape):
    return pl.BlockSpec(shape, lambda h: (0,) * len(shape), pipeline_mode=pl.Buffered(1))


ANY = pl.BlockSpec(memory_space=pl.ANY)
SMEM = pl.BlockSpec(memory_space=pltpu.SMEM)


def flat_row(ref):
    return ref[...].astype(F32).reshape(1, ref.shape[0])


def front_kernel(
    count, resolution, cells, low_t, high_t, bits, slot_of, is_patch, patches, masks,
    ln1_gain, ln1_bias, q_bias, v_bias, w_qkv, tokens, grad_out,
    to_slot, inputs, qkv, probs, mixed, raw_up, bias, raw, landed, inner_low, inner_high, wide, full, spread, *refs,
):
    step = pl.program_id(0)
    me = lax.axis_index("blk")
    high = resolution[me] == 1
    seq = full.shape[0]
    heads = low_t.shape[0]
    width = inputs.shape[1]
    size = len(Exchange(count).scratch())
    move = Exchange(count).bind(tokens, raw, refs[:size])
    move_up = Exchange(count).bind(grad_out, landed, refs[size:])

    @pl.when(step == 0)
    def _():
        greet(move.partners())
        move.start()
        here = cells[pl.ds(me, 1), :]
        grid = jnp.where(high, G_HIGH, G_LOW)
        row = jnp.zeros_like(here)
        for k in range(1, G_HIGH):
            row += (here >= k * grid).astype(jnp.int32)
        at = row * G_HIGH + here - row * grid
        patch = jnp.where(high, is_patch[1:2, :], is_patch[0:1, :])
        other = jnp.where(high, slot_of[1:2, :], slot_of[0:1, :])
        slot = jnp.where(patch > 0, at, other)
        spots = lax.broadcasted_iota(jnp.int32, (seq, seq), 0)
        to_slot[...] = jnp.where(spots == slot, 1.0, 0.0).astype(BF16)
        spread[...] = spread_of(48, 0)
        inner_low[...] = jnp.zeros_like(inner_low)
        inner_high[...] = jnp.zeros_like(inner_high)
        low_f, high_f = low_t[...].astype(F32), high_t[...].astype(F32)
        pad = G_HIGH - G_LOW
        for j in range(SIDE):
            r = SIDE - 1 - j
            inner_high[j * 16 : j * 16 + heads, 0:SIDE] = high_f[:, r * SIDE : (r + 1) * SIDE]
            r -= pad
            if 0 <= r < SIDE_LOW:
                inner_low[j * 16 : j * 16 + heads, pad : pad + SIDE_LOW] = low_f[
                    :, r * SIDE_LOW : (r + 1) * SIDE_LOW
                ]

    @pl.when(step < heads)
    def _():
        rows = pl.ds(step, 48, stride=16)
        table = jnp.where(high, inner_high[rows, :], inner_low[rows, :]).astype(BF16)
        wide[...] = slide(t_matmul(table, spread[...])[0:48], bits, False)[0:G_HIGH]
        for r in range(G_HIGH):
            at = (G_HIGH - 1 - r) * G_HIGH
            full[r * G_HIGH : (r + 1) * G_HIGH, 0:CELLS] = wide[:, at : at + CELLS]
        column = lax.broadcasted_iota(jnp.int32, (1, seq), 1)
        ends = [t[:, t.shape[1] - 3 : t.shape[1]].astype(F32) for t in (low_t, high_t)]
        special = jnp.where(high, ends[1], ends[0])
        here = lax.broadcasted_iota(jnp.int32, special.shape, 0) == step
        special = jnp.sum(jnp.where(here, special, 0.0), axis=0, keepdims=True)
        inner_row = jnp.where(column < CELLS, special[:, 0:1], special[:, 2:3])
        values = jnp.where(column < CELLS, full[...], special[:, 1:2])
        patch = jnp.where(high, patches[:, 1:2], patches[:, 0:1])
        mask = jnp.where(high, masks[1:2, :], masks[0:1, :])
        values = jnp.where(patch > 0.0, values, inner_row)
        bias[step] = (values + mask).astype(BF16)

    @pl.when(step == heads)
    def _():
        move.finish()
        move_up.start()
        value = matmul(to_slot[...], raw[...].reshape(seq, width))
        inputs[...] = value
        hidden = (normalize(value)[0] * flat_row(ln1_gain) + flat_row(ln1_bias)).astype(BF16)
        shifts = [flat_row(q_bias), 0.0, flat_row(v_bias)]
        for n in range(3):
            part = slice(n * width, (n + 1) * width)
            qkv[:, part] = (matmul(hidden, w_qkv[:, part]) + shifts[n]).astype(BF16)

    @pl.when(step >= heads)
    def _():
        pair = step - heads
        query, keys, values = [
            qkv[:, pl.ds(pl.multiple_of(n * width + pair * 128, 128), 128)] for n in range(3)
        ]
        for h in range(2):
            at = slice(h * 64, h * 64 + 64)
            scores = matmul_t(query[:, at] * 0.125, keys[:, at]) + bias[2 * pair + h].astype(F32)
            expo = jnp.exp(scores - jnp.max(scores, axis=-1, keepdims=True))
            low = (expo * (1.0 / jnp.sum(expo, axis=-1, keepdims=True))).astype(BF16)
            probs[h] = low
            mixed[:, at] = matmul(low, values[:, at]).astype(BF16)

    @pl.when(step == pl.num_programs(0) - 1)
    def _():
        move_up.finish()
        raw_up[...] = landed[...]


def front(resolution, cells, rel_low, rel_high, bits, patches, vectors, w_qkv, tokens, grad_out, count):
    heads = rel_low.shape[1]
    seq = cells.shape[1]
    width = w_qkv.shape[0]
    slot_np, token_np, _, key_np = slot_tables(seq)
    slot_of = jnp.asarray(slot_np, jnp.int32)
    is_patch = jnp.asarray(token_np, jnp.int32)
    masks = jnp.asarray(np.where(key_np, 0.0, -1e30), F32)
    operands = (rel_low.T, rel_high.T, bits, slot_of, is_patch, patches, masks) + vectors + (w_qkv,)
    late = lambda i: jnp.maximum(i - heads, 0)
    return pl.pallas_call(
        functools.partial(front_kernel, count),
        grid=(heads + heads // 2,),
        out_shape=(
            jax.ShapeDtypeStruct((seq, seq), BF16),
            jax.ShapeDtypeStruct((seq, width), F32),
            jax.ShapeDtypeStruct((seq, 3 * width), BF16),
            jax.ShapeDtypeStruct((heads, seq, seq), BF16),
            jax.ShapeDtypeStruct((seq, width), BF16),
            jax.ShapeDtypeStruct(grad_out.shape, BF16),
        ),
        in_specs=[SMEM, whole(cells.shape)] + [whole(o.shape) for o in operands] + [ANY, ANY],
        out_specs=(
            whole((seq, seq)),
            whole((seq, width)),
            whole((seq, 3 * width)),
            pl.BlockSpec((2, seq, seq), lambda i: (late(i), 0, 0)),
            pl.BlockSpec((seq, 128), lambda i: (0, late(i))),
            once(grad_out.shape),
        ),
        scratch_shapes=[
            pltpu.VMEM((heads, seq, seq), BF16),
            pltpu.VMEM(tokens.shape, BF16),
            pltpu.VMEM(grad_out.shape, BF16),
            pltpu.VMEM((48 * 16, 128), F32),
            pltpu.VMEM((48 * 16, 128), F32),
            pltpu.VMEM((G_HIGH, SPAN), F32),
            pltpu.VMEM((seq, seq), F32),
            pltpu.VMEM((48, SPAN), BF16),
        ]
        + Exchange(count).scratch()
        + Exchange(count).scratch(),
        compiler_params=pltpu.CompilerParams(
            collective_id=0, has_side_effects=True, vmem_limit_bytes=VMEM_LIMIT
        ),
        name="front",
    )(resolution, cells, *operands, tokens, grad_out)


def head_grads(query, keys, values, weights, up, patch, spread, bits, score, wide, lanes):
    ups = matmul_t(up, values)
    weight = weights.astype(F32)
    product = weight * ups
    ds = product - weight * jnp.sum(product, axis=-1, keepdims=True)
    ds_low = ds.astype(BF16)
    d_query = (matmul(ds_low, keys) * 0.125).astype(BF16)
    d_key = t_matmul(ds_low, query * 0.125).astype(BF16)
    d_value = t_matmul(weights, up).astype(BF16)
    total = jnp.sum(ds, axis=0, keepdims=True)
    ds = ds * patch
    score[...] = ds
    inside = jnp.sum(ds, axis=0, keepdims=True)
    wide[...] = jnp.zeros_like(wide)
    for r in range(G_HIGH):
        off = (G_HIGH - 1 - r) * G_HIGH
        wide[:, off : off + CELLS] += score[r * G_HIGH : (r + 1) * G_HIGH, 0:CELLS]
    flat = slide(jnp.concatenate([wide[...], jnp.zeros_like(wide)], axis=0), bits, True)
    first = flat.astype(BF16)
    rest = flat - first.astype(F32)
    second = rest.astype(BF16)
    third = (rest - second.astype(F32)).astype(BF16)
    table = matmul_t(first, spread) + matmul_t(second, spread) + matmul_t(third, spread)
    column = lax.broadcasted_iota(jnp.int32, total.shape, 1)
    lane = lax.broadcasted_iota(jnp.int32, (1, 128), 1)
    outside = total - inside
    edge = jnp.zeros((1, 128), F32)
    for i, value in enumerate((
        jnp.where(column < CELLS, outside, 0.0),
        jnp.where(column == CELLS, inside, 0.0),
        jnp.where(column == CELLS, outside, 0.0),
    )):
        edge += jnp.where(lane == lanes + i, jnp.sum(value, axis=1, keepdims=True), 0.0)
    return d_query, d_key, d_value, table, edge


def by_lanes(row):
    return jnp.concatenate([row[:, i : i + 128] for i in range(0, row.shape[1], 128)], axis=0)


FC1_SLOTS = ((0, 2, 6, 10, 16, 20, 26), (0, 3, 8, 11, 16, 20, 26), (1, 3, 9, 12, 17, 20, 26))
PROJ_SLOTS = ((8, 10, 16, 17, 21, 22, 26),)
QKV_SLOTS = ((8, 10, 16, 17, 21, 22, 26), (9, 11, 16, 17, 21, 22, 26), (12, 13, 17, 18, 21, 22, 26))
FC2_SLOTS = ((0, 4, 7, 18, 26), (0, 5, 8, 18, 26))
EARLY_SLOTS = (0, 1, 3, 5, 7, 9)
TABLE_SLOTS = ((8, 9, 11, 16, 17, 18), (12, 13, 16, 17, 18, 19))
LATE_SLOTS = (15, 15, 16, 17, 18, 19)
TABLE_PAIRS = 4


def tail_kernel(setup, *refs):
    count, groups, grads = setup
    direct = grads > 0
    fc1_pairs, proj_pairs, fc2_second, qkv_groups = groups
    refs = list(refs)
    take = lambda n: [refs.pop(0) for _ in range(n)]
    resolution, query, keys, values, probs, upstream, patches, bits, ln1_gain, ln1_bias = take(10)
    sources = take(4)
    partials = take(grads)
    early, *p_fc2 = take(1 + len(fc2_second)) if direct else [None]
    moved, g_qkv = take(2)
    g_fc1, g_proj, g_fc2, early_sum = take(4) if direct else [None] * 4
    late_sum, table_sum = take(2)
    score, wide, d_qkv, hidden, table_a, table_b, tokens, landed, late, spread = take(10)
    loaded = take(4)
    load_sems = take(1)[0]
    move = Exchange(count)
    move.bind(tokens, landed, take(len(move.scratch())))
    step = pl.program_id(0)
    steps = pl.num_programs(0) - 1
    seq, width = loaded[0].shape
    first_rows = table_a.shape[1]
    slots = [[] for _ in range(28)]

    def run(slot):
        for tick in slots[slot]:
            tick()

    if direct:
        grad = take(1)[0]
        scratch_of = lambda part: take(len(part.scratch()))

        def plan(bound, own, numbers=range(7)):
            for number, slot in zip(numbers, own):
                slots[slot].append(functools.partial(run_stage, bound, number))

        small = VectorSum(early.shape[1:])
        plan([small.bind(early, early_sum, scratch_of(small))], EARLY_SLOTS)
        for ref, at, own in zip((table_a, table_b), (0, first_rows), TABLE_SLOTS):
            part = VectorSum(ref.shape[1:], True)
            plan([part.bind(ref, table_sum, scratch_of(part), at)], own)
        part = VectorSum(late.shape, split=False)
        plan([part.bind(late, late_sum, scratch_of(part))], LATE_SLOTS)
        for pair, own, source in zip(fc2_second, FC2_SLOTS, p_fc2):
            bound = [part.bind(source.at[f], g_fc2, scratch_of(part)) for f, part in enumerate(pair)]
            plan(bound, own, (2, 3, 4, 5, 6))
        for k, (pair, spots) in enumerate(zip(fc1_pairs, FC1_SLOTS)):
            plan([part.bind(partials[0].at[2 * k + f], g_fc1, scratch_of(part), 0) for f, part in enumerate(pair)], spots)
        for pair, spots in zip(proj_pairs, PROJ_SLOTS):
            plan([part.bind(partials[1], g_proj, scratch_of(part)) for part in pair], spots)
        for group, spots in zip(qkv_groups, QKV_SLOTS):
            plan([part.bind(grad, g_qkv, scratch_of(part)) for part in group], spots)

    loads = [
        pltpu.make_async_copy(source, target, load_sems.at[i])
        for i, (source, target) in enumerate(zip(sources, loaded))
    ]
    inputs, d_resid, to_slot, w_qkv = loaded

    @pl.when(step == 0)
    def _():
        greet(sum_partners() if direct else move.partners())
        for load in loads:
            load.start()
        for h in range(2):
            spread[h] = spread_of(128, 64 * h)

    high = resolution[lax.axis_index("blk")] == 1

    @pl.when(step < steps)
    def _():
        patch = jnp.where(high, patches[:, 1:2], patches[:, 0:1])
        total = jnp.zeros((48, 128), F32)
        edge = jnp.zeros((1, 128), F32)
        parts3 = [[], [], []]
        for h in range(2):
            for k in range(6):
                if slots[2 * k + h]:
                    pl.when(step == k)(functools.partial(run, 2 * k + h))

            at = slice(h * 64, h * 64 + 64)
            *heads3, part, ends = head_grads(
                query[:, at], keys[:, at], values[:, at], probs[h], upstream[:, at],
                patch, spread[h], bits, score, wide, h * 64,
            )
            total += part
            edge += ends
            for n in range(3):
                parts3[n].append(heads3[n])
        for n in range(3):
            at = pl.ds(pl.multiple_of(n * width + step * 128, 128), 128)
            d_qkv[:, at] = jnp.concatenate(parts3[n], axis=1)
        row = lax.broadcasted_iota(jnp.int32, (48, 128), 0)
        total = jnp.where(row == 47, edge, total)
        for k in range(6):

            @pl.when(step == k)
            def _(k=k):
                ref, at = (table_a, k) if k < TABLE_PAIRS else (table_b, k - TABLE_PAIRS)
                ref[0, at * 48 : at * 48 + 48, :] = jnp.where(high, 0.0, total)
                ref[1, at * 48 : at * 48 + 48, :] = jnp.where(high, total, 0.0)

    @pl.when(step == 1)
    def _():
        loads[0].wait()
        hidden[...] = (normalize(inputs[...])[0] * flat_row(ln1_gain) + flat_row(ln1_bias)).astype(BF16)

    for k in range(3):

        @pl.when(step == 2 * k + 1)
        def _(k=k):
            for n in range(3):
                at = slice(n * width + k * 256, n * width + k * 256 + 256)
                partial = t_matmul(hidden[...], d_qkv[:, at]).astype(BF16)
                if direct:
                    grad[:, :, :, :, at] = partial.reshape(2, 2, 2, width // 8, 256)
                else:
                    g_qkv[:, at] = partial

    @pl.when(step == steps)
    def _():
        run(12)
        for load in loads[1:]:
            load.wait()
        gain = flat_row(ln1_gain)
        def enter(rows, totals):
            d_gain, d_shift = totals
            back = matmul_t(d_qkv[rows, :], w_qkv[...])
            value, scale = normalize(inputs[rows, :])
            hidden[rows, :] = (d_resid[rows, :] + norm_back(back, value, scale, gain)).astype(BF16)
            return d_gain + row_sum(back * value), d_shift + row_sum(back)

        d_gain, d_shift = row_blocks(seq, seq // 2, enter, (jnp.zeros((1, width), F32),) * 2)
        run(13)
        run(14)
        ordered = t_matmul(to_slot[...], hidden[...]).astype(BF16)
        tokens[...] = ordered.reshape(tokens.shape)
        sums4 = [d_gain, d_shift] + [
            row_sum(d_qkv[:, n * width : (n + 1) * width].astype(F32)) for n in (0, 2)
        ]
        late[...] = jnp.concatenate([by_lanes(v) for v in sums4], axis=0)
        run(15)
        move.start()
        if direct:
            for slot in range(16, 28):
                run(slot)
        else:
            late_sum[...] = late[...]
            table_sum[:, 0:first_rows] = table_a[...]
            table_sum[:, first_rows:] = table_b[...]
        move.finish()
        moved[...] = landed[...]


def tail(resolution, qkv, probs, upstream, patches, bits, vectors, inputs, d_resid, to_slot, w_qkv, partials, p_fc2, early, count, direct):
    seq, width = inputs.shape
    steps = width // 128
    clip = lambda h: jnp.minimum(h, steps - 1)
    column = lambda part: pl.BlockSpec((seq, 128), lambda h: (0, part * steps + clip(h)))
    blocks = jax.ShapeDtypeStruct((count, seq // count, width), BF16)
    late, table = (24, 128), (2, 48 * steps, 128)
    tables = [(2, 48 * TABLE_PAIRS, 128), (2, 48 * (steps - TABLE_PAIRS), 128)]
    groups, views, more, outs = ((), (), (), ()), [], [], []
    g_qkv = jax.ShapeDtypeStruct((width, 3 * width), BF16)
    if direct:
        views = [g.reshape(*g.shape[:-2], 2, 2, 2, g.shape[-2] // 8, g.shape[-1]) for g in partials]
        more = [early, *p_fc2]
        chunks, _, chunk = partials[0].shape
        hidden = chunks * chunk
        share = lambda columns, rows=width: jax.ShapeDtypeStruct((rows // 32, columns), F32)
        outs = [share(hidden), share(width), share(width, hidden), jax.ShapeDtypeStruct(early.shape, F32)]
        g_qkv = share(3 * width)
        fc1_pairs = [
            [WeightSum(width // 8, (2 * k + f) * chunk, chunk, f == 1) for f in (0, 1)] for k in range(chunks // 2)
        ]
        proj_pairs = [[WeightSum(width // 8, 0, 256, False), WeightSum(width // 8, 256, 512, True)]]
        fc2_second = fc2_pairs(hidden, "second")
        qkv_groups = [
            [WeightSum(width // 8, n * width + k * 256, 256, (n + k) % 2 == 1, True) for n in range(3)]
            for k in range(3)
        ]
        groups = (fc1_pairs, proj_pairs, fc2_second, qkv_groups)
    outs = list(outs) + [jax.ShapeDtypeStruct(late, F32), jax.ShapeDtypeStruct(table, F32)]
    held = (inputs, d_resid, to_slot, w_qkv)
    scratch = [
        pltpu.VMEM((seq, seq), F32),
        pltpu.VMEM((G_HIGH, SPAN), F32),
        pltpu.VMEM((seq, 3 * width), BF16),
        pltpu.VMEM((seq, width), BF16),
        pltpu.VMEM(tables[0], F32),
        pltpu.VMEM(tables[1], F32),
        pltpu.VMEM(blocks.shape, BF16),
        pltpu.VMEM(blocks.shape, BF16),
        pltpu.VMEM(late, F32),
        pltpu.VMEM((2, 128, SPAN), BF16),
    ]
    scratch += [pltpu.VMEM(o.shape, o.dtype) for o in held] + [pltpu.SemaphoreType.DMA((4,))]
    scratch += Exchange(count).scratch()
    if direct:
        scratch.append(pltpu.VMEM((2, 2, 2, width // 8, 3 * width), BF16))
        parts = [VectorSum(early.shape[1:])] + [VectorSum(t[1:], True) for t in tables] + [VectorSum(late, split=False)]
        parts += [part for pair in fc2_second + fc1_pairs + proj_pairs + qkv_groups for part in pair]
        scratch += [s for part in parts for s in part.scratch()]
    return pl.pallas_call(
        functools.partial(tail_kernel, (count, groups, len(views))),
        grid=(steps + 1,),
        out_shape=[blocks, g_qkv] + outs,
        in_specs=[
            SMEM,
            column(0),
            column(1),
            column(2),
            pl.BlockSpec((2, seq, seq), lambda h: (clip(h), 0, 0)),
            column(0),
            whole(patches.shape),
            whole(bits.shape),
        ]
        + [whole(v.shape) for v in vectors]
        + [ANY] * (4 + len(views))
        + [whole(v.shape) for v in more],
        out_specs=[once(blocks.shape), whole(g_qkv.shape)] + [whole(o.shape) for o in outs],
        scratch_shapes=scratch,
        compiler_params=pltpu.CompilerParams(
            collective_id=2, has_side_effects=True, vmem_limit_bytes=VMEM_LIMIT
        ),
        name="tail",
    )(resolution, qkv, qkv, qkv, probs, upstream, patches, bits, *vectors, *held, *views, *more)


MESH = pl.DeviceIdType.MESH


def place():
    b, z = lax.axis_index("batch"), lax.axis_index("blk")
    return b, z, lax.rem(b, 2), lax.rem(b // 2, 2), b // 4


def greet(partners):
    barrier = pltpu.get_barrier_semaphore()
    for partner in partners:
        pl.semaphore_signal(barrier, inc=1, device_id=partner, device_id_type=MESH)
    pl.semaphore_wait(barrier, len(partners))


def sum_partners():
    b, z, c, x, y = place()
    near = [(b + 1 - 2 * c, z), (b + 2 - 4 * x, z), (b + 4 - 8 * y, z)]
    return near + [(b, lax.rem(z + s, 4)) for s in (1, 2, 3)]


class Exchange:
    def __init__(self, count):
        self.count = count

    def scratch(self):
        sems = pltpu.SemaphoreType.DMA((self.count - 1,))
        return [sems, sems, pltpu.SemaphoreType.DMA]

    def bind(self, source, target, refs):
        self.source, self.target = source, target
        self.sent, self.come, self.own = refs
        return self

    def partners(self):
        b, z = lax.axis_index("batch"), lax.axis_index("blk")
        return [(b, lax.rem(z + s, self.count)) for s in range(1, self.count)]

    def local(self):
        z = lax.axis_index("blk")
        return pltpu.make_async_copy(self.source.at[z], self.target.at[z], self.own)

    def copy(self, i):
        device = self.partners()[i]
        return pltpu.make_async_remote_copy(
            src_ref=self.source.at[device[1]],
            dst_ref=self.target.at[lax.axis_index("blk")],
            send_sem=self.sent.at[i],
            recv_sem=self.come.at[i],
            device_id=device,
            device_id_type=MESH,
        )

    def start(self):
        for i in range(self.count - 1):
            self.copy(i).start()
        self.local().start()

    def finish(self):
        self.local().wait()
        for i in range(self.count - 1):
            self.copy(i).wait_recv()
        for i in range(self.count - 1):
            self.copy(i).wait_send()


class VectorSum:
    STAGES = 6

    def __init__(self, size, low=False, split=True):
        self.size, self.dtype, self.split = tuple(size), BF16 if low else F32, split

    def scratch(self):
        part = pltpu.VMEM(self.size, F32)
        sems = pltpu.SemaphoreType.DMA((7,))
        return [part] * 7 + [pltpu.VMEM((4,) + self.size, self.dtype), sems, sems]

    def bind(self, source, target, refs, at=0):
        self.source, self.target, self.at = source, target, at
        self.got0, self.sum1, self.got1, self.sum2, self.got2, self.mine, self.other, self.all = refs[:8]
        self.sent, self.come = refs[8:]
        return self

    def copy(self, i):
        b, z, c, x, y = place()
        near = sum_partners()
        source, target, device = (
            (self.source.at[1 - c] if self.split else None, self.got0, near[0]),
            (self.all.at[z], self.all.at[z], near[3]),
            (self.all.at[z], self.all.at[z], near[4]),
            (self.all.at[z], self.all.at[z], near[5]),
            (self.sum1, self.got1, near[1]),
            (self.sum2, self.got2, near[2]),
            (self.mine, self.other, near[0]),
        )[i]
        return pltpu.make_async_remote_copy(
            src_ref=source,
            dst_ref=target,
            send_sem=self.sent.at[i],
            recv_sem=self.come.at[i],
            device_id=device,
            device_id_type=MESH,
        )

    def stage(self, number):
        b, z, c, x, y = place()
        if number == 0:
            if self.split:
                self.copy(0).start()
        elif number == 1:
            if self.split:
                self.copy(0).wait_recv()
                self.all[z] = (self.source[c] + self.got0[...]).astype(self.dtype)
            else:
                self.all[z] = self.source[...].astype(self.dtype)
            for i in (1, 2, 3):
                self.copy(i).start()
        elif number == 2:
            for i in (1, 2, 3):
                self.copy(i).wait_recv()
            value = [self.all[k].astype(F32) for k in range(4)]
            self.sum1[...] = value[0] + value[1] + value[2] + value[3]
            self.copy(4).start()
        elif number == 3:
            self.copy(4).wait_recv()
            self.sum2[...] = self.sum1[...] + self.got1[...]
            self.copy(5).start()
        elif number == 4:
            self.copy(5).wait_recv()
            self.mine[...] = self.sum2[...] + self.got2[...]
            self.copy(6).start()
        else:
            self.copy(6).wait_recv()
            if self.split:
                rows = slice(self.at, self.at + self.size[0])
                self.target[c, rows] = self.mine[...]
                self.target[1 - c, rows] = self.other[...]
            else:
                self.target[...] = self.mine[...] + self.other[...]
            for i in range(0 if self.split else 1, 7):
                self.copy(i).wait_send()


def in_steps(rows, width, body):
    step = rows
    while step * width > 49152 and step % 32 == 0:
        step //= 2
    if step == rows:
        body(pl.ds(0, rows))
    else:

        def one(i, carry):
            body(pl.ds(pl.multiple_of(i * step, step), step))
            return carry

        lax.fori_loop(0, rows // step, one, 0)


class WeightSum:
    COPIES = 5

    def __init__(self, rows, at, width, flip, resident=False, half=""):
        self.rows, self.at, self.width, self.flip, self.resident = rows, at, width, flip, resident
        self.half = half
        self.fold = 2 if (rows // 4) % 16 else 1

    def strip(self):
        return (self.rows // 4 * self.fold, self.width // self.fold)

    def scratch(self):
        r, w = self.rows, self.width
        strip = self.strip()
        refs = [pltpu.SemaphoreType.DMA((self.COPIES,))] * 2
        if self.half != "first":
            refs += [pltpu.VMEM((2, 2) + strip, BF16), pltpu.VMEM((2,) + strip, BF16), pltpu.VMEM(strip, BF16)]
            refs += [pltpu.VMEM((r, w), BF16)]
        if self.half != "second":
            refs += [pltpu.VMEM((2, 2, r, w), BF16), pltpu.VMEM((2, r, w), BF16)]
            if not self.resident:
                refs += [pltpu.VMEM((2, 2, r, w), BF16), pltpu.SemaphoreType.DMA]
        return refs

    def bind(self, grad, out, refs, at=None):
        self.grad, self.out = grad, out
        self.source_at = self.at if at is None else at
        refs = list(refs)
        take = lambda n: [refs.pop(0) for _ in range(n)]
        self.sent, self.come = take(2)
        if self.half != "first":
            self.mine, self.got3, self.got4, self.got2 = take(4)
        if self.half != "second":
            self.got0, self.got1 = take(2)
            if not self.resident:
                self.kept, self.own = take(2)
        return self

    def columns(self):
        return pl.ds(self.source_at, self.width)

    def keep(self, i, j):
        if self.half == "second":
            return self.grad.at[j if self.flip else i]
        if self.resident:
            return self.grad.at[i, j, place()[2], :, self.columns()]
        return self.kept.at[i, j]

    def local(self):
        c = place()[2]
        return pltpu.make_async_copy(self.grad.at[:, :, c, :, self.columns()], self.kept, self.own)

    def copy(self, i):
        b, z, c, x, y = place()
        to = sum_partners()
        every = slice(None)
        if i == 0:
            source, target, device = self.grad.at[:, :, 1 - c, :, self.columns()], self.got0, to[0]
        elif i == 1:
            source = self.keep(1 - y, every) if self.flip else self.keep(every, 1 - x)
            target, device = self.got1, to[2 if self.flip else 1]
        elif i == 2:
            source = self.keep(y, 1 - x) if self.flip else self.keep(1 - y, x)
            target, device = self.got2, to[1 if self.flip else 2]
        elif i == 3:
            z0 = lax.rem(z, 2)
            source, target, device = self.mine.at[:, 1 - z0], self.got3, (b, z + 1 - 2 * z0)
        else:
            z0, z1 = lax.rem(z, 2), z // 2
            source, target, device = self.mine.at[1 - z1, z0], self.got4, (b, z + 2 - 4 * z1)
        return pltpu.make_async_remote_copy(
            src_ref=source,
            dst_ref=target,
            send_sem=self.sent.at[i],
            recv_sem=self.come.at[i],
            device_id=device,
            device_id_type=MESH,
        )

    def add(self, target, source):
        self.put(target, target, source)

    def put(self, target, first, second):
        def body(rows):
            target[rows, :] = first[rows, :] + second[rows, :]

        in_steps(self.rows, self.width, body)

    def stage(self, number):
        b, z, c, x, y = place()
        keep = self.keep
        if self.half != "second":
            got0, got1 = self.got0, self.got1
        if self.half == "second" and number == 2:
            self.copy(2).start()
            return
        if self.half == "first" and number == 2:
            self.copy(1).wait_recv()
            for k in range(2):
                self.put(self.out.at[k], keep(y, k) if self.flip else keep(k, x), got1.at[k])
            return
        if number == 0:
            if not self.resident:
                self.local().start()
            self.copy(0).start()
        elif number == 1:
            if not self.resident:
                self.local().wait()
            self.copy(0).wait_recv()
            spots = lambda k: [(k, 0), (k, 1)] if self.flip else [(0, k), (1, k)]
            mine = y if self.flip else x
            for i, j in spots(1 - mine):
                self.add(keep(i, j), got0.at[i, j])
            self.copy(1).start()
            for i, j in spots(mine):
                self.add(keep(i, j), got0.at[i, j])
        elif number == 2:
            self.copy(1).wait_recv()
            if self.flip:
                self.add(keep(y, 1 - x), got1.at[1 - x])
                self.copy(2).start()
                self.add(keep(y, x), got1.at[x])
            else:
                self.add(keep(1 - y, x), got1.at[1 - y])
                self.copy(2).start()
                self.add(keep(y, x), got1.at[y])
        elif number == 3:
            self.copy(2).wait_recv()
            r = self.rows // 4
            mine = keep(y, x)
            for k in range(4):
                rows = slice(k * r, k * r + r)
                value = mine[rows, :].astype(F32) + self.got2[rows, :].astype(F32)
                if self.fold == 2:
                    half = self.width // 2
                    value = jnp.concatenate([value[:, :half], value[:, half:]], axis=0)
                self.mine[k // 2, k % 2] = value.astype(BF16)
            self.copy(3).start()
        elif number == 4:
            self.copy(3).wait_recv()
            z0, z1 = lax.rem(z, 2), z // 2
            self.mine[1 - z1, z0] = self.mine[1 - z1, z0] + self.got3[1 - z1]
            self.copy(4).start()
        elif number == 5:
            self.copy(4).wait_recv()
            z0, z1 = lax.rem(z, 2), z // 2
            value = self.mine[z1, z0].astype(F32) + self.got3[z1].astype(F32) + self.got4[...].astype(F32)
            r, half = self.rows // 4, self.width // 2
            if self.fold == 2:
                self.out[:, self.at : self.at + half] = value[:r]
                self.out[:, self.at + half : self.at + self.width] = value[r:]
            else:
                self.out[:, self.at : self.at + self.width] = value
        else:
            for i in {"": range(5), "first": range(2), "second": range(2, 5)}[self.half]:
                self.copy(i).wait_send()


def run_stage(pair, number):
    for part in pair:
        part.stage(number)


def row_blocks(rows, size, body, carry):
    return lax.fori_loop(
        0, rows // size, lambda i, c: body(pl.ds(pl.multiple_of(i * size, size), size), c), carry
    )


def row_sum(values):
    return jnp.sum(values, axis=0, keepdims=True)


MLP_ROWS = 320
MLP_CHUNK = 512
FC2_SPANS = (512, 256)
MLP_SLOTS = (
    (0, 5, 20, 21),
    (3, 6, 21, 21),
)


def mlp_kernel(setup, *refs):
    count, direct, pairs = setup
    refs = list(refs)
    take = lambda n: [refs.pop(0) for _ in range(n)]
    inputs, mixed, raw_up, to_slot, w_proj, *vectors = take(11)
    b1, w1_all, w2_all = take(3)
    output, d_resid, d_mixed, p_proj, p_fc1, vector, *p_fc2 = take(6 + (len(pairs) or 1))
    hidden, d_branch, upstream, attn, resid, branch, d_hidden, act, slope, d_pre, d_bias, blocks_out, landed = take(13)
    held1, held2, load_sems = take(3)
    move = Exchange(count)
    move.bind(blocks_out, landed, take(len(move.scratch())))
    step = pl.program_id(0)
    seq, width = inputs.shape
    steps, _, chunk = held1.shape
    w1, w2 = held1.at[lax.rem(step, steps)], held2.at[lax.rem(step, steps)]
    proj_bias, gain1, gain2, shift2, fc2_bias, gain_out = [flat_row(v) for v in vectors]
    slots = [[] for _ in range(3 * steps + 4)]
    at_chunk = pl.ds(pl.multiple_of(lax.rem(step, steps) * chunk, chunk), chunk)
    grads = []

    def run(slot):
        for tick in slots[slot]:
            tick()

    def run_here(spot):
        for k in range(steps):
            if slots[3 * k + spot]:
                pl.when(step == steps + k)(functools.partial(run, 3 * k + spot))

    if direct:
        grads = take(len(pairs))
        for n, (grad, pair) in enumerate(zip(grads, pairs)):
            bound = [
                part.bind(grad, p_fc2[n].at[f], take(len(part.scratch())), at=f * part.width)
                for f, part in enumerate(pair)
            ]
            for number, slot in zip((0, 1, 2, 6), MLP_SLOTS[n]):
                slots[slot].append(functools.partial(run_stage, bound, number))

    def load(k):
        at = slice(k * chunk, (k + 1) * chunk)
        return [
            pltpu.make_async_copy(w1_all.at[:, at], held1.at[k], load_sems.at[2 * k]),
            pltpu.make_async_copy(w2_all.at[at, :], held2.at[k], load_sems.at[2 * k + 1]),
        ]

    @pl.when(step == 0)
    def _():
        for k in range(steps):
            for copy in load(k):
                copy.start()
        greet(sum_partners() if direct else move.partners())
        d_bias[...] = flat_row(b1)

        def enter(rows, carry):
            up = matmul(to_slot[rows, :], raw_up[...])
            upstream[rows, :] = up
            d_branch[rows, :] = (gain_out * up).astype(BF16)
            value = matmul(mixed[rows, :], w_proj[...]) + proj_bias
            attn[rows, :] = value
            value = inputs[rows, :] + gain1 * value
            resid[rows, :] = value
            hidden[rows, :] = (normalize(value)[0] * gain2 + shift2).astype(BF16)
            return carry

        row_blocks(seq, MLP_ROWS, enter, 0)
        branch[...] = jnp.zeros_like(branch)
        d_hidden[...] = jnp.zeros_like(d_hidden)

    for k in range(steps):

        @pl.when(step == k)
        def _(k=k):
            for copy in load(k):
                copy.wait()

    @pl.when(step < steps)
    def _():
        bias_here = d_bias[:, at_chunk]

        def forward(rows, carry):
            pre = matmul(hidden[rows, :], w1[...]) + bias_here
            half = 0.5 * (1.0 + lax.erf(pre * 0.7071067811865476))
            slope[rows, at_chunk] = (half + pre * jnp.exp(-0.5 * pre * pre) * 0.3989422804014327).astype(BF16)
            low = (pre * half).astype(BF16)
            act[rows, at_chunk] = low
            branch[rows, :] += matmul(low, w2[...])
            return carry

        row_blocks(seq, MLP_ROWS, forward, 0)

    @pl.when(step == steps)
    def _():
        def finish(rows, total):
            mlp = branch[rows, :] + fc2_bias
            d_mixed[rows, :] = (resid[rows, :] + gain_out * mlp).astype(BF16)
            return total + row_sum(upstream[rows, :] * mlp)

        vector[0, 0:1, :] = row_blocks(seq, MLP_ROWS, finish, jnp.zeros((1, width), F32))
        ordered = t_matmul(to_slot[...], d_mixed[...]).astype(BF16)
        blocks_out[...] = ordered.reshape(blocks_out.shape)
        move.start()

    if direct:
        for k in range(len(grads)):

            @pl.when(step == steps + k)
            def _(k=k):
                at = sum(FC2_SPANS[:k])
                partial = t_matmul(act[...], d_branch[:, at : at + FC2_SPANS[k]]).astype(BF16)
                grads[k][...] = partial.reshape(grads[k].shape)
    else:

        @pl.when(step == steps)
        def _():
            p_fc2[0][...] = t_matmul(act[...], d_branch[...]).astype(BF16)

    run_here(0)

    @pl.when(step >= steps)
    def _():
        def backward(rows, total):
            back = (matmul_t(d_branch[rows, :], w2[...]) * slope[rows, at_chunk].astype(F32)).astype(BF16)
            d_pre[rows, :] = back
            d_hidden[rows, :] += matmul_t(back, w1[...])
            return total + row_sum(back.astype(F32))

        bias_sum = row_blocks(seq, MLP_ROWS, backward, jnp.zeros((1, chunk), F32))
        d_bias[:, at_chunk] = bias_sum
        run_here(2)
        p_fc1[0] = t_matmul(hidden[...], d_pre[...]).astype(BF16)

    @pl.when(step == 2 * steps - 1)
    def _():
        run(3 * steps)

        def leave(rows, totals):
            d_fc2b, d_ln2g, d_ln2b, d_gamma1, d_projb = totals
            d_fc2b += row_sum(d_branch[rows, :].astype(F32))
            normed, factor = normalize(resid[rows, :])
            grad = d_hidden[rows, :]
            d_ln2g += row_sum(grad * normed)
            d_ln2b += row_sum(grad)
            grad = upstream[rows, :] + norm_back(grad, normed, factor, gain2)
            d_resid[rows, :] = grad
            d_gamma1 += row_sum(grad * attn[rows, :])
            grad = (gain1 * grad).astype(BF16)
            d_branch[rows, :] = grad
            d_projb += row_sum(grad.astype(F32))
            d_mixed[rows, :] = matmul_t(grad, w_proj[...]).astype(BF16)
            return d_fc2b, d_ln2g, d_ln2b, d_gamma1, d_projb

        totals = row_blocks(seq, MLP_ROWS, leave, (jnp.zeros((1, width), F32),) * 5)
        run(3 * steps + 1)
        run(3 * steps + 2)
        p_proj[...] = t_matmul(mixed[...], d_branch[...]).astype(BF16)
        zero = jnp.zeros((2, width), F32)
        vector[0, 1:8, :] = jnp.concatenate([*totals, zero], axis=0)
        pieces = [d_bias[:, i * width : (i + 1) * width] for i in range(4)]
        vector[1] = jnp.concatenate(pieces + [zero, zero], axis=0)
        run(3 * steps + 3)
        move.finish()
        output[...] = landed[...]


def fc2_pairs(hidden, half):
    pairs, at = [], 0
    for span in FC2_SPANS:
        part = span // 2
        pairs.append([WeightSum(hidden // 8, at + f * part, part, f == 1, True, half) for f in (0, 1)])
        at += span
    return pairs


def mlp(inputs, mixed, raw_up, to_slot, w_proj, vectors, w1, b1, w2, count, direct):
    seq, width = inputs.shape
    hidden = w1.shape[1]
    chunk = MLP_CHUNK
    steps = hidden // chunk
    pairs = fc2_pairs(hidden, "first") if direct else []
    flat = lambda dtype: jax.ShapeDtypeStruct((seq, width), dtype)
    vmem = lambda dtype: pltpu.VMEM((seq, width), dtype)
    parts = [(2, 2, hidden // 8, span // 2) for span in FC2_SPANS] if direct else [(hidden, width)]
    turn = lambda k: lax.rem(k, steps)
    blocks = (count, seq // count, width)
    return pl.pallas_call(
        functools.partial(mlp_kernel, (count, direct, pairs)),
        grid=(2 * steps,),
        out_shape=[
            jax.ShapeDtypeStruct(blocks, BF16),
            flat(F32),
            flat(BF16),
            jax.ShapeDtypeStruct((width, width), BF16),
            jax.ShapeDtypeStruct((steps, width, chunk), BF16),
            jax.ShapeDtypeStruct((2, 8, width), F32),
        ]
        + [jax.ShapeDtypeStruct(p, BF16) for p in parts],
        in_specs=[
            once(inputs.shape),
            once(mixed.shape),
            once(raw_up.shape),
            once(to_slot.shape),
            once(w_proj.shape),
        ]
        + [whole(v.shape) for v in vectors]
        + [whole(b1.shape), ANY, ANY],
        out_specs=[
            once(blocks),
            once((seq, width)),
            once((seq, width)),
            once((width, width)),
            pl.BlockSpec((1, width, chunk), lambda k: (jnp.maximum(k - steps, 0), 0, 0)),
            whole((2, 8, width)),
        ]
        + [once(p) for p in parts],
        scratch_shapes=[
            vmem(BF16), vmem(BF16), vmem(F32), vmem(F32), vmem(F32), vmem(F32), vmem(F32),
            pltpu.VMEM((seq, hidden), BF16), pltpu.VMEM((seq, hidden), BF16),
            pltpu.VMEM((seq, chunk), BF16), pltpu.VMEM((1, hidden), F32), pltpu.VMEM(blocks, BF16),
            pltpu.VMEM(blocks, BF16),
            pltpu.VMEM((steps, width, chunk), BF16), pltpu.VMEM((steps, chunk, width), BF16),
            pltpu.SemaphoreType.DMA((2 * steps,)),
        ]
        + Exchange(count).scratch()
        + [pltpu.VMEM((2, 2, 2, hidden // 8, span), BF16) for span in FC2_SPANS[: len(pairs)]]
        + [s for pair in pairs for part in pair for s in part.scratch()],
        compiler_params=pltpu.CompilerParams(
            collective_id=1, has_side_effects=True, vmem_limit_bytes=VMEM_LIMIT
        ),
        name="mlp",
    )(inputs, mixed, raw_up, to_slot, w_proj, *vectors, b1, w1, w2)


def swap(value, axis, bit, count):
    return lax.ppermute(value, axis, [(i, i ^ bit) for i in range(count)])


def bits_of(count):
    return [1 << i for i in range(count.bit_length() - 1)]


def scatter_sum(grad, batch, blk):
    places = [("batch", bit, batch) for bit in bits_of(batch)][::-1]
    places += [("blk", bit, blk) for bit in bits_of(blk)][::-1]
    value = grad.reshape((2,) * len(places) + (grad.shape[0] >> len(places), grad.shape[1]))
    left = list(places)
    for spot in places:
        axis, bit, count = spot
        at = left.index(spot)
        left.remove(spot)
        mine = jnp.bitwise_and(lax.axis_index(axis) // bit, 1)
        sent = lax.dynamic_index_in_dim(value, 1 - mine, at, keepdims=False)
        kept = lax.dynamic_index_in_dim(value, mine, at, keepdims=False)
        got = swap(sent, axis, bit, count)
        value = kept.astype(F32) + got.astype(F32)
        if left:
            value = value.astype(BF16)
    return value


def total_sum(value, batch, blk):
    for bit in bits_of(batch):
        value = value + swap(value, "batch", bit, batch)
    for bit in bits_of(blk):
        value = value + swap(value, "blk", bit, blk)
    return value


def unpack_kernel(plan, early, late, table, *refs):
    refs = list(refs)
    take = lambda n: [refs.pop(0) for _ in range(n)]
    sources = [take(n) for n in plan]
    vectors = take(11)
    out_low, out_high = take(2)
    targets = take(len(plan))
    turned = take(1)[0]
    for group, target in zip(sources, targets):
        at = 0
        for source in group:
            size = source.shape[-1]
            target[..., at : at + size] = source[...]
            at += size
    for i in range(6):
        vectors[i][...] = early[0, i : i + 1, :].reshape(vectors[i].shape)
    for n in range(4):
        rows = [late[6 * n + k : 6 * n + k + 1, :] for k in range(6)]
        vectors[6 + n][...] = jnp.concatenate(rows, axis=1).reshape(vectors[6 + n].shape)
    rows = [early[1, i : i + 1, :] for i in range(4)]
    vectors[10][...] = jnp.concatenate(rows, axis=1).reshape(vectors[10].shape)
    heads = out_low.shape[0]
    for n, (out, side, pad) in enumerate(((out_low, SIDE_LOW, G_HIGH - G_LOW), (out_high, SIDE, 0))):
        value = jnp.concatenate([table[n, k * 48 : (k + 1) * 48, :] for k in range(heads // 2)], axis=1)
        turned[n] = jnp.concatenate([value, jnp.zeros((80, 64 * heads), F32)], axis=0).T
        here = turned.at[n]
        for r in range(side):
            rows = pl.ds(SIDE - 1 - r - pad, heads, stride=64)
            out[:, r * side : (r + 1) * side] = here[rows, :][:, pad : pad + side]
        for i in range(3):
            out[:, side * side + i : side * side + i + 1] = here[pl.ds(i, heads, stride=64), :][:, 47:48]


def unpack(early, late, table, groups, width, hidden, heads):
    outs = [jax.ShapeDtypeStruct((width,), F32)] * 10 + [jax.ShapeDtypeStruct((hidden,), F32)]
    outs += [jax.ShapeDtypeStruct((heads, side * side + 3), F32) for side in (SIDE_LOW, SIDE)]
    outs += [
        jax.ShapeDtypeStruct(g[0].shape[:-1] + (sum(p.shape[-1] for p in g),), g[0].dtype) for g in groups
    ]
    pieces = [p for g in groups for p in g]
    vmem = pl.BlockSpec(memory_space=pltpu.VMEM)
    result = pl.pallas_call(
        functools.partial(unpack_kernel, [len(g) for g in groups]),
        out_shape=outs,
        in_specs=[vmem] * (3 + len(pieces)),
        out_specs=[vmem] * (13 + len(groups)),
        scratch_shapes=[pltpu.VMEM((2, 64 * heads, 128), F32)],
        compiler_params=pltpu.CompilerParams(vmem_limit_bytes=VMEM_LIMIT),
        name="unpack",
    )(early, late, table, *pieces)
    return result[:11], result[11].T, result[12].T, result[13:]


def swap(value, axis, bit, count):
    return lax.ppermute(value, axis, [(i, i ^ bit) for i in range(count)])


def bits_of(count):
    return [1 << i for i in range(count.bit_length() - 1)]


def scatter_sum(grad, batch, blk):
    places = [("batch", bit, batch) for bit in bits_of(batch)][::-1]
    places += [("blk", bit, blk) for bit in bits_of(blk)][::-1]
    value = grad.reshape((2,) * len(places) + (grad.shape[0] >> len(places), grad.shape[1]))
    left = list(places)
    for spot in places:
        axis, bit, count = spot
        at = left.index(spot)
        left.remove(spot)
        mine = jnp.bitwise_and(lax.axis_index(axis) // bit, 1)
        sent = lax.dynamic_index_in_dim(value, 1 - mine, at, keepdims=False)
        kept = lax.dynamic_index_in_dim(value, mine, at, keepdims=False)
        got = swap(sent, axis, bit, count)
        value = kept.astype(F32) + got.astype(F32)
        if left:
            value = value.astype(BF16)
    return value


def total_sum(value, batch, blk):
    for bit in bits_of(batch):
        value = value + swap(value, "batch", bit, batch)
    for bit in bits_of(blk):
        value = value + swap(value, "blk", bit, blk)
    return value


def shards(
    batch,
    blk,
    tokens,
    resolution,
    positions,
    ln1_gain,
    ln1_bias,
    w_qkv,
    q_bias,
    v_bias,
    w_proj,
    proj_bias,
    gamma1,
    ln2_gain,
    ln2_bias,
    w_fc1,
    fc1_bias,
    w_fc2,
    fc2_bias,
    gamma2,
    rel_low,
    rel_high,
    grad_out,
):
    images, rows, width = tokens.shape
    seq = positions.shape[1]
    heads = rel_low.shape[1]
    assert images == blk and rows * blk == seq and width == heads * 64
    direct = (batch, blk) == (8, 4)
    bits = jnp.asarray(lane_tables())
    patches = jnp.asarray(slot_tables(seq)[2].T, F32)
    to_slot, inputs, qkv, probs, mixed, raw_up = front(
        resolution,
        positions,
        rel_low,
        rel_high,
        bits,
        patches,
        (ln1_gain, ln1_bias, q_bias, v_bias),
        w_qkv,
        tokens,
        grad_out,
        blk,
    )
    output, d_resid, d_mixed, p_proj, p_fc1, early, *p_fc2 = mlp(
        inputs,
        mixed,
        raw_up.reshape(seq, width),
        to_slot,
        w_proj,
        (proj_bias, gamma1, ln2_gain, ln2_bias, fc2_bias, gamma2),
        w_fc1,
        fc1_bias,
        w_fc2,
        blk,
        direct,
    )
    grad_tokens, g_qkv, *sums, late, d_table = tail(
        resolution,
        qkv,
        probs,
        d_mixed,
        patches,
        bits,
        (ln1_gain, ln1_bias),
        inputs,
        d_resid,
        to_slot,
        w_qkv,
        (p_fc1, p_proj),
        p_fc2,
        early,
        blk,
        direct,
    )
    groups = [[output], [grad_tokens]]
    if direct:
        g_fc1, g_proj, g_fc2, early = sums
        groups += [[g] for g in (g_fc1, g_fc2, g_proj, g_qkv)]
    else:
        g_fc1, g_fc2, g_proj, g_qkv = [scatter_sum(g, batch, blk) for g in (p_fc1.transpose(1, 0, 2).reshape(width, -1), *p_fc2, p_proj, g_qkv)]
        early, late, d_table = [total_sum(v, batch, blk) for v in (early, late, d_table)]
    vectors, s_low, s_high, rest = unpack(early, late, d_table, groups, width, w_fc1.shape[1], heads)
    s_gamma2, s_fc2b, s_ln2g, s_ln2b, s_gamma1, s_projb, s_ln1g, s_ln1b, s_qb, s_vb, s_fc1b = vectors
    output, grad_tokens = rest[:2]
    if direct:
        g_fc1, g_fc2, g_proj, g_qkv = rest[2:]
    return (
        output,
        grad_tokens,
        s_ln1g,
        s_ln1b,
        g_qkv,
        s_qb,
        s_vb,
        g_proj,
        s_projb,
        s_gamma1,
        s_ln2g,
        s_ln2b,
        g_fc1,
        s_fc1b,
        g_fc2,
        s_fc2b,
        s_gamma2,
        s_low,
        s_high,
    )


def solution(mesh):
    rows = P("batch", "blk", None)
    shared = P(("batch", "blk"), None)
    in_specs = (rows, P("batch"), P("batch", None)) + (P(),) * 17 + (rows,)
    out_specs = (
        (rows, rows, P(), P(), shared, P(), P(), shared)
        + (P(),) * 4
        + (shared, P(), shared)
        + (P(),) * 4
    )
    return jax.shard_map(
        functools.partial(shards, mesh.shape["batch"], mesh.shape["blk"]),
        mesh=mesh,
        in_specs=in_specs,
        out_specs=out_specs,
        check_vma=False,
    )
```
